32 devices in a mesh: dp: 8 (over z, y), seq: 4 (over x, core).
Axes of the slice: x: 2, y: 2, z: 4, core: 2. Of those that a mesh axis runs over, the one named last changes fastest.
Arguments:
- tokens: bfloat16 [8, 2048, 768], P('dp', 'seq'), may hold values from -6 to 6
- cotangent: bfloat16 [8, 2048, 768], P('dp', 'seq'), may hold values from -6 to 6
- segments: int32 [8, 2048], P('dp', 'seq'), may hold values from 0 to 3, as said below
- w_query: bfloat16 [768, 768], P(('dp', 'seq')), may hold values from -0.3125 to 0.3125
- w_key: bfloat16 [768, 768], P(('dp', 'seq')), may hold values from -0.3125 to 0.3125
- w_value: bfloat16 [768, 768], P(('dp', 'seq')), may hold values from -0.21875 to 0.21875
- w_out: bfloat16 [768, 768], P(('dp', 'seq')), may hold values from -1.25 to 1.25
- w_up: bfloat16 [768, 3072], P(('dp', 'seq')), may hold values from -0.21875 to 0.21875
- w_down: bfloat16 [3072, 768], P(('dp', 'seq')), may hold values from -0.109375 to 0.109375
- ln1_gain: bfloat16 [768], P(('dp', 'seq')), may hold values from 0.25 to 1.75
- ln1_shift: bfloat16 [768], P(('dp', 'seq')), may hold values from -4 to 4
- query_bias: bfloat16 [768], P(('dp', 'seq')), may hold values from -4 to 4
- value_bias: bfloat16 [768], P(('dp', 'seq')), may hold values from -4 to 4
- out_bias: bfloat16 [768], P(('dp', 'seq')), may hold values from -4 to 4
- ln2_gain: bfloat16 [768], P(('dp', 'seq')), may hold values from 0.25 to 1.75
- ln2_shift: bfloat16 [768], P(('dp', 'seq')), may hold values from -4 to 4
- up_bias: bfloat16 [3072], P(('dp', 'seq')), may hold values from -4 to 4
- down_bias: bfloat16 [768], P(('dp', 'seq')), may hold values from -4 to 4
Outputs:
- output: float32 [8, 2048, 768], P('dp', 'seq')
- grad_tokens: float32 [8, 2048, 768], P('dp', 'seq')
- grad_w_query: float32 [768, 768], P(('dp', 'seq'))
- grad_w_key: float32 [768, 768], P(('dp', 'seq'))
- grad_w_value: float32 [768, 768], P(('dp', 'seq'))
- grad_w_out: float32 [768, 768], P(('dp', 'seq'))
- grad_w_up: float32 [768, 3072], P(('dp', 'seq'))
- grad_w_down: float32 [3072, 768], P(('dp', 'seq'))
- grad_ln1_gain: float32 [768], P(('dp', 'seq'))
- grad_ln1_shift: float32 [768], P(('dp', 'seq'))
- grad_query_bias: float32 [768], P(('dp', 'seq'))
- grad_value_bias: float32 [768], P(('dp', 'seq'))
- grad_out_bias: float32 [768], P(('dp', 'seq'))
- grad_ln2_gain: float32 [768], P(('dp', 'seq'))
- grad_ln2_shift: float32 [768], P(('dp', 'seq'))
- grad_up_bias: float32 [3072], P(('dp', 'seq'))
- grad_down_bias: float32 [768], P(('dp', 'seq'))
The draws below stay inside these ranges and needn't reach their ends.
Inputs may be any that keep to these rules, and one draw needn't show every extreme that they name: `segments`: along each sequence the numbers start at 0 and rise by one at each document boundary; each document has 200 to 2048 tokens; in every sequence document 0 ends within the first 2048 // 4 positions and document 1 reaches into the last 2048 // 4 positions.
All inputs are finite; a program needn't handle non-finite values.
Results may differ from the reference program's by a relative error of at most 0.015.
Values may be sent and summed in bfloat16 or wider, within the bound.
No kernel may reach another device: no remote copies, remote signals or barrier semaphores. Data moves between devices by JAX's collectives and lax.ppermute only.
A program may use at most 256 MiB of HBM per device.

```python
import math
import jax
import jax.numpy as jnp
from jax import lax

D = 768
H = 12
HD = 64
FF = 3072
S_DEV = 1
LEN = 2048
MINDOC = 200
NSEQ = 8
N_SEQ = 4


def draw_segments(key, part):
    key = jax.random.fold_in(key, 7)
    keys = jax.random.split(key, 4)
    span = LEN // N_SEQ
    head_len = jax.random.randint(keys[0], (NSEQ, 1), MINDOC, span)
    long_end = jax.random.randint(keys[1], (NSEQ, 1), LEN - span + 1, LEN - MINDOC + 1)
    forced = jax.random.randint(keys[2], (), 0, NSEQ)
    is_forced = jnp.arange(NSEQ)[:, None] == forced
    long_end = jnp.where(is_forced, LEN - span + 1, long_end)
    tail_most = (LEN - long_end) // MINDOC
    picked = jax.random.randint(keys[3], (NSEQ, 1), 0, 1 << 30) % tail_most + 1
    tail_count = jnp.where(is_forced, tail_most, picked)
    positions = jnp.arange(LEN)[None, :]
    in_tail = 2 + jnp.minimum((positions - long_end) // MINDOC, tail_count - 1)
    result = jnp.where(positions < head_len, 0, jnp.where(positions < long_end, 1, in_tail))
    return result.astype(jnp.int32)


def level_of(own_key, extent, cuts, smallest, top_value):
    def one(dim, shards_of):
        steps = jax.random.uniform(jax.random.fold_in(jax.random.fold_in(own_key, 6), dim), (shards_of,), jnp.float32, smallest / len(cuts), top_value / len(cuts))
        return jnp.repeat(jnp.exp(steps), extent[dim] // shards_of).reshape((-1,) + (1,) * (len(extent) - dim - 1))

    factor_of = one(*cuts[0])
    for cut in cuts[1:]:
        factor_of = factor_of * one(*cut)
    return factor_of


def gaussian(key, dims, deviation, most, pieces=(), held_as=jnp.bfloat16):
    array = jax.random.normal(key, dims, jnp.float32) * deviation
    if len(pieces) > 0:
        array = level_of(key, dims, pieces, -0.22, 0.18) * array
    return jnp.clip(array, min=-most, max=most).astype(held_as)


def setup_inputs(seed: int = 0) -> dict:
    splits = jax.random.split(jax.random.key(seed), 19)
    tokens = gaussian(splits[0], (NSEQ, LEN, D), 1.0, 6.0, ((0, 8), (1, 4)))
    cotangent = gaussian(splits[1], (NSEQ, LEN, D), 1.0, 6.0, ((0, 8), (1, 4)))
    segments = draw_segments(jax.random.fold_in(splits[18], 71), 0)
    w_query = gaussian(splits[3], (D, D), (D // 2) ** -0.5, 0.3125, ((0, 32),))
    w_key = gaussian(splits[4], (D, D), (D // 2) ** -0.5, 0.3125, ((0, 32),))
    w_value = gaussian(splits[5], (D, D), D ** -0.5, 0.21875, ((0, 32),))
    w_out = gaussian(splits[6], (D, D), (D // 32) ** -0.5, 1.25, ((0, 32),))
    w_up = gaussian(splits[7], (D, FF), D ** -0.5, 0.21875, ((0, 32),))
    w_down = gaussian(splits[8], (FF, D), FF ** -0.5, 0.109375, ((0, 32),))
    ln1_gain = jnp.clip(1.0 + 0.15 * jax.random.normal(splits[9], (D,), jnp.float32), 0.25, 1.75).astype(jnp.bfloat16)
    ln1_shift = gaussian(splits[10], (D,), 0.3, 4.0, ((0, 32),))
    query_bias = gaussian(splits[11], (D,), 0.3, 4.0, ((0, 32),))
    value_bias = gaussian(splits[12], (D,), 0.3, 4.0, ((0, 32),))
    out_bias = gaussian(splits[13], (D,), 0.3, 4.0, ((0, 32),))
    ln2_gain = jnp.clip(1.0 + 0.15 * jax.random.normal(splits[14], (D,), jnp.float32), 0.25, 1.75).astype(jnp.bfloat16)
    ln2_shift = gaussian(splits[15], (D,), 0.3, 4.0, ((0, 32),))
    up_bias = gaussian(splits[16], (FF,), 0.5, 4.0, ((0, 32),))
    down_bias = gaussian(splits[17], (D,), 0.3, 4.0, ((0, 32),))
    return dict(tokens=tokens, cotangent=cotangent, segments=segments, w_query=w_query, w_key=w_key, w_value=w_value, w_out=w_out, w_up=w_up, w_down=w_down, ln1_gain=ln1_gain, ln1_shift=ln1_shift, query_bias=query_bias, value_bias=value_bias, out_bias=out_bias, ln2_gain=ln2_gain, ln2_shift=ln2_shift, up_bias=up_bias, down_bias=down_bias)


EPSILON = 1e-05
MASKED = -1e+30

@jax.custom_vjp
def low(v):
    return lax.optimization_barrier(v.astype(jnp.bfloat16)).astype(jnp.float32)

@jax.custom_vjp
def low_back(v):
    return v

def low_keep(v):
    return (low(v), None)

def low_pass(kept, grad):
    return (grad,)

def back_keep(v):
    return (v, None)

def back_low(kept, grad):
    return (low(grad),)
low.defvjp(low_keep, low_pass)
low_back.defvjp(back_keep, back_low)

def product(left, right):
    return jnp.matmul(left, right, precision=lax.Precision.HIGHEST)

def layer_norm(value, gain, shift):
    mean = lax.optimization_barrier(jnp.mean(value, -1, keepdims=True))
    centred = value - mean
    variance = lax.optimization_barrier(jnp.mean(centred * centred, -1, keepdims=True))
    return centred * lax.rsqrt(variance + EPSILON) * gain + shift

def attend(operands):
    query, key_rows, value_rows, segment = operands
    positions = jnp.arange(LEN)
    score_scale = 1.0 / math.sqrt(HD)
    scores = jnp.einsum('qhd,khd->hqk', query.reshape(LEN, H, HD), key_rows.reshape(LEN, H, HD), precision=lax.Precision.HIGHEST) * score_scale
    scores = low_back(scores)
    allowed = (segment[:, None] == segment[None, :]) & (positions[None, :] <= positions[:, None])
    scores = jnp.where(allowed[None], scores, MASKED)
    attn_weights = low(jax.nn.softmax(scores, axis=-1))
    mixed = jnp.einsum('hqk,khd->qhd', attn_weights, value_rows.reshape(LEN, H, HD), precision=lax.Precision.HIGHEST)
    return mixed.reshape(LEN, D)

def forward(params, inputs, segment):
    w_query, w_key, w_value, w_out, w_up, w_down, ln1_gain, ln1_shift, query_bias, value_bias, out_bias, ln2_gain, ln2_shift, up_bias, down_bias = params
    first = low(layer_norm(inputs, ln1_gain, ln1_shift))
    query = low(low_back(product(first, w_query) + query_bias))
    key_rows = low(low_back(product(first, w_key)))
    value_rows = low(low_back(product(first, w_value) + value_bias))
    mixed = lax.map(jax.checkpoint(attend), (query, key_rows, value_rows, segment))
    mixed = low(low_back(mixed))
    resid = inputs + low_back(product(mixed, w_out) + out_bias)
    second = low(layer_norm(resid, ln2_gain, ln2_shift))
    hidden_pre = low_back(product(second, w_up) + up_bias)
    hidden = low(jax.nn.gelu(hidden_pre, approximate=False))
    return resid + low_back(product(hidden, w_down) + down_bias)

def reference(tokens, cotangent, segments, w_query, w_key, w_value, w_out, w_up, w_down, ln1_gain, ln1_shift, query_bias, value_bias, out_bias, ln2_gain, ln2_shift, up_bias, down_bias):
    params = tuple((array_in.astype(jnp.float32) for array_in in (w_query, w_key, w_value, w_out, w_up, w_down, ln1_gain, ln1_shift, query_bias, value_bias, out_bias, ln2_gain, ln2_shift, up_bias, down_bias)))
    groups = NSEQ // S_DEV
    inputs = tokens.astype(jnp.float32).reshape(groups, S_DEV, LEN, D)
    grads_in = cotangent.astype(jnp.float32).reshape(groups, S_DEV, LEN, D)
    seg_groups = segments.reshape(groups, S_DEV, LEN)

    def one_group(summed, entry):
        group_in, group_grad, group_seg = entry
        group_out, pull = jax.vjp(lambda prm, val: forward(prm, val, group_seg), params, group_in)
        grad_params, grad_group = pull(group_grad)
        summed = jax.tree.map(jnp.add, summed, grad_params)
        return (summed, (group_out, grad_group))
    zeros = tuple((jnp.zeros_like(array_in) for array_in in params))
    summed, (outputs, grad_inputs) = lax.scan(one_group, zeros, (inputs, grads_in, seg_groups))
    g_query, g_key, g_value, g_out, g_up, g_down, g_gain1, g_shift1, g_qbias, g_vbias, g_obias, g_gain2, g_shift2, g_upbias, g_downbias = summed
    return (outputs.reshape(NSEQ, LEN, D), grad_inputs.reshape(NSEQ, LEN, D), g_query, g_key, g_value, g_out, g_up, g_down, g_gain1, g_shift1, g_qbias, g_vbias, g_obias, g_gain2, g_shift2, g_upbias, g_downbias)
```

```python
import functools
import math

import jax
import jax.numpy as jnp
from jax import lax
from jax.experimental import pallas as pl
from jax.experimental.pallas import tpu as pltpu
from jax.sharding import PartitionSpec as P

H = 12
EPSILON = 1e-05
MASKED = -1e30
F32 = jnp.float32
BF16 = jnp.bfloat16
LANES = 128


def dot_nt(a, b):
    return lax.dot_general(a, b, (((1,), (1,)), ((), ())), preferred_element_type=F32)


def dot_tn(a, b):
    return lax.dot_general(a, b, (((0,), (0,)), ((), ())), preferred_element_type=F32)


def dot_nn(a, b):
    return jnp.dot(a, b, preferred_element_type=F32)


def attend_kernel(me_ref, qkv_ref, seg_row_ref, seg_col_ref, low_ref, full_ref, lse_ref, *, heads, hd):
    me = me_ref[0]
    qi = pl.program_id(0)
    rq = qi ^ me
    block = qkv_ref.shape[1]
    width = heads * hd
    scale = jnp.asarray(1.0 / math.sqrt(hd), BF16)
    queries = [qkv_ref[rq, :, h * hd : (h + 1) * hd] * scale for h in range(heads)]
    seg_q = seg_row_ref[rq]

    def step(rk, state, causal):
        allowed = seg_col_ref[rk] == seg_q
        if causal:
            k_pos = lax.broadcasted_iota(jnp.int32, (block, block), 0)
            q_pos = lax.broadcasted_iota(jnp.int32, (block, block), 1)
            allowed = allowed & (k_pos <= q_pos)
        new = []
        for h in range(heads):
            top, total, mixed = state[h]
            key = qkv_ref[rk, :, width + h * hd : width + (h + 1) * hd]
            value = qkv_ref[rk, :, 2 * width + h * hd : 2 * width + (h + 1) * hd]
            scores = jnp.where(allowed, dot_nt(key, queries[h]), MASKED)
            higher = jnp.maximum(top, jnp.max(scores, 0, keepdims=True))
            weights = jnp.exp(scores - higher)
            fade = jnp.exp(top - higher)
            total = total * fade + jnp.sum(weights, 0, keepdims=True)
            mixed = mixed * fade + dot_tn(value, weights.astype(BF16))
            new.append((higher, total, mixed))
        return tuple(new)

    start = tuple(
        (jnp.full((1, block), MASKED, F32), jnp.zeros((1, block), F32), jnp.zeros((hd, block), F32))
        for _ in range(heads)
    )
    state = lax.fori_loop(0, qi, lambda kj, c: step(kj ^ me, c, False), start)
    state = step(rq, state, True)
    rows = []
    for h in range(heads):
        top, total, mixed = state[h]
        rows.append(mixed / total)
        lse_ref[0, h : h + 1, :] = top + jnp.log(total)
    full = jnp.concatenate(rows, 0)
    full_ref[0] = full
    low_ref[0] = full.T.astype(BF16)


def attend(me, qkv, seg_row, seg_col, heads, hd):
    n, block, _ = qkv.shape
    width = heads * hd

    def whole(shape):
        return pl.BlockSpec(shape, lambda i, me: (0,) * len(shape))

    def own(shape):
        return pl.BlockSpec(shape, lambda i, me: (i ^ me[0], 0, 0))

    return pl.pallas_call(
        functools.partial(attend_kernel, heads=heads, hd=hd),
        grid_spec=pltpu.PrefetchScalarGridSpec(
            num_scalar_prefetch=1,
            grid=(n,),
            in_specs=[whole(qkv.shape), whole(seg_row.shape), whole(seg_col.shape)],
            out_specs=[own((1, block, width)), own((1, width, block)), own((1, 8, block))],
        ),
        out_shape=[
            jax.ShapeDtypeStruct((n, block, width), BF16),
            jax.ShapeDtypeStruct((n, width, block), F32),
            jax.ShapeDtypeStruct((n, 8, block), F32),
        ],
        compiler_params=pltpu.CompilerParams(vmem_limit_bytes=40 * 1024 * 1024),
        cost_estimate=pl.CostEstimate(
            flops=20 * 1000**3, bytes_accessed=8 * 1000**2, transcendentals=8 * 1000**2
        ),
        name="attend",
    )(me, qkv, seg_row, seg_col)


def attend_back_kernel(
    me_ref, qkv_ref, go_ref, full_ref, lse_ref, seg_row_ref, seg_col_ref, grad_ref, gq_ref, dot_ref, *, heads, hd
):
    me = me_ref[0]
    kj = pl.program_id(0)
    rk = kj ^ me
    n, block, _ = qkv_ref.shape
    width = heads * hd
    scale = 1.0 / math.sqrt(hd)
    low_scale = jnp.asarray(scale, BF16)

    @pl.when(kj == 0)
    def _():
        gq_ref[...] = jnp.zeros_like(gq_ref)
        for b in range(n):
            prod = go_ref[b].astype(F32).T * full_ref[b]
            for h in range(heads):
                dot_ref[b, h : h + 1, :] = jnp.sum(prod[h * hd : (h + 1) * hd], 0, keepdims=True)

    keys = [qkv_ref[rk, :, width + h * hd : width + (h + 1) * hd] for h in range(heads)]
    values = [qkv_ref[rk, :, 2 * width + h * hd : 2 * width + (h + 1) * hd] for h in range(heads)]
    seg_k = seg_col_ref[rk]

    def step(rq, state, causal):
        allowed = seg_k == seg_row_ref[rq]
        if causal:
            k_pos = lax.broadcasted_iota(jnp.int32, (block, block), 0)
            q_pos = lax.broadcasted_iota(jnp.int32, (block, block), 1)
            allowed = allowed & (k_pos <= q_pos)
        new = []
        for h in range(heads):
            gk, gv = state[h]
            query = qkv_ref[rq, :, h * hd : (h + 1) * hd] * low_scale
            go = go_ref[rq, :, h * hd : (h + 1) * hd]
            scores = jnp.where(allowed, dot_nt(keys[h], query), MASKED)
            weights = jnp.exp(scores - lse_ref[rq, h : h + 1, :])
            gw = dot_nt(values[h], go)
            ds = (weights * (gw - dot_ref[rq, h : h + 1, :])).astype(BF16)
            gv = gv + dot_nn(weights.astype(BF16), go)
            gk = gk + dot_nn(ds, query)
            gq_ref[rq, h * hd : (h + 1) * hd, :] += dot_tn(keys[h], ds)
            new.append((gk, gv))
        return tuple(new)

    zero = jnp.zeros((block, hd), F32)
    state = step(rk, tuple((zero, zero) for _ in range(heads)), True)
    state = lax.fori_loop(kj + 1, n, lambda qi, c: step(qi ^ me, c, False), state)
    grad_ref[0, :, :width] = (gq_ref[rk] * scale).T.astype(BF16)
    for h in range(heads):
        gk, gv = state[h]
        grad_ref[0, :, width + h * hd : width + (h + 1) * hd] = gk.astype(BF16)
        grad_ref[0, :, 2 * width + h * hd : 2 * width + (h + 1) * hd] = gv.astype(BF16)


def attend_back(me, qkv, go, full, lse, seg_row, seg_col, heads, hd):
    n, block, wide = qkv.shape
    width = heads * hd

    def whole(shape):
        return pl.BlockSpec(shape, lambda i, me: (0,) * len(shape))

    return pl.pallas_call(
        functools.partial(attend_back_kernel, heads=heads, hd=hd),
        grid_spec=pltpu.PrefetchScalarGridSpec(
            num_scalar_prefetch=1,
            grid=(n,),
            in_specs=[whole(a.shape) for a in (qkv, go, full, lse, seg_row, seg_col)],
            out_specs=pl.BlockSpec((1, block, wide), lambda i, me: (i ^ me[0], 0, 0)),
            scratch_shapes=[pltpu.VMEM((n, width, block), F32), pltpu.VMEM((n, 8, block), F32)],
        ),
        out_shape=jax.ShapeDtypeStruct((n, block, wide), BF16),
        compiler_params=pltpu.CompilerParams(vmem_limit_bytes=40 * 1024 * 1024),
        cost_estimate=pl.CostEstimate(
            flops=40 * 1000**3, bytes_accessed=12 * 1000**2, transcendentals=8 * 1000**2
        ),
        name="attend_back",
    )(me, qkv, go, full, lse, seg_row, seg_col)


def normed_parts(value):
    mean = jnp.mean(value, -1, keepdims=True)
    centred = value - mean
    inv_std = lax.rsqrt(jnp.mean(centred * centred, -1, keepdims=True) + EPSILON)
    return centred * inv_std, inv_std


def normalize_back(grad_in, normed, inv_std, gain):
    scaled = grad_in * gain
    return inv_std * (
        scaled
        - jnp.mean(scaled, -1, keepdims=True)
        - normed * jnp.mean(scaled * normed, -1, keepdims=True)
    )


def gelu_and_slope(value):
    cumul = 0.5 * (1.0 + lax.erf(value * (1.0 / math.sqrt(2.0))))
    slope = cumul + value * jnp.exp(-0.5 * value * value) * (1.0 / math.sqrt(2.0 * math.pi))
    return value * cumul, slope


def swap(value, axis, size, mask):
    return lax.ppermute(value, axis, [(i, i ^ mask) for i in range(size)])


def bits_of(size):
    count = size.bit_length() - 1
    return [1 << b for b in range(count)]


def ordered(parts, index):
    parts = [part[None] for part in parts]
    bit = 1
    while len(parts) > 1:
        on = (index & bit) != 0
        parts = [
            jnp.where(on, jnp.concatenate([b, a], 0), jnp.concatenate([a, b], 0))
            for a, b in zip(parts[::2], parts[1::2])
        ]
        bit *= 2
    return parts[0]


def spread_dp(value, index, size):
    masks = bits_of(size)[::-1]
    shape = value.shape
    value = value.reshape((1,) * len(masks) + shape)
    for axis, mask in enumerate(masks):
        other = swap(value, "dp", size, mask)
        on = (index & mask) != 0
        value = jnp.where(
            on, jnp.concatenate([other, value], axis), jnp.concatenate([value, other], axis)
        )
    return value.reshape((size,) + shape)


def collect_dp(value, index, size, last=F32):
    masks = bits_of(size)
    shape = value.shape[1:]
    value = value.reshape((2,) * len(masks) + shape)
    for step, mask in enumerate(masks):
        axis = len(masks) - 1 - step
        on = ((index & mask) != 0).astype(jnp.int32)
        keep = lax.dynamic_index_in_dim(value, on, axis, False)
        send = lax.dynamic_index_in_dim(value, 1 - on, axis, False)
        got = swap(send, "dp", size, mask)
        value = keep.astype(F32) + got.astype(F32)
        value = value.astype(BF16 if step < len(masks) - 1 else last)
    return value


def collect_seq(parts, size, last=BF16):
    mask = 1
    while len(parts) > 1:
        sent = [swap(b, "seq", size, mask) for b in parts[1::2]]
        kind = BF16 if len(parts) > 2 else last
        parts = [(a.astype(F32) + b.astype(F32)).astype(kind) for a, b in zip(parts[::2], sent)]
        mask *= 2
    return parts[0]


def spread_seq(value, size):
    got = {0: value}
    for mask in bits_of(size)[::-1]:
        for p in list(got):
            got[p | mask] = swap(got[p], "seq", size, mask)
    return [got[p] for p in range(size)]


def trade_seq(pieces, index, size):
    return [
        swap(lax.dynamic_index_in_dim(pieces, index ^ p, 0, False), "seq", size, p)
        if p
        else lax.dynamic_index_in_dim(pieces, index, 0, False)
        for p in range(size)
    ]


def body(
    nd,
    ns,
    tokens,
    cotangent,
    segments,
    w_query,
    w_key,
    w_value,
    w_out,
    w_up,
    w_down,
    ln1_gain,
    ln1_shift,
    query_bias,
    value_bias,
    out_bias,
    ln2_gain,
    ln2_shift,
    up_bias,
    down_bias,
):
    d = lax.axis_index("dp")
    s = lax.axis_index("seq")
    me = s.astype(jnp.int32).reshape(1)
    _, block, dm = tokens.shape
    hd = dm // H
    heads = H // ns
    width = heads * hd
    rows = w_query.shape[0]
    ff_rows, ff = w_down.shape[0], w_up.shape[1]
    ratio = ff_rows // rows
    part = ff // ns

    x_own = tokens.reshape(block, dm)
    x_all = jnp.stack(spread_seq(x_own, ns))
    segs = jnp.stack(spread_seq(segments.reshape(block), ns))
    seg_row = segs.reshape(ns, 1, block)
    seg_col = segs.reshape(ns, block, 1)

    cols = jnp.concatenate([w.reshape(rows, ns, width) for w in (w_query, w_key, w_value)], 2)
    vectors = [ln1_gain, ln1_shift, ln2_gain, ln2_shift, out_bias, down_bias, query_bias, value_bias]
    vec = jnp.concatenate([jnp.stack(vectors), up_bias.reshape(ratio, rows)], 0).T
    vec = jnp.pad(vec, ((0, 0), (0, LANES - vec.shape[1])))
    vec = jnp.broadcast_to(vec[:, None], (rows, ns, LANES))
    pieces = jnp.concatenate([cols, vec], 2).transpose(1, 0, 2)
    got = spread_dp(ordered(trade_seq(pieces, s, ns), s), d, nd)
    got = got.reshape(dm, 3 * width + LANES)
    w_qkv = got[:, : 3 * width]
    vecs = got[:, 3 * width :].T.astype(F32)
    gain_one, shift_one, gain_two, shift_two, out_add, down_add, q_add, v_add = [vecs[i] for i in range(8)]
    up_add = vecs[8 : 8 + ratio].reshape(ratio, nd, ns, rows).transpose(2, 1, 0, 3).reshape(ns, part)
    up_add = jnp.stack([lax.dynamic_index_in_dim(up_add, s ^ p, 0, False) for p in range(ns)])

    up_cols = w_up.reshape(rows, nd, ns, ff_rows).transpose(2, 0, 1, 3).reshape(ns, rows, part)
    up_piece = ordered(trade_seq(up_cols, s, ns), s).reshape(ns * rows, part)
    up_out = spread_dp(jnp.concatenate([w_out, up_piece], 0), d, nd)
    up_out = spread_seq(up_out, ns)
    w_ups = [piece[:, rows:].reshape(dm, part) for piece in up_out]
    w_outs = ordered([piece[:, :rows] for piece in up_out], s)
    w_outs = w_outs.transpose(1, 0, 2, 3).reshape(ns, width, dm)
    w_outs = jnp.concatenate([lax.dynamic_index_in_dim(w_outs, s ^ p, 0, False) for p in range(ns)], 0)
    down = spread_dp(w_down, d, nd).reshape(part, dm)
    w_downs = spread_seq(down, ns)

    x_all_f = x_all.astype(F32)
    n_one, inv_one = normed_parts(x_all_f)
    h_one = (n_one * gain_one + shift_one).astype(BF16)
    add = jnp.concatenate(
        [
            lax.dynamic_slice_in_dim(q_add, s * width, width),
            jnp.zeros((width,), F32),
            lax.dynamic_slice_in_dim(v_add, s * width, width),
        ]
    )
    qkv = (jnp.einsum("nbk,kc->nbc", h_one, w_qkv, preferred_element_type=F32) + add).astype(BF16)
    o_low, o_full, lse = attend(me, qkv, seg_row, seg_col, heads, hd)
    ol = jnp.concatenate([o_low[0]] + [swap(o_low[p], "seq", ns, p) for p in range(1, ns)], 1)
    x_f = x_own.astype(F32)
    x_two = x_f + dot_nn(ol, w_outs) + out_add
    n_two, inv_two = normed_parts(x_two)
    h_two = (n_two * gain_two + shift_two).astype(BF16)
    g = cotangent.reshape(block, dm)
    g_f = g.astype(F32)
    out = x_two + down_add
    gh_two = jnp.zeros((block, dm), F32)
    gus, d_downs, d_ups, d_up_adds = [], [], [], []
    for p in range(ns):
        u = dot_nn(h_two, w_ups[p]) + up_add[p]
        act, slope = gelu_and_slope(u)
        act = act.astype(BF16)
        out = out + dot_nn(act, w_downs[p])
        gu = (dot_nt(g, w_downs[p]) * slope).astype(BF16)
        d_downs.append(dot_tn(act, g).astype(BF16))
        gus.append(gu)
    for p in range(ns):
        d_ups.append(dot_tn(h_two, gus[p]).astype(BF16))
        d_up_adds.append(jnp.sum(gus[p].astype(F32), 0))
        gh_two = gh_two + dot_nt(gus[p], w_ups[p])
    gx_two = g_f + normalize_back(gh_two, n_two, inv_two, gain_two)
    gb = gx_two.astype(BF16)
    go = dot_nt(gb, w_outs).astype(BF16)
    d_out = dot_tn(ol, gb).astype(BF16).reshape(ns, width, dm)
    gos = [go[:, p * width : (p + 1) * width] for p in range(ns)]
    go_all = jnp.stack([gos[0]] + [swap(gos[p], "seq", ns, p) for p in range(1, ns)])

    sum_down = collect_seq(d_downs, ns).reshape(nd, ff_rows, dm)
    sum_down = collect_dp(sum_down, d, nd)
    d_out = ordered([d_out[p] for p in range(ns)], s).reshape(nd, ns, rows, dm)
    d_outs = [lax.dynamic_index_in_dim(d_out, s ^ p, 1, False) for p in range(ns)]
    mixed = [
        jnp.concatenate([d_outs[p], d_ups[p].reshape(nd, ns * rows, part)], 1) for p in range(ns)
    ]
    sum_up = collect_dp(collect_seq(mixed, ns), d, nd)
    sum_out = sum_up[:rows]
    sum_up = ordered(trade_seq(sum_up[rows:].reshape(ns, rows, part), s, ns), s)
    sum_up = sum_up.reshape(ns, rows, nd, ff_rows).transpose(1, 2, 0, 3).reshape(rows, ff)

    grads = attend_back(me, qkv, go_all, o_full, lse, seg_row, seg_col, heads, hd)
    gh_part = jnp.einsum("nbc,kc->nbk", grads, w_qkv, preferred_element_type=F32)
    d_qkv = jnp.einsum("nbk,nbc->kc", h_one, grads, preferred_element_type=F32)
    d_add = jnp.sum(grads.astype(F32), (0, 1))
    gh_low = gh_part.astype(BF16)
    gh_one = collect_seq([gh_low[p] for p in range(ns)], ns, F32)
    n_own, inv_own = normed_parts(x_f)
    grad_x = gx_two + normalize_back(gh_one, n_own, inv_own, gain_one)

    def at_heads(v):
        return lax.dynamic_update_slice_in_dim(jnp.zeros((dm,), F32), v, s * width, 0)

    d_vecs = jnp.stack(
        [
            jnp.sum(gh_part * n_one, (0, 1)),
            jnp.sum(gh_part, (0, 1)),
            jnp.sum(gh_two * n_two, 0),
            jnp.sum(gh_two, 0),
            jnp.sum(gb.astype(F32), 0),
            jnp.sum(g_f, 0),
            at_heads(d_add[:width]),
            at_heads(d_add[2 * width :]),
        ]
    )
    d_up_add = ordered(d_up_adds, s).reshape(ns, nd, ratio, rows).transpose(2, 1, 0, 3).reshape(ratio, dm)
    d_vecs = jnp.concatenate([d_vecs, d_up_add], 0)
    count = d_vecs.shape[0]
    d_vecs = jnp.pad(d_vecs, ((0, LANES - count), (0, 0))).T
    blob = jnp.concatenate([d_qkv, d_vecs], 1).astype(BF16)
    blob = collect_dp(blob.reshape(nd, ns * rows, 3 * width + LANES), d, nd)
    blobs = trade_seq(blob.reshape(ns, rows, 3 * width + LANES), s, ns)
    vec_sum = sum(b[:, 3 * width :] for b in blobs).T
    sums = ordered([b[:, : 3 * width] for b in blobs], s).reshape(ns, rows, 3, width)
    sums = sums.transpose(2, 1, 0, 3).reshape(3, rows, dm)
    v = [vec_sum[i] for i in range(8)]
    sum_up_bias = vec_sum[8 : 8 + ratio].reshape(ff_rows)
    return (
        out.reshape(1, block, dm),
        grad_x.reshape(1, block, dm),
        sums[0],
        sums[1],
        sums[2],
        sum_out,
        sum_up,
        sum_down,
        v[0],
        v[1],
        v[6],
        v[7],
        v[4],
        v[2],
        v[3],
        sum_up_bias,
        v[5],
    )


def solution(mesh):
    act = P("dp", "seq", None)
    weight = P(("dp", "seq"), None)
    vector = P(("dp", "seq"))
    return jax.shard_map(
        functools.partial(body, mesh.shape["dp"], mesh.shape["seq"]),
        mesh=mesh,
        in_specs=(act, act, P("dp", "seq")) + (weight,) * 6 + (vector,) * 9,
        out_specs=(act, act) + (weight,) * 6 + (vector,) * 9,
        check_vma=False,
    )
```

```python
import functools
import math

import jax
import jax.numpy as jnp
from jax import lax
from jax.experimental import pallas as pl
from jax.experimental.pallas import tpu as pltpu
from jax.sharding import PartitionSpec as P

H = 12
EPSILON = 1e-05
MASKED = -1e30
F32 = jnp.float32
BF16 = jnp.bfloat16
LANES = 128


def dot_nt(a, b):
    return lax.dot_general(a, b, (((1,), (1,)), ((), ())), preferred_element_type=F32)


def dot_tn(a, b):
    return lax.dot_general(a, b, (((0,), (0,)), ((), ())), preferred_element_type=F32)


def dot_nn(a, b):
    return jnp.dot(a, b, preferred_element_type=F32)


def attend_kernel(me_ref, qkv_ref, seg_row_ref, seg_col_ref, low_ref, full_ref, lse_ref, *, heads, hd):
    me = me_ref[0]
    qi = pl.program_id(0)
    rq = qi ^ me
    block = qkv_ref.shape[1]
    width = heads * hd
    scale = jnp.asarray(1.0 / math.sqrt(hd), BF16)
    queries = [qkv_ref[rq, :, h * hd : (h + 1) * hd] * scale for h in range(heads)]
    seg_q = seg_row_ref[rq]

    def step(rk, state, causal):
        allowed = seg_col_ref[rk] == seg_q
        if causal:
            k_pos = lax.broadcasted_iota(jnp.int32, (block, block), 0)
            q_pos = lax.broadcasted_iota(jnp.int32, (block, block), 1)
            allowed = allowed & (k_pos <= q_pos)
        new = []
        for h in range(heads):
            top, total, mixed = state[h]
            key = qkv_ref[rk, :, width + h * hd : width + (h + 1) * hd]
            value = qkv_ref[rk, :, 2 * width + h * hd : 2 * width + (h + 1) * hd]
            scores = jnp.where(allowed, dot_nt(key, queries[h]), MASKED)
            higher = jnp.maximum(top, jnp.max(scores, 0, keepdims=True))
            weights = jnp.exp(scores - higher)
            fade = jnp.exp(top - higher)
            total = total * fade + jnp.sum(weights, 0, keepdims=True)
            mixed = mixed * fade + dot_tn(value, weights.astype(BF16))
            new.append((higher, total, mixed))
        return tuple(new)

    start = tuple(
        (jnp.full((1, block), MASKED, F32), jnp.zeros((1, block), F32), jnp.zeros((hd, block), F32))
        for _ in range(heads)
    )
    state = lax.fori_loop(0, qi, lambda kj, c: step(kj ^ me, c, False), start)
    state = step(rq, state, True)
    rows = []
    for h in range(heads):
        top, total, mixed = state[h]
        rows.append(mixed / total)
        lse_ref[0, h : h + 1, :] = top + jnp.log(total)
    full = jnp.concatenate(rows, 0)
    full_ref[0] = full
    low_ref[0] = full.astype(BF16)


def attend(me, qkv, seg_row, seg_col, heads, hd):
    n, block, _ = qkv.shape
    width = heads * hd

    def whole(shape):
        return pl.BlockSpec(shape, lambda i, me: (0,) * len(shape))

    def own(shape):
        return pl.BlockSpec(shape, lambda i, me: (i ^ me[0], 0, 0))

    return pl.pallas_call(
        functools.partial(attend_kernel, heads=heads, hd=hd),
        grid_spec=pltpu.PrefetchScalarGridSpec(
            num_scalar_prefetch=1,
            grid=(n,),
            in_specs=[whole(qkv.shape), whole(seg_row.shape), whole(seg_col.shape)],
            out_specs=[own((1, width, block)), own((1, width, block)), own((1, 8, block))],
        ),
        out_shape=[
            jax.ShapeDtypeStruct((n, width, block), BF16),
            jax.ShapeDtypeStruct((n, width, block), F32),
            jax.ShapeDtypeStruct((n, 8, block), F32),
        ],
        compiler_params=pltpu.CompilerParams(vmem_limit_bytes=40 * 1024 * 1024),
        cost_estimate=pl.CostEstimate(
            flops=20 * 1000**3, bytes_accessed=8 * 1000**2, transcendentals=8 * 1000**2
        ),
        name="attend",
    )(me, qkv, seg_row, seg_col)


def attend_back_kernel(
    me_ref, qkv_ref, go_ref, full_ref, lse_ref, seg_row_ref, seg_col_ref, grad_ref, gq_ref, dot_ref, *, heads, hd
):
    me = me_ref[0]
    kj = pl.program_id(0)
    rk = kj ^ me
    n, block, _ = qkv_ref.shape
    width = heads * hd
    scale = 1.0 / math.sqrt(hd)
    low_scale = jnp.asarray(scale, BF16)

    @pl.when(kj == 0)
    def _():
        gq_ref[...] = jnp.zeros_like(gq_ref)
        for b in range(n):
            prod = go_ref[b].astype(F32) * full_ref[b]
            for h in range(heads):
                dot_ref[b, h : h + 1, :] = jnp.sum(prod[h * hd : (h + 1) * hd], 0, keepdims=True)

    keys = [qkv_ref[rk, :, width + h * hd : width + (h + 1) * hd] for h in range(heads)]
    values = [qkv_ref[rk, :, 2 * width + h * hd : 2 * width + (h + 1) * hd] for h in range(heads)]
    seg_k = seg_col_ref[rk]

    def step(rq, state, causal):
        allowed = seg_k == seg_row_ref[rq]
        if causal:
            k_pos = lax.broadcasted_iota(jnp.int32, (block, block), 0)
            q_pos = lax.broadcasted_iota(jnp.int32, (block, block), 1)
            allowed = allowed & (k_pos <= q_pos)
        new = []
        for h in range(heads):
            gk, gv = state[h]
            query = qkv_ref[rq, :, h * hd : (h + 1) * hd] * low_scale
            go = go_ref[rq, h * hd : (h + 1) * hd, :]
            scores = jnp.where(allowed, dot_nt(keys[h], query), MASKED)
            weights = jnp.exp(scores - lse_ref[rq, h : h + 1, :])
            gw = dot_nn(values[h], go)
            ds = (weights * (gw - dot_ref[rq, h : h + 1, :])).astype(BF16)
            gv = gv + dot_nt(weights.astype(BF16), go)
            gk = gk + dot_nn(ds, query)
            gq_ref[rq, h * hd : (h + 1) * hd, :] += dot_tn(keys[h], ds)
            new.append((gk, gv))
        return tuple(new)

    zero = jnp.zeros((block, hd), F32)
    state = step(rk, tuple((zero, zero) for _ in range(heads)), True)
    state = lax.fori_loop(kj + 1, n, lambda qi, c: step(qi ^ me, c, False), state)
    grad_ref[0, :, :width] = (gq_ref[rk] * scale).T.astype(BF16)
    for h in range(heads):
        gk, gv = state[h]
        grad_ref[0, :, width + h * hd : width + (h + 1) * hd] = gk.astype(BF16)
        grad_ref[0, :, 2 * width + h * hd : 2 * width + (h + 1) * hd] = gv.astype(BF16)


def attend_back(me, qkv, go, full, lse, seg_row, seg_col, heads, hd):
    n, block, wide = qkv.shape
    width = heads * hd

    def whole(shape):
        return pl.BlockSpec(shape, lambda i, me: (0,) * len(shape))

    return pl.pallas_call(
        functools.partial(attend_back_kernel, heads=heads, hd=hd),
        grid_spec=pltpu.PrefetchScalarGridSpec(
            num_scalar_prefetch=1,
            grid=(n,),
            in_specs=[whole(a.shape) for a in (qkv, go, full, lse, seg_row, seg_col)],
            out_specs=pl.BlockSpec((1, block, wide), lambda i, me: (i ^ me[0], 0, 0)),
            scratch_shapes=[pltpu.VMEM((n, width, block), F32), pltpu.VMEM((n, 8, block), F32)],
        ),
        out_shape=jax.ShapeDtypeStruct((n, block, wide), BF16),
        compiler_params=pltpu.CompilerParams(vmem_limit_bytes=40 * 1024 * 1024),
        cost_estimate=pl.CostEstimate(
            flops=40 * 1000**3, bytes_accessed=12 * 1000**2, transcendentals=8 * 1000**2
        ),
        name="attend_back",
    )(me, qkv, go, full, lse, seg_row, seg_col)


def normed_parts(value):
    mean = jnp.mean(value, -1, keepdims=True)
    centred = value - mean
    inv_std = lax.rsqrt(jnp.mean(centred * centred, -1, keepdims=True) + EPSILON)
    return centred * inv_std, inv_std


def normalize_back(grad_in, normed, inv_std, gain):
    scaled = grad_in * gain
    return inv_std * (
        scaled
        - jnp.mean(scaled, -1, keepdims=True)
        - normed * jnp.mean(scaled * normed, -1, keepdims=True)
    )


def gelu_and_slope(value):
    cumul = 0.5 * (1.0 + lax.erf(value * (1.0 / math.sqrt(2.0))))
    slope = cumul + value * jnp.exp(-0.5 * value * value) * (1.0 / math.sqrt(2.0 * math.pi))
    return value * cumul, slope


def tie(value, *others):
    return lax.optimization_barrier((value,) + others)[0] if others else value


def swap(value, axis, size, mask):
    return lax.ppermute(value, axis, [(i, i ^ mask) for i in range(size)])


def bits_of(size):
    count = size.bit_length() - 1
    return [1 << b for b in range(count)]


def ordered(parts, index):
    parts = [part[None] for part in parts]
    bit = 1
    while len(parts) > 1:
        on = (index & bit) != 0
        parts = [
            jnp.where(on, jnp.concatenate([b, a], 0), jnp.concatenate([a, b], 0))
            for a, b in zip(parts[::2], parts[1::2])
        ]
        bit *= 2
    return parts[0]


def gathered_ids(masks):
    held, lists = [0], [[0]]
    for mask in masks:
        new = [r ^ mask for r in held]
        lists.append(new)
        held = held + new
    return lists


def settle(parts, index, size, masks, count):
    ids = gathered_ids(masks)
    rows = parts[0].shape[1] // count
    if rows % 16 == 0:
        return parts, ids
    held = sum(ids, [])
    at = jnp.asarray([held.index(r) for r in range(size)])
    whole = jnp.concatenate(parts, 0)[at[jnp.arange(size) ^ index]]
    whole = whole.reshape(size, count, rows, -1).transpose(1, 0, 2, 3)
    return [whole.reshape(1, size * count * rows, -1)], [[None]]


def place(refs, ids, index, count, put):
    for ref, held in zip(refs, ids):
        rows = ref.shape[1] // count
        for j, r in enumerate(held):
            where = slice(None) if r is None else pl.ds(pl.multiple_of((index ^ r) * rows, rows), rows)
            for k in range(count):
                put(k, where, ref[j, k * rows : (k + 1) * rows, :])


def halves(value, index, size, mask):
    value = value.reshape((-1, 2, mask) + value.shape[1:])
    on = ((index & mask) != 0).astype(jnp.int32)
    shape = (-1,) + value.shape[3:]
    keep = lax.dynamic_index_in_dim(value, on, 1, False).reshape(shape)
    return keep, lax.dynamic_index_in_dim(value, 1 - on, 1, False).reshape(shape)


def add_low(a, b, kind=BF16):
    return (a.astype(F32) + b.astype(F32)).astype(kind)


def collect_dp(value, index, size, last=F32, shift=0):
    masks = bits_of(size)
    shape = value.shape[1:]
    value = value.reshape((2,) * len(masks) + shape)
    for step, mask in enumerate(masks):
        axis = len(masks) - 1 - step
        on = ((index & mask) != 0).astype(jnp.int32)
        keep = lax.dynamic_index_in_dim(value, on, axis, False)
        send = lax.dynamic_index_in_dim(value, 1 - on, axis, False)
        got = swap(send, "dp", size << shift, mask << shift)
        value = keep.astype(F32) + got.astype(F32)
        value = value.astype(BF16 if step < len(masks) - 1 else last)
    return value


def collect_pairs(even, odd, size, tied=()):
    got = swap(odd, "seq", size, 1)
    sums = [(even[i].astype(F32) + got[i].astype(F32)).astype(BF16) for i in range(size // 2)]
    mask = 2
    while len(sums) > 2:
        sent = [swap(b, "seq", size, mask) for b in sums[1::2]]
        sums = [(a.astype(F32) + b.astype(F32)).astype(BF16) for a, b in zip(sums[::2], sent)]
        mask *= 2
    return sums[0], sums[1], swap(tie(sums[1], *tied), "seq", size, mask)


def spread_seq(value, size, gate=()):
    got = {0: value}
    for mask in bits_of(size)[::-1]:
        for p in list(got):
            got[p | mask] = swap(tie(got[p], *gate) if p else got[p], "seq", size, mask)
    return [got[p] for p in range(size)]


def trade_seq(pieces, index, size):
    return [
        swap(lax.dynamic_index_in_dim(pieces, index ^ p, 0, False), "seq", size, p)
        if p
        else lax.dynamic_index_in_dim(pieces, index, 0, False)
        for p in range(size)
    ]


def enter_kernel(me_ref, *refs, ids, n, width):
    count = len(ids)
    pieces, (x_ref, qkv_ref, w_ref, vec_ref, tile_ref, add_ref) = refs[:count], refs[count:]
    me = me_ref[0]

    @pl.when(pl.program_id(0) == 0)
    def _():
        def put(k, where, rows):
            w_ref[where, :] = rows[:, : 3 * width]
            tile_ref[where, :] = rows[:, 3 * width :].astype(F32)

        place(pieces, ids, me_ref[1], 1, put)
        vecs = tile_ref[...].T[:16]
        vec_ref[...] = vecs
        for i, row in ((0, 6), (2, 7)):
            add = vecs[row : row + 1, :width]
            for t in range(1, n):
                add = jnp.where(me == t, vecs[row : row + 1, t * width : (t + 1) * width], add)
            add_ref[0:1, i * width : (i + 1) * width] = add
        add_ref[0:1, width : 2 * width] = jnp.zeros((1, width), F32)

    normed, _ = normed_parts(x_ref[0].astype(F32))
    h = (normed * vec_ref[0:1, :] + vec_ref[1:2, :]).astype(BF16)
    qkv_ref[0] = (dot_nn(h, w_ref[...]) + add_ref[0:1, :]).astype(BF16)


def enter(me, pieces, ids, x_all, width):
    n, block, dm = x_all.shape

    def whole(shape):
        return pl.BlockSpec(shape, lambda i, me: (0,) * len(shape))

    def one(width):
        return pl.BlockSpec((1, block, width), lambda i, me: (i, 0, 0))

    return pl.pallas_call(
        functools.partial(enter_kernel, ids=ids, n=n, width=width),
        grid_spec=pltpu.PrefetchScalarGridSpec(
            num_scalar_prefetch=1,
            grid=(n,),
            in_specs=[whole(a.shape) for a in pieces] + [one(dm)],
            out_specs=[one(3 * width), whole((dm, 3 * width)), whole((16, dm))],
            scratch_shapes=[pltpu.VMEM((dm, LANES), F32), pltpu.VMEM((8, 3 * width), F32)],
        ),
        out_shape=[
            jax.ShapeDtypeStruct((n, block, 3 * width), BF16),
            jax.ShapeDtypeStruct((dm, 3 * width), BF16),
            jax.ShapeDtypeStruct((16, dm), F32),
        ],
        compiler_params=pltpu.CompilerParams(vmem_limit_bytes=40 * 1024 * 1024),
        cost_estimate=pl.CostEstimate(flops=5 * 1000**3, bytes_accessed=8 * 1000**2, transcendentals=0),
        name="enter",
    )(me, *pieces, x_all)


def feed_kernel(
    me_ref, *refs, n, tile, ids
):
    count = len(ids[0])
    got, left, right, refs = refs[:n], refs[n : n + count], refs[n + count : n + 2 * count], refs[n + 2 * count :]
    x_ref, g_ref, vec_ref = refs[:3]
    h_ref, act_ref, gu_ref, even_ref, odd_ref, x_two_ref, sum_ref, out_w_ref, down_ref, up_ref = refs[3:]
    me = me_ref[0]
    i = pl.program_id(0)
    part = up_ref.shape[1]
    width = got[0].shape[1]

    @pl.when(i == 0)
    def _():
        sum_ref[...] = jnp.zeros_like(sum_ref)
        for first, pieces, held in ((0, left, ids[0]), (part // 2, right, ids[1])):

            def put(k, where, rows, first=first):
                (out_w_ref, up_ref, down_ref)[k][where, first : first + part // 2] = rows

            place(pieces, held, me_ref[1], 3, put)

    x_two = x_ref[0].astype(F32) + vec_ref[4:5, :]
    for p in range(n):
        own = pl.ds(pl.multiple_of((me ^ p) * width, width), width)
        x_two = x_two + dot_tn(got[p][0], out_w_ref[own, :])

    @pl.when(i == 0)
    def _():
        x_two_ref[...] = x_two

    normed, _ = normed_parts(x_two)
    h = (normed * vec_ref[2:3, :] + vec_ref[3:4, :]).astype(BF16)
    h_ref[0] = h
    g = g_ref[0]
    total = None
    for t in range(0, part, tile):
        cols = slice(t, t + tile)
        u = dot_nn(h, up_ref[:, cols]) + vec_ref[8:9, cols]
        act, slope = gelu_and_slope(u)
        act_ref[0, :, cols] = act.astype(BF16)
        gu = (dot_nt(g, down_ref[cols, :]) * slope).astype(BF16)
        gu_ref[0, :, cols] = gu
        sum_ref[0:1, cols] += jnp.sum(gu.astype(F32), 0, keepdims=True)
        term = dot_nt(gu, up_ref[:, cols])
        total = term if total is None else total + term
    total = total.astype(BF16)

    @pl.when(i % 2 == 0)
    def _():
        even_ref[0] = total

    @pl.when(i % 2 == 1)
    def _():
        odd_ref[0] = total


def feed(me, got, left, right, ids, x_all, g_all, vecs):
    n, _, dm = x_all.shape
    block = g_all.shape[1]
    part = 2 * left[0].shape[2]
    width = got[0].shape[1]

    def whole(shape):
        return pl.BlockSpec(shape, lambda i, me: (0,) * len(shape))

    def one(width):
        return pl.BlockSpec((1, block, width), lambda i, me: (i, 0, 0))

    def half(width):
        return pl.BlockSpec((1, block, width), lambda i, me: (i // 2, 0, 0))

    def piece(p):
        return pl.BlockSpec((1, width, block), lambda i, me: (i ^ p, 0, 0))

    wide = jax.ShapeDtypeStruct((n, block, dm), BF16)
    pair = jax.ShapeDtypeStruct((n // 2, block, dm), BF16)
    hidden = jax.ShapeDtypeStruct((n, block, part), BF16)
    return pl.pallas_call(
        functools.partial(feed_kernel, n=n, tile=256 if part % 256 == 0 else part, ids=ids),
        grid_spec=pltpu.PrefetchScalarGridSpec(
            num_scalar_prefetch=1,
            grid=(n,),
            in_specs=[piece(p) for p in range(n)]
            + [whole(a.shape) for a in (*left, *right)]
            + [one(dm), one(dm), whole(vecs.shape)],
            out_specs=[
                one(dm),
                one(part),
                one(part),
                half(dm),
                half(dm),
                whole((block, dm)),
                whole((8, part)),
                whole((dm, dm)),
                whole((part, dm)),
            ],
            scratch_shapes=[pltpu.VMEM((dm, part), BF16)],
        ),
        out_shape=[
            wide,
            hidden,
            hidden,
            pair,
            pair,
            jax.ShapeDtypeStruct((block, dm), F32),
            jax.ShapeDtypeStruct((8, part), F32),
            jax.ShapeDtypeStruct((dm, dm), BF16),
            jax.ShapeDtypeStruct((part, dm), BF16),
        ],
        compiler_params=pltpu.CompilerParams(vmem_limit_bytes=48 * 1024 * 1024),
        cost_estimate=pl.CostEstimate(
            flops=15 * 1000**3, bytes_accessed=16 * 1000**2, transcendentals=3 * 1000**2
        ),
        name="feed",
    )(me, *got, *left, *right, x_all, g_all, vecs)


def turn_kernel(me_ref, *refs, n):
    got, refs = refs[:n], refs[n:]
    keep_ref, far_ref, x_two_ref, g_ref, out_w_ref, vec_ref = refs[:6]
    gos, (gx_ref, d_out_ref, sum_ref) = refs[6 : 6 + n], refs[6 + n :]
    me = me_ref[0]
    width = got[0].shape[1]
    gh = keep_ref[...].astype(F32) + far_ref[...].astype(F32)
    normed, inv_std = normed_parts(x_two_ref[...])
    g = g_ref[...].astype(F32)
    gx = g + normalize_back(gh, normed, inv_std, vec_ref[2:3, :])
    gx_ref[...] = gx
    gb = gx.astype(BF16)
    for p in range(n):
        own = pl.ds(pl.multiple_of((me ^ p) * width, width), width)
        gos[p][...] = dot_nt(out_w_ref[own, :], gb).astype(BF16)
        d_out_ref[own, :] = dot_nn(got[p][0], gb).astype(BF16)
    sum_ref[0:1, :] = jnp.sum(gh * normed, 0, keepdims=True)
    sum_ref[1:2, :] = jnp.sum(gh, 0, keepdims=True)
    sum_ref[2:3, :] = jnp.sum(gb.astype(F32), 0, keepdims=True)
    sum_ref[3:4, :] = jnp.sum(g, 0, keepdims=True)


def turn(me, got, keep, far, x_two, g, out_w, vecs):
    n = len(got)
    _, width, block = got[0].shape
    dm = out_w.shape[1]

    def whole(shape):
        return pl.BlockSpec(shape, lambda i, me: (0,) * len(shape))

    def piece(p):
        return pl.BlockSpec((1, width, block), lambda i, me: (p, 0, 0))

    outs = [jax.ShapeDtypeStruct((width, block), BF16)] * n + [
        jax.ShapeDtypeStruct((block, dm), F32),
        jax.ShapeDtypeStruct(out_w.shape, BF16),
        jax.ShapeDtypeStruct((8, dm), F32),
    ]
    return pl.pallas_call(
        functools.partial(turn_kernel, n=n),
        grid_spec=pltpu.PrefetchScalarGridSpec(
            num_scalar_prefetch=1,
            grid=(1,),
            in_specs=[piece(p) for p in range(n)]
            + [whole(a.shape) for a in (keep, far, x_two, g, out_w, vecs)],
            out_specs=[whole(o.shape) for o in outs],
        ),
        out_shape=outs,
        compiler_params=pltpu.CompilerParams(vmem_limit_bytes=48 * 1024 * 1024),
        cost_estimate=pl.CostEstimate(flops=3 * 1000**3, bytes_accessed=8 * 1000**2, transcendentals=0),
        name="turn",
    )(me, *got, keep, far, x_two, g, out_w, vecs)


def leave_kernel(
    me_ref, x_ref, grad_ref, w_ref, vec_ref, two_ref, up_ref, even_ref, odd_ref, d_w_ref, sum_ref, add_ref, total_ref, tile_ref
):
    i = pl.program_id(0)

    @pl.when(i == 0)
    def _():
        sum_ref[...] = jnp.zeros_like(sum_ref)
        add_ref[...] = jnp.zeros_like(add_ref)
        total_ref[...] = jnp.zeros_like(total_ref)

    grads = grad_ref[0]
    gh = dot_nt(grads, w_ref[...])
    normed, _ = normed_parts(x_ref[0].astype(F32))
    h = (normed * vec_ref[0:1, :] + vec_ref[1:2, :]).astype(BF16)
    low = gh.astype(BF16)

    @pl.when(i % 2 == 0)
    def _():
        even_ref[0] = low

    @pl.when(i % 2 == 1)
    def _():
        odd_ref[0] = low

    sum_ref[0:1, :] += jnp.sum(gh * normed, 0, keepdims=True)
    sum_ref[1:2, :] += jnp.sum(gh, 0, keepdims=True)
    add_ref[0:1, :] += jnp.sum(grads.astype(F32), 0, keepdims=True)
    total_ref[...] += dot_tn(h, grads)

    @pl.when(i == pl.num_programs(0) - 1)
    def _():
        wide = total_ref.shape[1]
        width = wide // 3
        d_w_ref[:, :wide] = total_ref[...].astype(BF16)
        dm = w_ref.shape[0]
        rows = [sum_ref[0:2, :], two_ref[0:4, :], jnp.zeros((2, dm), F32), up_ref[0:1, :]]
        rows = jnp.concatenate(rows + [jnp.zeros((LANES - 9, dm), F32)], 0)
        tile_ref[...] = rows.T
        add = jnp.concatenate(
            [
                jnp.zeros((6, width), F32),
                add_ref[0:1, :width],
                add_ref[0:1, 2 * width :],
                jnp.zeros((LANES - 8, width), F32),
            ],
            0,
        )
        own = pl.ds(pl.multiple_of(me_ref[0] * width, width), width)
        tile_ref[own, :] += add.T
        d_w_ref[:, wide:] = tile_ref[...].astype(BF16)


def leave(me, x_all, grads, w, vecs, sums_two, sums_up):
    n, block, wide = grads.shape
    dm = w.shape[0]

    def whole(shape):
        return pl.BlockSpec(shape, lambda i, me: (0,) * len(shape))

    def one(width):
        return pl.BlockSpec((1, block, width), lambda i, me: (i, 0, 0))

    def half(width):
        return pl.BlockSpec((1, block, width), lambda i, me: (i // 2, 0, 0))

    pair = jax.ShapeDtypeStruct((n // 2, block, dm), BF16)
    return pl.pallas_call(
        leave_kernel,
        grid_spec=pltpu.PrefetchScalarGridSpec(
            num_scalar_prefetch=1,
            grid=(n,),
            in_specs=[one(dm), one(wide)] + [whole(a.shape) for a in (w, vecs, sums_two, sums_up)],
            out_specs=[half(dm), half(dm), whole((dm, wide + LANES))],
            scratch_shapes=[
                pltpu.VMEM((8, dm), F32),
                pltpu.VMEM((8, wide), F32),
                pltpu.VMEM(w.shape, F32),
                pltpu.VMEM((dm, LANES), F32),
            ],
        ),
        out_shape=[
            pair,
            pair,
            jax.ShapeDtypeStruct((dm, wide + LANES), BF16),
        ],
        compiler_params=pltpu.CompilerParams(vmem_limit_bytes=48 * 1024 * 1024),
        cost_estimate=pl.CostEstimate(flops=6 * 1000**3, bytes_accessed=10 * 1000**2, transcendentals=0),
        name="leave",
    )(me, x_all, grads, w, vecs, sums_two, sums_up)


def finish_kernel(me_ref, *refs, n, width):
    pieces, (q_ref, k_ref, v_ref, vec_ref) = refs[:n], refs[n:]
    vec_ref[...] = sum(p[:, 3 * width :] for p in pieces)
    parts = [p[:, : 3 * width] for p in pieces]
    bit = 1
    while bit < n:
        on = (me_ref[0] & bit) != 0
        for p in range(n):
            if not p & bit:
                a, b = parts[p], parts[p | bit]
                parts[p] = jnp.where(on, b, a)
                parts[p | bit] = jnp.where(on, a, b)
        bit *= 2
    for t in range(n):
        for i, ref in enumerate((q_ref, k_ref, v_ref)):
            ref[:, t * width : (t + 1) * width] = parts[t][:, i * width : (i + 1) * width]


def finish(me, pieces, width):
    n = len(pieces)
    rows = pieces[0].shape[0]
    weight = jax.ShapeDtypeStruct((rows, n * width), F32)
    return pl.pallas_call(
        functools.partial(finish_kernel, n=n, width=width),
        in_specs=[pl.BlockSpec(memory_space=pltpu.SMEM)] + [pl.BlockSpec(memory_space=pltpu.VMEM)] * n,
        out_specs=[pl.BlockSpec(memory_space=pltpu.VMEM)] * 4,
        out_shape=[weight] * 3 + [jax.ShapeDtypeStruct((rows, LANES), F32)],
        name="finish",
    )(me, *pieces)


def body(
    nd,
    ns,
    tokens,
    cotangent,
    segments,
    w_query,
    w_key,
    w_value,
    w_out,
    w_up,
    w_down,
    ln1_gain,
    ln1_shift,
    query_bias,
    value_bias,
    out_bias,
    ln2_gain,
    ln2_shift,
    up_bias,
    down_bias,
):
    d = lax.axis_index("dp")
    s = lax.axis_index("seq")
    me = s.astype(jnp.int32).reshape(1)
    _, block, dm = tokens.shape
    hd = dm // H
    heads = H // ns
    width = heads * hd
    rows = w_query.shape[0]
    ff_rows, ff = w_down.shape[0], w_up.shape[1]
    ratio = ff_rows // rows
    part = ff // ns
    pad = 16

    me = jnp.stack([s, d]).astype(jnp.int32)
    masks = bits_of(nd)[::-1]
    far = bits_of(ns)[-1]
    x_own = tokens.reshape(block, dm)
    g = cotangent.reshape(block, dm)
    x_far = swap(x_own, "seq", ns, far)

    cols = [w.reshape(rows, ns, width) for w in (w_query, w_key, w_value)]
    vec = jnp.stack([ln1_gain, ln1_shift, ln2_gain, ln2_shift, out_bias, down_bias, query_bias, value_bias], 1)
    vec = jnp.pad(vec, ((0, 0), (0, LANES - vec.shape[1])))
    up_cols = w_up.reshape(rows, nd, ns, ff_rows).transpose(0, 2, 1, 3).reshape(rows, ns, part)
    lanes = LANES * -(-block // (rows * LANES))
    seg = jnp.pad(segments.reshape(block).astype(BF16), (0, rows * lanes - block)).reshape(rows, lanes)
    same = jnp.concatenate([vec, w_out, seg], 1)
    same = jnp.broadcast_to(same[:, None], (rows, ns, same.shape[1]))
    pieces = jnp.concatenate(cols + [same, up_cols], 2).transpose(1, 0, 2)
    first = 3 * width + LANES
    size = ns * rows
    pieces = trade_seq(pieces, s, ns)
    start = first + dm
    segs = jnp.stack([p[:, start : start + lanes].reshape(-1)[:block] for p in pieces]).astype(jnp.int32)
    seg_row = segs.reshape(ns, 1, block)
    seg_col = segs.reshape(ns, block, 1)
    pieces = ordered(pieces, s).reshape(size, -1)
    lane = lax.broadcasted_iota(jnp.int32, (size, first), 1)
    one = jnp.where(lane == 3 * width + 8, jnp.pad(up_bias, (0, size - ff_rows))[:, None], pieces[:, :first])
    two = jnp.concatenate([pieces[:, first:start], pieces[:, start + lanes :], w_down], 0)
    left, right = two[:, : dm // 2], two[:, dm // 2 :]

    ones, lefts = [one[None]], [left[None]]
    g_far = None
    for step, mask in enumerate(masks):
        got = swap(jnp.concatenate(ones, 0), "dp", nd, mask)
        if step == 1:
            got, x_far = lax.optimization_barrier((got, x_far))
            g_far = swap(tie(g, x_far), "seq", ns, far)
        if step > 0:
            lefts.append(swap(tie(jnp.concatenate(lefts, 0), got), "dp", nd, masks[step - 1]))
        ones.append(got)
    lefts.append(swap(tie(jnp.concatenate(lefts, 0), ones[-1]), "dp", nd, masks[-1]))
    rights = [right[None]]
    turned = masks[:-2] + masks[:-3:-1]
    for step, mask in enumerate(turned):
        rights.append(swap(tie(jnp.concatenate(rights, 0), lefts[min(step + 1, len(masks) - 1)]), "dp", nd, mask))
    parts = {0: x_own, far: x_far}
    g_parts = {0: g, far: g_far}
    for mask in bits_of(ns)[-2::-1]:
        for p in list(parts):
            parts[p | mask] = swap(parts[p], "seq", ns, mask)
            g_parts[p | mask] = swap(g_parts[p], "seq", ns, mask)
    x_all = jnp.stack([parts[p] for p in range(ns)])
    g_all = jnp.stack([g_parts[p] for p in range(ns)])

    ones, ids = settle(ones, d, nd, masks, 1)
    ones[-1], x_all, g_all = lax.optimization_barrier((ones[-1], x_all, g_all))
    qkv, w_qkv, vecs = enter(me, ones, ids, x_all, width)
    qkv, *rights[1:-1] = lax.optimization_barrier((qkv, *rights[1:-1]))
    o_low, o_full, lse = attend(me, qkv, seg_row, seg_col, heads, hd)
    o_got = spread_seq(o_low, ns)
    lefts, left_ids = settle(lefts, d, nd, masks, 3)
    rights, right_ids = settle(rights, d, nd, turned, 3)
    ids = (left_ids, right_ids)
    h_two, act, gu, even, odd, x_two, sums_up, w_out_all, w_down_own = feed(
        me, o_got, lefts, rights, ids, x_all, g_all, vecs
    )
    keep, sent, got = collect_pairs(even, odd, ns)
    act, gu, h_two = lax.optimization_barrier((act, gu, h_two, sent))[:3]
    d_down = jnp.einsum("nbk,nbc->kc", act, g_all, preferred_element_type=F32).astype(BF16)
    d_up = jnp.einsum("nbk,nbc->kc", h_two, gu, preferred_element_type=F32).astype(BF16)
    feeds = jnp.concatenate([d_up.reshape(nd, size, part), d_down.reshape(nd, ff_rows, dm)], 1)
    feed_keep, feed_sent = halves(feeds, d, nd, 1)
    feed_got = swap(feed_sent, "dp", nd, 1)
    got, feed_sent = lax.optimization_barrier((got, feed_sent))
    out_part = jnp.einsum("nbk,kc->nbc", act, w_down_own, preferred_element_type=F32).astype(BF16)
    *gos, gx_two, d_out, sums_two = turn(me, o_got, keep, got, x_two, g, w_out_all, vecs)
    go_got = [gos[0]] + [swap(gos[p], "seq", ns, p) for p in range(1, ns)]
    outs_keep, outs_sent = halves(d_out.reshape(nd, size, dm), d, nd, 1)
    outs_got = swap(outs_sent, "dp", nd, 1)
    out_keep, _, out_got = collect_pairs(out_part[::2], out_part[1::2], ns, (go_got[-1],))

    go_all = jnp.stack(go_got)
    go_all, feed_got = lax.optimization_barrier((go_all, feed_got))
    feeds = add_low(feed_keep, feed_got)
    feed_keep, feed_sent = halves(feeds, d >> 1, nd // 2, 1)
    feed_got = swap(feed_sent, "dp", nd, 2)
    grads = attend_back(me, qkv, go_all, o_full, lse, seg_row, seg_col, heads, hd)
    grads, out_got, outs_got, feed_got = lax.optimization_barrier((grads, out_got, outs_got, feed_got))
    feeds = add_low(feed_keep, feed_got)
    outs = add_low(outs_keep, outs_got)
    out = out_keep.astype(F32) + out_got.astype(F32) + x_two + vecs[5:6]
    even, odd, blob = leave(me, x_all, grads, w_qkv, vecs, sums_two, sums_up)
    keep, sent, got = collect_pairs(even, odd, ns)
    blob_keep, blob_sent = halves(blob.reshape(nd, size, first), d, nd, 1)
    blob_got = swap(tie(blob_sent, sent), "dp", nd, 1)
    blob = add_low(blob_keep, blob_got)
    blob_keep, blob_sent = halves(blob, d >> 1, nd // 2, 1)
    blob_got = swap(blob_sent, "dp", nd, 2)
    blob_got, got, feeds, outs = lax.optimization_barrier((blob_got, got, feeds, outs))
    blob = add_low(blob_keep, blob_got)
    blob = collect_dp(blob, d >> 2, nd // 4, shift=2)
    trades = trade_seq(blob.reshape(ns, rows, first), s, ns)
    sum_up_bias = blob[:ff_rows, 3 * width + 8]
    gh_one = keep.astype(F32) + got.astype(F32)
    n_own, inv_own = normed_parts(x_own.astype(F32))
    grad_x = gx_two + normalize_back(gh_one, n_own, inv_own, vecs[0:1])
    sum_q, sum_k, sum_v, vec_sum = finish(me, trades, width)
    vec_sum = vec_sum.T
    outs = collect_dp(outs, d >> 1, nd // 2, shift=1)
    feeds = collect_dp(feeds, d >> 2, nd // 4, shift=2)
    sum_down = feeds[size:]
    both = jnp.concatenate([outs, feeds[:size]], 1).reshape(ns, rows, dm + part)
    both = trade_seq(both, s, ns)
    sum_out = sum(b[:, :dm] for b in both)
    sum_up = ordered([b[:, dm:] for b in both], s)
    sum_up = sum_up.reshape(ns, rows, nd, ff_rows).transpose(1, 2, 0, 3).reshape(rows, ff)
    v = [vec_sum[i] for i in range(8)]
    return (
        out.reshape(1, block, dm),
        grad_x.reshape(1, block, dm),
        sum_q,
        sum_k,
        sum_v,
        sum_out,
        sum_up,
        sum_down,
        v[0],
        v[1],
        v[6],
        v[7],
        v[4],
        v[2],
        v[3],
        sum_up_bias,
        v[5],
    )


def solution(mesh):
    act = P("dp", "seq", None)
    weight = P(("dp", "seq"), None)
    vector = P(("dp", "seq"))
    return jax.shard_map(
        functools.partial(body, mesh.shape["dp"], mesh.shape["seq"]),
        mesh=mesh,
        in_specs=(act, act, P("dp", "seq")) + (weight,) * 6 + (vector,) * 9,
        out_specs=(act, act) + (weight,) * 6 + (vector,) * 9,
        check_vma=False,
    )
```

```python
import functools
import math

import jax
import jax.numpy as jnp
from jax import lax
from jax.experimental import pallas as pl
from jax.experimental.pallas import tpu as pltpu
from jax.sharding import PartitionSpec as P

H = 12
EPSILON = 1e-05
MASKED = -1e30
F32 = jnp.float32
BF16 = jnp.bfloat16
LANES = 128


def dot_nt(a, b):
    return lax.dot_general(a, b, (((1,), (1,)), ((), ())), preferred_element_type=F32)


def dot_tn(a, b):
    return lax.dot_general(a, b, (((0,), (0,)), ((), ())), preferred_element_type=F32)


def dot_nn(a, b):
    return jnp.dot(a, b, preferred_element_type=F32)


def attend_kernel(me_ref, qkv_ref, seg_row_ref, seg_col_ref, low_ref, full_ref, lse_ref, *, heads, hd):
    me = me_ref[0]
    qi = pl.program_id(0)
    rq = qi ^ me
    block = qkv_ref.shape[1]
    width = heads * hd
    scale = jnp.asarray(1.0 / math.sqrt(hd), BF16)
    queries = [qkv_ref[rq, :, h * hd : (h + 1) * hd] * scale for h in range(heads)]
    seg_q = seg_row_ref[rq]

    def step(rk, state, causal):
        allowed = seg_col_ref[rk] == seg_q
        if causal:
            k_pos = lax.broadcasted_iota(jnp.int32, (block, block), 0)
            q_pos = lax.broadcasted_iota(jnp.int32, (block, block), 1)
            allowed = allowed & (k_pos <= q_pos)
        new = []
        for h in range(heads):
            top, total, mixed = state[h]
            key = qkv_ref[rk, :, width + h * hd : width + (h + 1) * hd]
            value = qkv_ref[rk, :, 2 * width + h * hd : 2 * width + (h + 1) * hd]
            scores = jnp.where(allowed, dot_nt(key, queries[h]), MASKED)
            higher = jnp.maximum(top, jnp.max(scores, 0, keepdims=True))
            weights = jnp.exp(scores - higher)
            fade = jnp.exp(top - higher)
            total = total * fade + jnp.sum(weights, 0, keepdims=True)
            mixed = mixed * fade + dot_tn(value, weights.astype(BF16))
            new.append((higher, total, mixed))
        return tuple(new)

    start = tuple(
        (jnp.full((1, block), MASKED, F32), jnp.zeros((1, block), F32), jnp.zeros((hd, block), F32))
        for _ in range(heads)
    )
    state = lax.fori_loop(0, qi, lambda kj, c: step(kj ^ me, c, False), start)
    state = step(rq, state, True)
    rows = []
    for h in range(heads):
        top, total, mixed = state[h]
        rows.append(mixed / total)
        lse_ref[0, h : h + 1, :] = top + jnp.log(total)
    full = jnp.concatenate(rows, 0)
    full_ref[0] = full
    low_ref[0] = full.astype(BF16)


def attend(me, qkv, seg_row, seg_col, heads, hd):
    n, block, _ = qkv.shape
    width = heads * hd

    def whole(shape):
        return pl.BlockSpec(shape, lambda i, me: (0,) * len(shape))

    def own(shape):
        return pl.BlockSpec(shape, lambda i, me: (i ^ me[0], 0, 0))

    return pl.pallas_call(
        functools.partial(attend_kernel, heads=heads, hd=hd),
        grid_spec=pltpu.PrefetchScalarGridSpec(
            num_scalar_prefetch=1,
            grid=(n,),
            in_specs=[whole(qkv.shape), whole(seg_row.shape), whole(seg_col.shape)],
            out_specs=[own((1, width, block)), own((1, width, block)), own((1, 8, block))],
        ),
        out_shape=[
            jax.ShapeDtypeStruct((n, width, block), BF16),
            jax.ShapeDtypeStruct((n, width, block), F32),
            jax.ShapeDtypeStruct((n, 8, block), F32),
        ],
        compiler_params=pltpu.CompilerParams(vmem_limit_bytes=40 * 1024 * 1024),
        cost_estimate=pl.CostEstimate(
            flops=20 * 1000**3, bytes_accessed=8 * 1000**2, transcendentals=8 * 1000**2
        ),
        name="attend",
    )(me, qkv, seg_row, seg_col)


def attend_back_kernel(
    me_ref, qkv_ref, go_ref, full_ref, lse_ref, seg_row_ref, seg_col_ref, grad_ref, gq_ref, dot_ref, *, heads, hd
):
    me = me_ref[0]
    kj = pl.program_id(0)
    rk = kj ^ me
    n, block, _ = qkv_ref.shape
    width = heads * hd
    scale = 1.0 / math.sqrt(hd)
    low_scale = jnp.asarray(scale, BF16)

    @pl.when(kj == 0)
    def _():
        gq_ref[...] = jnp.zeros_like(gq_ref)
        for b in range(n):
            prod = go_ref[b].astype(F32) * full_ref[b]
            for h in range(heads):
                dot_ref[b, h : h + 1, :] = jnp.sum(prod[h * hd : (h + 1) * hd], 0, keepdims=True)

    keys = [qkv_ref[rk, :, width + h * hd : width + (h + 1) * hd] for h in range(heads)]
    values = [qkv_ref[rk, :, 2 * width + h * hd : 2 * width + (h + 1) * hd] for h in range(heads)]
    seg_k = seg_col_ref[rk]

    def step(rq, state, causal):
        allowed = seg_k == seg_row_ref[rq]
        if causal:
            k_pos = lax.broadcasted_iota(jnp.int32, (block, block), 0)
            q_pos = lax.broadcasted_iota(jnp.int32, (block, block), 1)
            allowed = allowed & (k_pos <= q_pos)
        new = []
        for h in range(heads):
            gk, gv = state[h]
            query = qkv_ref[rq, :, h * hd : (h + 1) * hd] * low_scale
            go = go_ref[rq, h * hd : (h + 1) * hd, :]
            scores = jnp.where(allowed, dot_nt(keys[h], query), MASKED)
            weights = jnp.exp(scores - lse_ref[rq, h : h + 1, :])
            gw = dot_nn(values[h], go)
            ds = (weights * (gw - dot_ref[rq, h : h + 1, :])).astype(BF16)
            gv = gv + dot_nt(weights.astype(BF16), go)
            gk = gk + dot_nn(ds, query)
            gq_ref[rq, h * hd : (h + 1) * hd, :] += dot_tn(keys[h], ds)
            new.append((gk, gv))
        return tuple(new)

    zero = jnp.zeros((block, hd), F32)
    state = step(rk, tuple((zero, zero) for _ in range(heads)), True)
    state = lax.fori_loop(kj + 1, n, lambda qi, c: step(qi ^ me, c, False), state)
    grad_ref[0, :, :width] = (gq_ref[rk] * scale).T.astype(BF16)
    for h in range(heads):
        gk, gv = state[h]
        grad_ref[0, :, width + h * hd : width + (h + 1) * hd] = gk.astype(BF16)
        grad_ref[0, :, 2 * width + h * hd : 2 * width + (h + 1) * hd] = gv.astype(BF16)


def attend_back(me, qkv, go, full, lse, seg_row, seg_col, heads, hd):
    n, block, wide = qkv.shape
    width = heads * hd

    def whole(shape):
        return pl.BlockSpec(shape, lambda i, me: (0,) * len(shape))

    return pl.pallas_call(
        functools.partial(attend_back_kernel, heads=heads, hd=hd),
        grid_spec=pltpu.PrefetchScalarGridSpec(
            num_scalar_prefetch=1,
            grid=(n,),
            in_specs=[whole(a.shape) for a in (qkv, go, full, lse, seg_row, seg_col)],
            out_specs=pl.BlockSpec((1, block, wide), lambda i, me: (i ^ me[0], 0, 0)),
            scratch_shapes=[pltpu.VMEM((n, width, block), F32), pltpu.VMEM((n, 8, block), F32)],
        ),
        out_shape=jax.ShapeDtypeStruct((n, block, wide), BF16),
        compiler_params=pltpu.CompilerParams(vmem_limit_bytes=40 * 1024 * 1024),
        cost_estimate=pl.CostEstimate(
            flops=40 * 1000**3, bytes_accessed=12 * 1000**2, transcendentals=8 * 1000**2
        ),
        name="attend_back",
    )(me, qkv, go, full, lse, seg_row, seg_col)


def normed_parts(value):
    mean = jnp.mean(value, -1, keepdims=True)
    centred = value - mean
    inv_std = lax.rsqrt(jnp.mean(centred * centred, -1, keepdims=True) + EPSILON)
    return centred * inv_std, inv_std


def normalize_back(grad_in, normed, inv_std, gain):
    scaled = grad_in * gain
    return inv_std * (
        scaled
        - jnp.mean(scaled, -1, keepdims=True)
        - normed * jnp.mean(scaled * normed, -1, keepdims=True)
    )


def gelu_and_slope(value):
    cumul = 0.5 * (1.0 + lax.erf(value * (1.0 / math.sqrt(2.0))))
    slope = cumul + value * jnp.exp(-0.5 * value * value) * (1.0 / math.sqrt(2.0 * math.pi))
    return value * cumul, slope


def tie(value, *others):
    return lax.optimization_barrier((value,) + others)[0] if others else value


def swap(value, axis, size, mask):
    return lax.ppermute(value, axis, [(i, i ^ mask) for i in range(size)])


def bits_of(size):
    count = size.bit_length() - 1
    return [1 << b for b in range(count)]


def ordered(parts, index):
    parts = [part[None] for part in parts]
    bit = 1
    while len(parts) > 1:
        on = (index & bit) != 0
        parts = [
            jnp.where(on, jnp.concatenate([b, a], 0), jnp.concatenate([a, b], 0))
            for a, b in zip(parts[::2], parts[1::2])
        ]
        bit *= 2
    return parts[0]


def gathered_ids(masks):
    held, lists = [0], [[0]]
    for mask in masks:
        new = [r ^ mask for r in held]
        lists.append(new)
        held = held + new
    return lists


def settle(parts, index, size, masks, count):
    ids = gathered_ids(masks)
    rows = parts[0].shape[1] // count
    if rows % 16 == 0:
        return parts, ids
    held = sum(ids, [])
    at = jnp.asarray([held.index(r) for r in range(size)])
    whole = jnp.concatenate(parts, 0)[at[jnp.arange(size) ^ index]]
    whole = whole.reshape(size, count, rows, -1).transpose(1, 0, 2, 3)
    return [whole.reshape(1, size * count * rows, -1)], [[None]]


def place(refs, ids, index, count, put):
    for ref, held in zip(refs, ids):
        rows = ref.shape[1] // count
        for j, r in enumerate(held):
            where = slice(None) if r is None else pl.ds(pl.multiple_of((index ^ r) * rows, rows), rows)
            for k in range(count):
                put(k, where, ref[j, k * rows : (k + 1) * rows, :])


def halves(value, index, size, mask):
    value = value.reshape((-1, 2, mask) + value.shape[1:])
    on = ((index & mask) != 0).astype(jnp.int32)
    shape = (-1,) + value.shape[3:]
    keep = lax.dynamic_index_in_dim(value, on, 1, False).reshape(shape)
    return keep, lax.dynamic_index_in_dim(value, 1 - on, 1, False).reshape(shape)


def add_low(a, b, kind=BF16):
    return (a.astype(F32) + b.astype(F32)).astype(kind)


def collect_dp(value, index, size, last=F32, shift=0):
    masks = bits_of(size)
    shape = value.shape[1:]
    value = value.reshape((2,) * len(masks) + shape)
    for step, mask in enumerate(masks):
        axis = len(masks) - 1 - step
        on = ((index & mask) != 0).astype(jnp.int32)
        keep = lax.dynamic_index_in_dim(value, on, axis, False)
        send = lax.dynamic_index_in_dim(value, 1 - on, axis, False)
        got = swap(send, "dp", size << shift, mask << shift)
        value = keep.astype(F32) + got.astype(F32)
        value = value.astype(BF16 if step < len(masks) - 1 else last)
    return value


def collect_pairs(even, odd, size, tied=()):
    got = swap(odd, "seq", size, 1)
    sums = [(even[i].astype(F32) + got[i].astype(F32)).astype(BF16) for i in range(size // 2)]
    mask = 2
    while len(sums) > 2:
        sent = [swap(b, "seq", size, mask) for b in sums[1::2]]
        sums = [(a.astype(F32) + b.astype(F32)).astype(BF16) for a, b in zip(sums[::2], sent)]
        mask *= 2
    return sums[0], sums[1], swap(tie(sums[1], *tied), "seq", size, mask)


def spread_seq(value, size, gate=()):
    got = {0: value}
    for mask in bits_of(size)[::-1]:
        for p in list(got):
            got[p | mask] = swap(tie(got[p], *gate) if p else got[p], "seq", size, mask)
    return [got[p] for p in range(size)]


def trade_seq(pieces, index, size):
    return [
        swap(lax.dynamic_index_in_dim(pieces, index ^ p, 0, False), "seq", size, p)
        if p
        else lax.dynamic_index_in_dim(pieces, index, 0, False)
        for p in range(size)
    ]


def enter_kernel(me_ref, *refs, ids, n, width):
    count = len(ids)
    pieces, (x_ref, qkv_ref, w_ref, vec_ref, tile_ref, add_ref) = refs[:count], refs[count:]
    me = me_ref[0]

    @pl.when(pl.program_id(0) == 0)
    def _():
        def put(k, where, rows):
            w_ref[where, :] = rows[:, : 3 * width]
            tile_ref[where, :] = rows[:, 3 * width :].astype(F32)

        place(pieces, ids, me_ref[1], 1, put)
        vecs = tile_ref[...].T[:16]
        vec_ref[...] = vecs
        for i, row in ((0, 6), (2, 7)):
            add = vecs[row : row + 1, :width]
            for t in range(1, n):
                add = jnp.where(me == t, vecs[row : row + 1, t * width : (t + 1) * width], add)
            add_ref[0:1, i * width : (i + 1) * width] = add
        add_ref[0:1, width : 2 * width] = jnp.zeros((1, width), F32)

    normed, _ = normed_parts(x_ref[0].astype(F32))
    h = (normed * vec_ref[0:1, :] + vec_ref[1:2, :]).astype(BF16)
    qkv_ref[0] = (dot_nn(h, w_ref[...]) + add_ref[0:1, :]).astype(BF16)


def enter(me, pieces, ids, x_all, width):
    n, block, dm = x_all.shape

    def whole(shape):
        return pl.BlockSpec(shape, lambda i, me: (0,) * len(shape))

    def one(width):
        return pl.BlockSpec((1, block, width), lambda i, me: (i, 0, 0))

    return pl.pallas_call(
        functools.partial(enter_kernel, ids=ids, n=n, width=width),
        grid_spec=pltpu.PrefetchScalarGridSpec(
            num_scalar_prefetch=1,
            grid=(n,),
            in_specs=[whole(a.shape) for a in pieces] + [one(dm)],
            out_specs=[one(3 * width), whole((dm, 3 * width)), whole((16, dm))],
            scratch_shapes=[pltpu.VMEM((dm, LANES), F32), pltpu.VMEM((8, 3 * width), F32)],
        ),
        out_shape=[
            jax.ShapeDtypeStruct((n, block, 3 * width), BF16),
            jax.ShapeDtypeStruct((dm, 3 * width), BF16),
            jax.ShapeDtypeStruct((16, dm), F32),
        ],
        compiler_params=pltpu.CompilerParams(vmem_limit_bytes=40 * 1024 * 1024),
        cost_estimate=pl.CostEstimate(flops=5 * 1000**3, bytes_accessed=8 * 1000**2, transcendentals=0),
        name="enter",
    )(me, *pieces, x_all)


def feed_kernel(me_ref, *refs, n, base, tile, ids):
    got, refs = refs[:n], refs[n:]
    me = me_ref[0]
    i = pl.program_id(0)
    if base:
        count = len(ids[0])
        left, right, refs = refs[:count], refs[count : 2 * count], refs[2 * count :]
        x_ref, g_ref, vec_ref = refs[:3]
        h_ref, act_ref, gu_ref, low_ref, high_ref, sum_ref, out_w_ref, up_ref, down_ref = refs[3:]
    else:
        x_ref, g_ref, vec_ref, out_w_ref, up_ref, down_ref, sum_in_ref = refs[:7]
        h_ref, act_ref, gu_ref, low_ref, high_ref, sum_ref, x_two_ref = refs[10:]
    part = up_ref.shape[1]
    width = got[0].shape[1]

    @pl.when(i == 0)
    def _():
        if base:
            sum_ref[...] = jnp.zeros_like(sum_ref)
            for first, pieces, held in ((0, left, ids[0]), (part // 2, right, ids[1])):

                def put(k, where, rows, first=first):
                    (out_w_ref, up_ref, down_ref)[k][where, first : first + part // 2] = rows

                place(pieces, held, me_ref[1], 3, put)
        else:
            sum_ref[...] = sum_in_ref[...]

    x_two = x_ref[0].astype(F32) + vec_ref[4:5, :]
    for p in range(n):
        own = pl.ds(pl.multiple_of((me ^ p) * width, width), width)
        x_two = x_two + dot_tn(got[p][0], out_w_ref[own, :])
    if not base:

        @pl.when(i == 0)
        def _():
            x_two_ref[...] = x_two

    normed, _ = normed_parts(x_two)
    h = (normed * vec_ref[2:3, :] + vec_ref[3:4, :]).astype(BF16)
    h_ref[0] = h
    g = g_ref[0]
    total = None
    for t in range(0, part, tile):
        cols = slice(t, t + tile)
        u = dot_nn(h, up_ref[:, cols]) + vec_ref[8:9, cols]
        act, slope = gelu_and_slope(u)
        act_ref[0, :, cols] = act.astype(BF16)
        gu = (dot_nt(g, down_ref[cols, :]) * slope).astype(BF16)
        gu_ref[0, :, cols] = gu
        sum_ref[0:1, cols] += jnp.sum(gu.astype(F32), 0, keepdims=True)
        term = dot_nt(gu, up_ref[:, cols])
        total = term if total is None else total + term
    total = total.astype(BF16)

    @pl.when(i == 0)
    def _():
        low_ref[...] = total

    @pl.when(i == 1)
    def _():
        high_ref[...] = total


def feed(me, got, x_all, g_all, vecs, base, weights, ids=None, held=()):
    n, block, dm = x_all.shape
    part = dm if base else weights[1].shape[1]
    width = got[0].shape[1]

    def whole(shape):
        return pl.BlockSpec(shape, lambda i, me: (0,) * len(shape))

    def one(width):
        return pl.BlockSpec((1, block, width), lambda i, me: (i + base, 0, 0))

    def piece(p):
        return pl.BlockSpec((1, width, block), lambda i, me: ((i + base) ^ p, 0, 0))

    if base:
        part = 2 * weights[0][0].shape[2]
        weights = [*weights[0], *weights[1]]
    wide = jax.ShapeDtypeStruct((n, block, dm), BF16)
    hidden = jax.ShapeDtypeStruct((n, block, part), BF16)
    low = jax.ShapeDtypeStruct((block, dm), BF16)
    outs = [wide, hidden, hidden, low, low, jax.ShapeDtypeStruct((8, part), F32)]
    specs = [one(dm), one(part), one(part)] + [whole(o.shape) for o in outs[3:]]
    more = [(dm, dm), (dm, part), (part, dm)] if base else []
    outs += [jax.ShapeDtypeStruct(m, BF16) for m in more] or [jax.ShapeDtypeStruct((block, dm), F32)]
    specs += [whole(o.shape) for o in outs[6:]]
    args = [*got]
    ins = [piece(p) for p in range(n)]
    if base:
        args += [*weights, x_all, g_all, vecs]
        ins += [whole(a.shape) for a in weights] + [one(dm), one(dm), whole(vecs.shape)]
        alias = {}
    else:
        args += [x_all, g_all, vecs, *weights, *held]
        ins += [one(dm), one(dm)] + [whole(a.shape) for a in (vecs, *weights, held[0])]
        ins += [pl.BlockSpec(memory_space=pl.ANY)] * 3
        alias = {len(args) - 3 + k + 1: k for k in range(3)}
    return pl.pallas_call(
        functools.partial(feed_kernel, n=n, base=base, tile=256 if part % 256 == 0 else part, ids=ids),
        grid_spec=pltpu.PrefetchScalarGridSpec(num_scalar_prefetch=1, grid=(2,), in_specs=ins, out_specs=specs),
        out_shape=outs,
        input_output_aliases=alias,
        compiler_params=pltpu.CompilerParams(vmem_limit_bytes=48 * 1024 * 1024),
        cost_estimate=pl.CostEstimate(
            flops=9 * 1000**3, bytes_accessed=16 * 1000**2, transcendentals=3 * 1000**2
        ),
        name="feed_far" if base else "feed_near",
    )(me, *args)


def turn_kernel(me_ref, *refs, n):
    got, refs = refs[:n], refs[n:]
    keep_ref, near_ref, far_ref, x_two_ref, g_ref, out_w_ref, vec_ref = refs[:7]
    gos, (gx_ref, d_out_ref, sum_ref) = refs[7 : 7 + n], refs[7 + n :]
    me = me_ref[0]
    width = got[0].shape[1]
    gh = keep_ref[...].astype(F32) + near_ref[...].astype(F32) + far_ref[...].astype(F32)
    normed, inv_std = normed_parts(x_two_ref[...])
    g = g_ref[...].astype(F32)
    gx = g + normalize_back(gh, normed, inv_std, vec_ref[2:3, :])
    gx_ref[...] = gx
    gb = gx.astype(BF16)
    for p in range(n):
        own = pl.ds(pl.multiple_of((me ^ p) * width, width), width)
        gos[p][...] = dot_nt(out_w_ref[own, :], gb).astype(BF16)
        d_out_ref[own, :] = dot_nn(got[p][0], gb).astype(BF16)
    sum_ref[0:1, :] = jnp.sum(gh * normed, 0, keepdims=True)
    sum_ref[1:2, :] = jnp.sum(gh, 0, keepdims=True)
    sum_ref[2:3, :] = jnp.sum(gb.astype(F32), 0, keepdims=True)
    sum_ref[3:4, :] = jnp.sum(g, 0, keepdims=True)


def turn(me, got, keep, near, far, x_two, g, out_w, vecs):
    n = len(got)
    _, width, block = got[0].shape
    dm = out_w.shape[1]

    def whole(shape):
        return pl.BlockSpec(shape, lambda i, me: (0,) * len(shape))

    def piece(p):
        return pl.BlockSpec((1, width, block), lambda i, me: (p, 0, 0))

    outs = [jax.ShapeDtypeStruct((width, block), BF16)] * n + [
        jax.ShapeDtypeStruct((block, dm), F32),
        jax.ShapeDtypeStruct(out_w.shape, BF16),
        jax.ShapeDtypeStruct((8, dm), F32),
    ]
    return pl.pallas_call(
        functools.partial(turn_kernel, n=n),
        grid_spec=pltpu.PrefetchScalarGridSpec(
            num_scalar_prefetch=1,
            grid=(1,),
            in_specs=[piece(p) for p in range(n)]
            + [whole(a.shape) for a in (keep, near, far, x_two, g, out_w, vecs)],
            out_specs=[whole(o.shape) for o in outs],
        ),
        out_shape=outs,
        compiler_params=pltpu.CompilerParams(vmem_limit_bytes=48 * 1024 * 1024),
        cost_estimate=pl.CostEstimate(flops=3 * 1000**3, bytes_accessed=8 * 1000**2, transcendentals=0),
        name="turn",
    )(me, *got, keep, near, far, x_two, g, out_w, vecs)


def leave_kernel(
    me_ref, x_ref, grad_ref, w_ref, vec_ref, two_ref, up_ref, even_ref, odd_ref, d_w_ref, sum_ref, add_ref, total_ref, tile_ref
):
    i = pl.program_id(0)

    @pl.when(i == 0)
    def _():
        sum_ref[...] = jnp.zeros_like(sum_ref)
        add_ref[...] = jnp.zeros_like(add_ref)
        total_ref[...] = jnp.zeros_like(total_ref)

    grads = grad_ref[0]
    gh = dot_nt(grads, w_ref[...])
    normed, _ = normed_parts(x_ref[0].astype(F32))
    h = (normed * vec_ref[0:1, :] + vec_ref[1:2, :]).astype(BF16)
    low = gh.astype(BF16)

    @pl.when(i % 2 == 0)
    def _():
        even_ref[0] = low

    @pl.when(i % 2 == 1)
    def _():
        odd_ref[0] = low

    sum_ref[0:1, :] += jnp.sum(gh * normed, 0, keepdims=True)
    sum_ref[1:2, :] += jnp.sum(gh, 0, keepdims=True)
    add_ref[0:1, :] += jnp.sum(grads.astype(F32), 0, keepdims=True)
    total_ref[...] += dot_tn(h, grads)

    @pl.when(i == pl.num_programs(0) - 1)
    def _():
        wide = total_ref.shape[1]
        width = wide // 3
        d_w_ref[:, :wide] = total_ref[...].astype(BF16)
        dm = w_ref.shape[0]
        rows = [sum_ref[0:2, :], two_ref[0:4, :], jnp.zeros((2, dm), F32), up_ref[0:1, :]]
        rows = jnp.concatenate(rows + [jnp.zeros((LANES - 9, dm), F32)], 0)
        tile_ref[...] = rows.T
        add = jnp.concatenate(
            [
                jnp.zeros((6, width), F32),
                add_ref[0:1, :width],
                add_ref[0:1, 2 * width :],
                jnp.zeros((LANES - 8, width), F32),
            ],
            0,
        )
        own = pl.ds(pl.multiple_of(me_ref[0] * width, width), width)
        tile_ref[own, :] += add.T
        d_w_ref[:, wide:] = tile_ref[...].astype(BF16)


def leave(me, x_all, grads, w, vecs, sums_two, sums_up):
    n, block, wide = grads.shape
    dm = w.shape[0]

    def whole(shape):
        return pl.BlockSpec(shape, lambda i, me: (0,) * len(shape))

    def one(width):
        return pl.BlockSpec((1, block, width), lambda i, me: (i, 0, 0))

    def half(width):
        return pl.BlockSpec((1, block, width), lambda i, me: (i // 2, 0, 0))

    pair = jax.ShapeDtypeStruct((n // 2, block, dm), BF16)
    return pl.pallas_call(
        leave_kernel,
        grid_spec=pltpu.PrefetchScalarGridSpec(
            num_scalar_prefetch=1,
            grid=(n,),
            in_specs=[one(dm), one(wide)] + [whole(a.shape) for a in (w, vecs, sums_two, sums_up)],
            out_specs=[half(dm), half(dm), whole((dm, wide + LANES))],
            scratch_shapes=[
                pltpu.VMEM((8, dm), F32),
                pltpu.VMEM((8, wide), F32),
                pltpu.VMEM(w.shape, F32),
                pltpu.VMEM((dm, LANES), F32),
            ],
        ),
        out_shape=[
            pair,
            pair,
            jax.ShapeDtypeStruct((dm, wide + LANES), BF16),
        ],
        compiler_params=pltpu.CompilerParams(vmem_limit_bytes=48 * 1024 * 1024),
        cost_estimate=pl.CostEstimate(flops=6 * 1000**3, bytes_accessed=10 * 1000**2, transcendentals=0),
        name="leave",
    )(me, x_all, grads, w, vecs, sums_two, sums_up)


def finish_kernel(me_ref, *refs, n, width):
    pieces, (q_ref, k_ref, v_ref, vec_ref) = refs[:n], refs[n:]
    vec_ref[...] = sum(p[:, 3 * width :] for p in pieces)
    parts = [p[:, : 3 * width] for p in pieces]
    bit = 1
    while bit < n:
        on = (me_ref[0] & bit) != 0
        for p in range(n):
            if not p & bit:
                a, b = parts[p], parts[p | bit]
                parts[p] = jnp.where(on, b, a)
                parts[p | bit] = jnp.where(on, a, b)
        bit *= 2
    for t in range(n):
        for i, ref in enumerate((q_ref, k_ref, v_ref)):
            ref[:, t * width : (t + 1) * width] = parts[t][:, i * width : (i + 1) * width]


def finish(me, pieces, width):
    n = len(pieces)
    rows = pieces[0].shape[0]
    weight = jax.ShapeDtypeStruct((rows, n * width), F32)
    return pl.pallas_call(
        functools.partial(finish_kernel, n=n, width=width),
        in_specs=[pl.BlockSpec(memory_space=pltpu.SMEM)] + [pl.BlockSpec(memory_space=pltpu.VMEM)] * n,
        out_specs=[pl.BlockSpec(memory_space=pltpu.VMEM)] * 4,
        out_shape=[weight] * 3 + [jax.ShapeDtypeStruct((rows, LANES), F32)],
        name="finish",
    )(me, *pieces)


def body(
    nd,
    ns,
    tokens,
    cotangent,
    segments,
    w_query,
    w_key,
    w_value,
    w_out,
    w_up,
    w_down,
    ln1_gain,
    ln1_shift,
    query_bias,
    value_bias,
    out_bias,
    ln2_gain,
    ln2_shift,
    up_bias,
    down_bias,
):
    d = lax.axis_index("dp")
    s = lax.axis_index("seq")
    me = s.astype(jnp.int32).reshape(1)
    _, block, dm = tokens.shape
    hd = dm // H
    heads = H // ns
    width = heads * hd
    rows = w_query.shape[0]
    ff_rows, ff = w_down.shape[0], w_up.shape[1]
    ratio = ff_rows // rows
    part = ff // ns
    pad = 16

    me = jnp.stack([s, d]).astype(jnp.int32)
    masks = bits_of(nd)[::-1]
    far = bits_of(ns)[-1]
    x_own = tokens.reshape(block, dm)
    g = cotangent.reshape(block, dm)
    x_far = swap(x_own, "seq", ns, far)

    cols = [w.reshape(rows, ns, width) for w in (w_query, w_key, w_value)]
    vec = jnp.stack([ln1_gain, ln1_shift, ln2_gain, ln2_shift, out_bias, down_bias, query_bias, value_bias], 1)
    vec = jnp.pad(vec, ((0, 0), (0, LANES - vec.shape[1])))
    up_cols = w_up.reshape(rows, nd, ns, ff_rows).transpose(0, 2, 1, 3).reshape(rows, ns, part)
    lanes = LANES * -(-block // (rows * LANES))
    seg = jnp.pad(segments.reshape(block).astype(BF16), (0, rows * lanes - block)).reshape(rows, lanes)
    same = jnp.concatenate([vec, w_out, seg], 1)
    same = jnp.broadcast_to(same[:, None], (rows, ns, same.shape[1]))
    pieces = jnp.concatenate(cols + [same, up_cols], 2).transpose(1, 0, 2)
    first = 3 * width + LANES
    size = ns * rows
    pieces = trade_seq(pieces, s, ns)
    start = first + dm
    segs = jnp.stack([p[:, start : start + lanes].reshape(-1)[:block] for p in pieces]).astype(jnp.int32)
    seg_row = segs.reshape(ns, 1, block)
    seg_col = segs.reshape(ns, block, 1)
    pieces = ordered(pieces, s).reshape(size, -1)
    lane = lax.broadcasted_iota(jnp.int32, (size, first), 1)
    one = jnp.where(lane == 3 * width + 8, jnp.pad(up_bias, (0, size - ff_rows))[:, None], pieces[:, :first])
    two = jnp.concatenate([pieces[:, first:start], pieces[:, start + lanes :], w_down], 0)
    left, right = two[:, : dm // 2], two[:, dm // 2 :]

    turned = masks[:-2] + masks[:-3:-1]
    ones, lefts, rights = [one[None]], [left[None]], [right[None]]
    for step, mask in enumerate(masks):
        got = swap(jnp.concatenate(ones, 0), "dp", nd, mask)
        if step == len(masks) - 2:
            got, x_far = lax.optimization_barrier((got, x_far))
            g_far = swap(tie(g, x_far), "seq", ns, far)
            lefts[0], rights[0] = tie(lefts[0], got), tie(rights[0], got)
        ones.append(got)

    def onward(step):
        for parts, order in ((lefts, masks), (rights, turned)):
            parts.append(swap(jnp.concatenate(parts, 0), "dp", nd, order[step]))

    for step in range(len(masks) - 2):
        onward(step)
    parts = {0: x_own, far: x_far}
    for mask in bits_of(ns)[-2::-1]:
        for p in list(parts):
            parts[p | mask] = swap(parts[p], "seq", ns, mask)
    x_all = jnp.stack([parts[p] for p in range(ns)])

    ones, ids = settle(ones, d, nd, masks, 1)
    ones[-1], x_all = lax.optimization_barrier((ones[-1], x_all))
    qkv, w_qkv, vecs = enter(me, ones, ids, x_all, width)
    qkv, g_far, lefts[-1], rights[-1] = lax.optimization_barrier((qkv, g_far, lefts[-1], rights[-1]))
    onward(len(masks) - 2)
    g_parts = {0: g, far: g_far}
    for mask in bits_of(ns)[-2::-1]:
        for p in list(g_parts):
            g_parts[p | mask] = swap(g_parts[p], "seq", ns, mask)
    o_low, o_full, lse = attend(me, qkv, seg_row, seg_col, heads, hd)
    o_got = spread_seq(o_low, ns)
    lefts[-1], rights[-1], g_parts[ns - 1] = lax.optimization_barrier((lefts[-1], rights[-1], g_parts[ns - 1], o_low))[:3]
    onward(len(masks) - 1)
    g_all = jnp.stack([g_parts[p] for p in range(ns)])
    lefts, left_ids = settle(lefts, d, nd, masks, 3)
    rights, right_ids = settle(rights, d, nd, turned, 3)
    ids = (left_ids, right_ids)
    h_two, act, gu, gh_two, gh_three, sums_up, *weights = feed(
        me, o_got, x_all, g_all, vecs, 2, (lefts, rights), ids
    )
    w_out_all, _, w_down_own = weights
    sent = add_low(gh_two, swap(gh_three, "seq", ns, 1))
    far_got = swap(sent, "seq", ns, 2)
    h_two, act, gu, sums_up = lax.optimization_barrier((h_two, act, gu, sums_up, sent))[:4]
    h_two, act, gu, gh_zero, gh_one, sums_up, x_two = feed(
        me, o_got, x_all, g_all, vecs, 0, weights, None, (sums_up, h_two, act, gu)
    )
    near_got = swap(gh_one, "seq", ns, 1)
    d_down = jnp.einsum("nbk,nbc->kc", act, g_all, preferred_element_type=F32).astype(BF16)
    d_up = jnp.einsum("nbk,nbc->kc", h_two, gu, preferred_element_type=F32).astype(BF16)
    feeds = jnp.concatenate([d_up.reshape(nd, size, part), d_down.reshape(nd, ff_rows, dm)], 1)
    feed_keep, feed_sent = halves(feeds, d, nd, 1)
    feed_got = swap(feed_sent, "dp", nd, 1)
    far_got, feed_sent = lax.optimization_barrier((far_got, feed_sent))
    *gos, gx_two, d_out, sums_two = turn(me, o_got, gh_zero, near_got, far_got, x_two, g, w_out_all, vecs)
    go_got = [gos[0]] + [swap(gos[p], "seq", ns, p) for p in range(1, ns)]
    outs_keep, outs_sent = halves(d_out.reshape(nd, size, dm), d, nd, 1)
    outs_got = swap(outs_sent, "dp", nd, 1)
    act = tie(act, gos[0])
    out_parts = [dot_nn(act[p], w_down_own).astype(BF16) for p in range(ns)]
    out_sent = add_low(out_parts[2], swap(out_parts[3], "seq", ns, 1))
    out_near = swap(out_parts[1], "seq", ns, 1)
    out_far = swap(tie(out_sent, go_got[-1]), "seq", ns, 2)

    go_all = jnp.stack(go_got)
    go_all, feed_got = lax.optimization_barrier((go_all, feed_got))
    feeds = add_low(feed_keep, feed_got)
    feed_keep, feed_sent = halves(feeds, d >> 1, nd // 2, 1)
    feed_got = swap(feed_sent, "dp", nd, 2)
    grads = attend_back(me, qkv, go_all, o_full, lse, seg_row, seg_col, heads, hd)
    grads, out_far, outs_got, feed_got = lax.optimization_barrier((grads, out_far, outs_got, feed_got))
    feed_keep, feed_sent = halves(add_low(feed_keep, feed_got), d >> 2, nd // 4, 1)
    feed_got = swap(feed_sent, "dp", nd, 4)
    outs_keep, outs_sent = halves(add_low(outs_keep, outs_got), d >> 1, nd // 2, 1)
    outs_got = swap(outs_sent, "dp", nd, 2)
    even, odd, blob = leave(me, x_all, grads, w_qkv, vecs, sums_two, sums_up)
    keep, sent, got = collect_pairs(even, odd, ns)
    blob_keep, blob_sent = halves(blob.reshape(nd, size, first), d, nd, 1)
    blob_got = swap(tie(blob_sent, sent), "dp", nd, 1)
    blob_got, feed_got, outs_got = lax.optimization_barrier((blob_got, feed_got, outs_got))
    blob = add_low(blob_keep, blob_got)
    blob_keep, blob_sent = halves(blob, d >> 1, nd // 2, 1)
    blob_got = swap(blob_sent, "dp", nd, 2)
    feeds = add_low(feed_keep, feed_got, F32 if nd == 8 else BF16)
    outs = add_low(outs_keep, outs_got)
    if nd > 8:
        feeds = collect_dp(feeds, d >> 3, nd // 8, shift=3)
    outs = collect_dp(outs, d >> 2, nd // 4, shift=2)
    blob_got, got = lax.optimization_barrier((blob_got, got))
    blob = add_low(blob_keep, blob_got)
    blob = collect_dp(blob, d >> 2, nd // 4, shift=2)
    out = out_parts[0].astype(F32) + out_near.astype(F32) + out_far.astype(F32) + x_two + vecs[5:6]
    trades = trade_seq(blob.reshape(ns, rows, first), s, ns)
    sum_up_bias = blob[:ff_rows, 3 * width + 8]
    gh_one = keep.astype(F32) + got.astype(F32)
    n_own, inv_own = normed_parts(x_own.astype(F32))
    grad_x = gx_two + normalize_back(gh_one, n_own, inv_own, vecs[0:1])
    sum_q, sum_k, sum_v, vec_sum = finish(me, trades, width)
    vec_sum = vec_sum.T
    feeds = feeds.reshape(size + ff_rows, dm)
    sum_down = feeds[size:]
    both = jnp.concatenate([outs, feeds[:size]], 1).reshape(ns, rows, dm + part)
    both = trade_seq(both, s, ns)
    sum_out = sum(b[:, :dm] for b in both)
    sum_up = ordered([b[:, dm:] for b in both], s)
    sum_up = sum_up.reshape(ns, rows, nd, ff_rows).transpose(1, 2, 0, 3).reshape(rows, ff)
    v = [vec_sum[i] for i in range(8)]
    return (
        out.reshape(1, block, dm),
        grad_x.reshape(1, block, dm),
        sum_q,
        sum_k,
        sum_v,
        sum_out,
        sum_up,
        sum_down,
        v[0],
        v[1],
        v[6],
        v[7],
        v[4],
        v[2],
        v[3],
        sum_up_bias,
        v[5],
    )


def solution(mesh):
    act = P("dp", "seq", None)
    weight = P(("dp", "seq"), None)
    vector = P(("dp", "seq"))
    return jax.shard_map(
        functools.partial(body, mesh.shape["dp"], mesh.shape["seq"]),
        mesh=mesh,
        in_specs=(act, act, P("dp", "seq")) + (weight,) * 6 + (vector,) * 9,
        out_specs=(act, act) + (weight,) * 6 + (vector,) * 9,
        check_vma=False,
    )
```

```python
import functools
import math

import jax
import jax.numpy as jnp
from jax import lax
from jax.experimental import pallas as pl
from jax.experimental.pallas import tpu as pltpu
from jax.sharding import PartitionSpec as P

H = 12
EPSILON = 1e-05
MASKED = -1e30
F32 = jnp.float32
BF16 = jnp.bfloat16
LANES = 128


def dot_nt(a, b):
    return lax.dot_general(a, b, (((1,), (1,)), ((), ())), preferred_element_type=F32)


def dot_tn(a, b):
    return lax.dot_general(a, b, (((0,), (0,)), ((), ())), preferred_element_type=F32)


def dot_nn(a, b):
    return jnp.dot(a, b, preferred_element_type=F32)


def attend_kernel(me_ref, qkv_ref, seg_row_ref, seg_col_ref, low_ref, full_ref, lse_ref, *, heads, hd):
    me = me_ref[0]
    qi = pl.program_id(0)
    rq = qi ^ me
    block = qkv_ref.shape[1]
    width = heads * hd
    scale = jnp.asarray(1.0 / math.sqrt(hd), BF16)
    queries = [qkv_ref[rq, :, h * hd : (h + 1) * hd] * scale for h in range(heads)]
    seg_q = seg_row_ref[rq]

    def step(rk, state, causal):
        allowed = seg_col_ref[rk] == seg_q
        if causal:
            k_pos = lax.broadcasted_iota(jnp.int32, (block, block), 0)
            q_pos = lax.broadcasted_iota(jnp.int32, (block, block), 1)
            allowed = allowed & (k_pos <= q_pos)
        new = []
        for h in range(heads):
            top, total, mixed = state[h]
            key = qkv_ref[rk, :, width + h * hd : width + (h + 1) * hd]
            value = qkv_ref[rk, :, 2 * width + h * hd : 2 * width + (h + 1) * hd]
            scores = jnp.where(allowed, dot_nt(key, queries[h]), MASKED)
            higher = jnp.maximum(top, jnp.max(scores, 0, keepdims=True))
            weights = jnp.exp(scores - higher)
            fade = jnp.exp(top - higher)
            total = total * fade + jnp.sum(weights, 0, keepdims=True)
            mixed = mixed * fade + dot_tn(value, weights.astype(BF16))
            new.append((higher, total, mixed))
        return tuple(new)

    start = tuple(
        (jnp.full((1, block), MASKED, F32), jnp.zeros((1, block), F32), jnp.zeros((hd, block), F32))
        for _ in range(heads)
    )
    state = lax.fori_loop(0, qi, lambda kj, c: step(kj ^ me, c, False), start)
    state = step(rq, state, True)
    rows = []
    for h in range(heads):
        top, total, mixed = state[h]
        rows.append(mixed / total)
        lse_ref[0, h : h + 1, :] = top + jnp.log(total)
    full = jnp.concatenate(rows, 0)
    full_ref[0] = full
    low_ref[0] = full.astype(BF16)


def attend(me, qkv, seg_row, seg_col, heads, hd):
    n, block, _ = qkv.shape
    width = heads * hd

    def whole(shape):
        return pl.BlockSpec(shape, lambda i, me: (0,) * len(shape))

    def own(shape):
        return pl.BlockSpec(shape, lambda i, me: (i ^ me[0], 0, 0))

    return pl.pallas_call(
        functools.partial(attend_kernel, heads=heads, hd=hd),
        grid_spec=pltpu.PrefetchScalarGridSpec(
            num_scalar_prefetch=1,
            grid=(n,),
            in_specs=[whole(qkv.shape), whole(seg_row.shape), whole(seg_col.shape)],
            out_specs=[own((1, width, block)), own((1, width, block)), own((1, 8, block))],
        ),
        out_shape=[
            jax.ShapeDtypeStruct((n, width, block), BF16),
            jax.ShapeDtypeStruct((n, width, block), F32),
            jax.ShapeDtypeStruct((n, 8, block), F32),
        ],
        compiler_params=pltpu.CompilerParams(vmem_limit_bytes=40 * 1024 * 1024),
        cost_estimate=pl.CostEstimate(
            flops=20 * 1000**3, bytes_accessed=8 * 1000**2, transcendentals=8 * 1000**2
        ),
        name="attend",
    )(me, qkv, seg_row, seg_col)


def attend_back_kernel(
    me_ref, qkv_ref, go_ref, full_ref, lse_ref, seg_row_ref, seg_col_ref, h_ref, grad_ref, d_w_ref,
    gq_ref, dot_ref, total_ref, *, heads, hd
):
    me = me_ref[0]
    kj = pl.program_id(0)
    rk = kj ^ me
    n, block, _ = qkv_ref.shape
    width = heads * hd
    scale = 1.0 / math.sqrt(hd)
    low_scale = jnp.asarray(scale, BF16)

    @pl.when(kj == 0)
    def _():
        gq_ref[...] = jnp.zeros_like(gq_ref)
        total_ref[...] = jnp.zeros_like(total_ref)
        for b in range(n):
            prod = go_ref[b].astype(F32) * full_ref[b]
            for h in range(heads):
                dot_ref[b, h : h + 1, :] = jnp.sum(prod[h * hd : (h + 1) * hd], 0, keepdims=True)

    keys = [qkv_ref[rk, :, width + h * hd : width + (h + 1) * hd] for h in range(heads)]
    values = [qkv_ref[rk, :, 2 * width + h * hd : 2 * width + (h + 1) * hd] for h in range(heads)]
    seg_k = seg_col_ref[rk]

    def step(rq, state, causal):
        allowed = seg_k == seg_row_ref[rq]
        if causal:
            k_pos = lax.broadcasted_iota(jnp.int32, (block, block), 0)
            q_pos = lax.broadcasted_iota(jnp.int32, (block, block), 1)
            allowed = allowed & (k_pos <= q_pos)
        new = []
        for h in range(heads):
            gk, gv = state[h]
            query = qkv_ref[rq, :, h * hd : (h + 1) * hd] * low_scale
            go = go_ref[rq, h * hd : (h + 1) * hd, :]
            scores = jnp.where(allowed, dot_nt(keys[h], query), MASKED)
            weights = jnp.exp(scores - lse_ref[rq, h : h + 1, :])
            gw = dot_nn(values[h], go)
            ds = (weights * (gw - dot_ref[rq, h : h + 1, :])).astype(BF16)
            gv = gv + dot_nt(weights.astype(BF16), go)
            gk = gk + dot_nn(ds, query)
            gq_ref[rq, h * hd : (h + 1) * hd, :] += dot_tn(keys[h], ds)
            new.append((gk, gv))
        return tuple(new)

    zero = jnp.zeros((block, hd), F32)
    state = step(rk, tuple((zero, zero) for _ in range(heads)), True)
    state = lax.fori_loop(kj + 1, n, lambda qi, c: step(qi ^ me, c, False), state)
    grad_ref[0, :, :width] = (gq_ref[rk] * scale).T.astype(BF16)
    for h in range(heads):
        gk, gv = state[h]
        grad_ref[0, :, width + h * hd : width + (h + 1) * hd] = gk.astype(BF16)
        grad_ref[0, :, 2 * width + h * hd : 2 * width + (h + 1) * hd] = gv.astype(BF16)
    total_ref[...] += dot_tn(h_ref[0], grad_ref[0])

    @pl.when(kj == n - 1)
    def _():
        d_w_ref[...] = total_ref[...].astype(BF16)


def attend_back(me, qkv, go, full, lse, seg_row, seg_col, h_one, heads, hd):
    n, block, wide = qkv.shape
    dm = h_one.shape[2]
    width = heads * hd

    def whole(shape):
        return pl.BlockSpec(shape, lambda i, me: (0,) * len(shape))

    return pl.pallas_call(
        functools.partial(attend_back_kernel, heads=heads, hd=hd),
        grid_spec=pltpu.PrefetchScalarGridSpec(
            num_scalar_prefetch=1,
            grid=(n,),
            in_specs=[whole(a.shape) for a in (qkv, go, full, lse, seg_row, seg_col)]
            + [pl.BlockSpec((1, block, dm), lambda i, me: (i ^ me[0], 0, 0))],
            out_specs=[pl.BlockSpec((1, block, wide), lambda i, me: (i ^ me[0], 0, 0)), whole((dm, wide))],
            scratch_shapes=[
                pltpu.VMEM((n, width, block), F32),
                pltpu.VMEM((n, 8, block), F32),
                pltpu.VMEM((dm, wide), F32),
            ],
        ),
        out_shape=[
            jax.ShapeDtypeStruct((n, block, wide), BF16),
            jax.ShapeDtypeStruct((dm, wide), BF16),
        ],
        compiler_params=pltpu.CompilerParams(vmem_limit_bytes=40 * 1024 * 1024),
        cost_estimate=pl.CostEstimate(
            flops=40 * 1000**3, bytes_accessed=12 * 1000**2, transcendentals=8 * 1000**2
        ),
        name="attend_back",
    )(me, qkv, go, full, lse, seg_row, seg_col, h_one)


def normed_parts(value):
    mean = jnp.mean(value, -1, keepdims=True)
    centred = value - mean
    inv_std = lax.rsqrt(jnp.mean(centred * centred, -1, keepdims=True) + EPSILON)
    return centred * inv_std, inv_std


def normalize_back(grad_in, normed, inv_std, gain):
    scaled = grad_in * gain
    return inv_std * (
        scaled
        - jnp.mean(scaled, -1, keepdims=True)
        - normed * jnp.mean(scaled * normed, -1, keepdims=True)
    )


def gelu_and_slope(value):
    cumul = 0.5 * (1.0 + lax.erf(value * (1.0 / math.sqrt(2.0))))
    slope = cumul + value * jnp.exp(-0.5 * value * value) * (1.0 / math.sqrt(2.0 * math.pi))
    return value * cumul, slope


def tie(value, *others):
    return lax.optimization_barrier((value,) + others)[0] if others else value


def swap(value, axis, size, mask):
    return lax.ppermute(value, axis, [(i, i ^ mask) for i in range(size)])


def bits_of(size):
    count = size.bit_length() - 1
    return [1 << b for b in range(count)]


def ordered(parts, index):
    parts = [part[None] for part in parts]
    bit = 1
    while len(parts) > 1:
        on = (index & bit) != 0
        parts = [
            jnp.where(on, jnp.concatenate([b, a], 0), jnp.concatenate([a, b], 0))
            for a, b in zip(parts[::2], parts[1::2])
        ]
        bit *= 2
    return parts[0]


def gathered_ids(masks):
    held, lists = [0], [[0]]
    for mask in masks:
        new = [r ^ mask for r in held]
        lists.append(new)
        held = held + new
    return lists


def settle(parts, index, size, masks, count):
    ids = gathered_ids(masks)
    rows = parts[0].shape[1] // count
    if rows % 16 == 0:
        return parts, ids
    held = sum(ids, [])
    at = jnp.asarray([held.index(r) for r in range(size)])
    whole = jnp.concatenate(parts, 0)[at[jnp.arange(size) ^ index]]
    whole = whole.reshape(size, count, rows, -1).transpose(1, 0, 2, 3)
    return [whole.reshape(1, size * count * rows, -1)], [[None]]


def place(refs, ids, index, count, put):
    for ref, held in zip(refs, ids):
        rows = ref.shape[1] // count
        for j, r in enumerate(held):
            where = slice(None) if r is None else pl.ds(pl.multiple_of((index ^ r) * rows, rows), rows)
            for k in range(count):
                put(k, where, ref[j, k * rows : (k + 1) * rows, :])


def halves(value, index, size, mask):
    value = value.reshape((-1, 2, mask) + value.shape[1:])
    on = ((index & mask) != 0).astype(jnp.int32)
    shape = (-1,) + value.shape[3:]
    keep = lax.dynamic_index_in_dim(value, on, 1, False).reshape(shape)
    return keep, lax.dynamic_index_in_dim(value, 1 - on, 1, False).reshape(shape)


def add_low(a, b, kind=BF16):
    return (a.astype(F32) + b.astype(F32)).astype(kind)


def collect_dp(value, index, size, last=F32, shift=0):
    masks = bits_of(size)
    shape = value.shape[1:]
    value = value.reshape((2,) * len(masks) + shape)
    for step, mask in enumerate(masks):
        axis = len(masks) - 1 - step
        on = ((index & mask) != 0).astype(jnp.int32)
        keep = lax.dynamic_index_in_dim(value, on, axis, False)
        send = lax.dynamic_index_in_dim(value, 1 - on, axis, False)
        got = swap(send, "dp", size << shift, mask << shift)
        value = keep.astype(F32) + got.astype(F32)
        value = value.astype(BF16 if step < len(masks) - 1 else last)
    return value


def collect_pairs(even, odd, size, tied=()):
    got = swap(odd, "seq", size, 1)
    sums = [(even[i].astype(F32) + got[i].astype(F32)).astype(BF16) for i in range(size // 2)]
    mask = 2
    while len(sums) > 2:
        sent = [swap(b, "seq", size, mask) for b in sums[1::2]]
        sums = [(a.astype(F32) + b.astype(F32)).astype(BF16) for a, b in zip(sums[::2], sent)]
        mask *= 2
    return sums[0], sums[1], swap(tie(sums[1], *tied), "seq", size, mask)


def spread_seq(value, size, gate=()):
    got = {0: value}
    for mask in bits_of(size)[::-1]:
        for p in list(got):
            got[p | mask] = swap(tie(got[p], *gate) if p else got[p], "seq", size, mask)
    return [got[p] for p in range(size)]


def trade_seq(pieces, index, size):
    return [
        swap(lax.dynamic_index_in_dim(pieces, index ^ p, 0, False), "seq", size, p)
        if p
        else lax.dynamic_index_in_dim(pieces, index, 0, False)
        for p in range(size)
    ]


def enter_kernel(me_ref, *refs, ids, n, width):
    count = len(ids)
    pieces, (x_ref, qkv_ref, h_ref, w_ref, vec_ref, tile_ref, add_ref) = refs[:count], refs[count:]
    me = me_ref[0]

    @pl.when(pl.program_id(0) == 0)
    def _():
        def put(k, where, rows):
            w_ref[where, :] = rows[:, : 3 * width]
            tile_ref[where, :] = rows[:, 3 * width :].astype(F32)

        place(pieces, ids, me_ref[1], 1, put)
        vecs = tile_ref[...].T[:16]
        vec_ref[...] = vecs
        for i, row in ((0, 6), (2, 7)):
            add = vecs[row : row + 1, :width]
            for t in range(1, n):
                add = jnp.where(me == t, vecs[row : row + 1, t * width : (t + 1) * width], add)
            add_ref[0:1, i * width : (i + 1) * width] = add
        add_ref[0:1, width : 2 * width] = jnp.zeros((1, width), F32)

    normed, _ = normed_parts(x_ref[0].astype(F32))
    h = (normed * vec_ref[0:1, :] + vec_ref[1:2, :]).astype(BF16)
    h_ref[0] = h
    qkv_ref[0] = (dot_nn(h, w_ref[...]) + add_ref[0:1, :]).astype(BF16)


def enter(me, pieces, ids, x_all, width):
    n, block, dm = x_all.shape

    def whole(shape):
        return pl.BlockSpec(shape, lambda i, me: (0,) * len(shape))

    def one(width):
        return pl.BlockSpec((1, block, width), lambda i, me: (i, 0, 0))

    return pl.pallas_call(
        functools.partial(enter_kernel, ids=ids, n=n, width=width),
        grid_spec=pltpu.PrefetchScalarGridSpec(
            num_scalar_prefetch=1,
            grid=(n,),
            in_specs=[whole(a.shape) for a in pieces] + [one(dm)],
            out_specs=[one(3 * width), one(dm), whole((dm, 3 * width)), whole((16, dm))],
            scratch_shapes=[pltpu.VMEM((dm, LANES), F32), pltpu.VMEM((8, 3 * width), F32)],
        ),
        out_shape=[
            jax.ShapeDtypeStruct((n, block, 3 * width), BF16),
            jax.ShapeDtypeStruct((n, block, dm), BF16),
            jax.ShapeDtypeStruct((dm, 3 * width), BF16),
            jax.ShapeDtypeStruct((16, dm), F32),
        ],
        compiler_params=pltpu.CompilerParams(vmem_limit_bytes=40 * 1024 * 1024),
        cost_estimate=pl.CostEstimate(flops=5 * 1000**3, bytes_accessed=8 * 1000**2, transcendentals=0),
        name="enter",
    )(me, *pieces, x_all)


def feed_kernel(me_ref, *refs, n, base, tile, ids):
    got, refs = refs[:n], refs[n:]
    me = me_ref[0]
    i = pl.program_id(0)
    if base:
        count = len(ids[0])
        left, right, refs = refs[:count], refs[count : 2 * count], refs[2 * count :]
        x_ref, g_ref, vec_ref = refs[:3]
        h_ref, act_ref, gu_ref, low_ref, high_ref, sum_ref, out_w_ref, up_ref, down_ref = refs[3:]
    else:
        x_ref, g_ref, vec_ref, out_w_ref, up_ref, down_ref, sum_in_ref = refs[:7]
        h_ref, act_ref, gu_ref, low_ref, high_ref, sum_ref, x_two_ref = refs[7:]
    part = up_ref.shape[1]
    width = got[0].shape[1]

    @pl.when(i == 0)
    def _():
        if base:
            sum_ref[...] = jnp.zeros_like(sum_ref)
            for first, pieces, held in ((0, left, ids[0]), (part // 2, right, ids[1])):

                def put(k, where, rows, first=first):
                    (out_w_ref, up_ref, down_ref)[k][where, first : first + part // 2] = rows

                place(pieces, held, me_ref[1], 3, put)
        else:
            sum_ref[...] = sum_in_ref[...]

    x_two = x_ref[0].astype(F32) + vec_ref[4:5, :]
    for p in range(n):
        own = pl.ds(pl.multiple_of((me ^ p) * width, width), width)
        x_two = x_two + dot_tn(got[p][0], out_w_ref[own, :])
    if not base:

        @pl.when(i == 0)
        def _():
            x_two_ref[...] = x_two

    normed, _ = normed_parts(x_two)
    h = (normed * vec_ref[2:3, :] + vec_ref[3:4, :]).astype(BF16)
    h_ref[0] = h
    g = g_ref[0]
    total = None
    for t in range(0, part, tile):
        cols = slice(t, t + tile)
        u = dot_nn(h, up_ref[:, cols]) + vec_ref[8:9, cols]
        act, slope = gelu_and_slope(u)
        act_ref[0, :, cols] = act.astype(BF16)
        gu = (dot_nt(g, down_ref[cols, :]) * slope).astype(BF16)
        gu_ref[0, :, cols] = gu
        sum_ref[0:1, cols] += jnp.sum(gu.astype(F32), 0, keepdims=True)
        term = dot_nt(gu, up_ref[:, cols])
        total = term if total is None else total + term
    total = total.astype(BF16)

    @pl.when(i == 0)
    def _():
        low_ref[...] = total

    @pl.when(i == 1)
    def _():
        high_ref[...] = total


def feed(me, got, x_all, g_all, vecs, base, weights, ids=None, held=()):
    n, block, dm = x_all.shape
    part = dm if base else weights[1].shape[1]
    width = got[0].shape[1]

    def whole(shape):
        return pl.BlockSpec(shape, lambda i, me: (0,) * len(shape))

    def one(width):
        return pl.BlockSpec((1, block, width), lambda i, me: (i + base, 0, 0))

    def new(width):
        return pl.BlockSpec((1, block, width), lambda i, me: (i, 0, 0))

    def piece(p):
        return pl.BlockSpec((1, width, block), lambda i, me: ((i + base) ^ p, 0, 0))

    if base:
        part = 2 * weights[0][0].shape[2]
        weights = [*weights[0], *weights[1]]
    wide = jax.ShapeDtypeStruct((2, block, dm), BF16)
    hidden = jax.ShapeDtypeStruct((2, block, part), BF16)
    low = jax.ShapeDtypeStruct((block, dm), BF16)
    outs = [wide, hidden, hidden, low, low, jax.ShapeDtypeStruct((8, part), F32)]
    specs = [new(dm), new(part), new(part)] + [whole(o.shape) for o in outs[3:]]
    more = [(dm, dm), (dm, part), (part, dm)] if base else []
    outs += [jax.ShapeDtypeStruct(m, BF16) for m in more] or [jax.ShapeDtypeStruct((block, dm), F32)]
    specs += [whole(o.shape) for o in outs[6:]]
    args = [*got]
    ins = [piece(p) for p in range(n)]
    if base:
        args += [*weights, x_all, g_all, vecs]
        ins += [whole(a.shape) for a in weights] + [one(dm), one(dm), whole(vecs.shape)]
    else:
        args += [x_all, g_all, vecs, *weights, held]
        ins += [one(dm), one(dm)] + [whole(a.shape) for a in (vecs, *weights, held)]
    return pl.pallas_call(
        functools.partial(feed_kernel, n=n, base=base, tile=256 if part % 256 == 0 else part, ids=ids),
        grid_spec=pltpu.PrefetchScalarGridSpec(num_scalar_prefetch=1, grid=(2,), in_specs=ins, out_specs=specs),
        out_shape=outs,
        compiler_params=pltpu.CompilerParams(vmem_limit_bytes=48 * 1024 * 1024),
        cost_estimate=pl.CostEstimate(
            flops=9 * 1000**3, bytes_accessed=16 * 1000**2, transcendentals=3 * 1000**2
        ),
        name="feed_far" if base else "feed_near",
    )(me, *args)


def turn_kernel(me_ref, *refs, n):
    got, refs = refs[:n], refs[n:]
    keep_ref, near_ref, far_ref, x_two_ref, g_ref, out_w_ref, vec_ref = refs[:7]
    gos, (gx_ref, d_out_ref, sum_ref) = refs[7 : 7 + n], refs[7 + n :]
    me = me_ref[0]
    width = got[0].shape[1]
    gh = keep_ref[...].astype(F32) + near_ref[...].astype(F32) + far_ref[...].astype(F32)
    normed, inv_std = normed_parts(x_two_ref[...])
    g = g_ref[...].astype(F32)
    gx = g + normalize_back(gh, normed, inv_std, vec_ref[2:3, :])
    gx_ref[...] = gx
    gb = gx.astype(BF16)
    for p in range(n):
        own = pl.ds(pl.multiple_of((me ^ p) * width, width), width)
        gos[p][...] = dot_nt(out_w_ref[own, :], gb).astype(BF16)
        d_out_ref[own, :] = dot_nn(got[p][0], gb).astype(BF16)
    sum_ref[0:1, :] = jnp.sum(gh * normed, 0, keepdims=True)
    sum_ref[1:2, :] = jnp.sum(gh, 0, keepdims=True)
    sum_ref[2:3, :] = jnp.sum(gb.astype(F32), 0, keepdims=True)
    sum_ref[3:4, :] = jnp.sum(g, 0, keepdims=True)


def turn(me, got, keep, near, far, x_two, g, out_w, vecs):
    n = len(got)
    _, width, block = got[0].shape
    dm = out_w.shape[1]

    def whole(shape):
        return pl.BlockSpec(shape, lambda i, me: (0,) * len(shape))

    def piece(p):
        return pl.BlockSpec((1, width, block), lambda i, me: (p, 0, 0))

    outs = [jax.ShapeDtypeStruct((width, block), BF16)] * n + [
        jax.ShapeDtypeStruct((block, dm), F32),
        jax.ShapeDtypeStruct(out_w.shape, BF16),
        jax.ShapeDtypeStruct((8, dm), F32),
    ]
    return pl.pallas_call(
        functools.partial(turn_kernel, n=n),
        grid_spec=pltpu.PrefetchScalarGridSpec(
            num_scalar_prefetch=1,
            grid=(1,),
            in_specs=[piece(p) for p in range(n)]
            + [whole(a.shape) for a in (keep, near, far, x_two, g, out_w, vecs)],
            out_specs=[whole(o.shape) for o in outs],
        ),
        out_shape=outs,
        compiler_params=pltpu.CompilerParams(vmem_limit_bytes=48 * 1024 * 1024),
        cost_estimate=pl.CostEstimate(flops=3 * 1000**3, bytes_accessed=8 * 1000**2, transcendentals=0),
        name="turn",
    )(me, *got, keep, near, far, x_two, g, out_w, vecs)


def leave_kernel(
    me_ref, x_ref, grad_ref, w_ref, vec_ref, two_ref, up_ref, even_ref, odd_ref, out_ref, sum_ref, add_ref, tile_ref
):
    i = pl.program_id(0)

    @pl.when(i == 0)
    def _():
        sum_ref[...] = jnp.zeros_like(sum_ref)
        add_ref[...] = jnp.zeros_like(add_ref)

    grads = grad_ref[0]
    gh = dot_nt(grads, w_ref[...])
    normed, _ = normed_parts(x_ref[0].astype(F32))
    low = gh.astype(BF16)

    @pl.when(i % 2 == 0)
    def _():
        even_ref[0] = low

    @pl.when(i % 2 == 1)
    def _():
        odd_ref[0] = low

    sum_ref[0:1, :] += jnp.sum(gh * normed, 0, keepdims=True)
    sum_ref[1:2, :] += jnp.sum(gh, 0, keepdims=True)
    add_ref[0:1, :] += jnp.sum(grads.astype(F32), 0, keepdims=True)

    @pl.when(i == pl.num_programs(0) - 1)
    def _():
        width = grads.shape[1] // 3
        dm = w_ref.shape[0]
        rows = [sum_ref[0:2, :], two_ref[0:4, :], jnp.zeros((2, dm), F32), up_ref[0:1, :]]
        rows = jnp.concatenate(rows + [jnp.zeros((LANES - 9, dm), F32)], 0)
        tile_ref[...] = rows.T
        add = jnp.concatenate(
            [
                jnp.zeros((6, width), F32),
                add_ref[0:1, :width],
                add_ref[0:1, 2 * width :],
                jnp.zeros((LANES - 8, width), F32),
            ],
            0,
        )
        own = pl.ds(pl.multiple_of(me_ref[0] * width, width), width)
        tile_ref[own, :] += add.T
        out_ref[...] = tile_ref[...].astype(BF16)


def leave(me, x_all, grads, w, vecs, sums_two, sums_up):
    n, block, wide = grads.shape
    dm = w.shape[0]

    def whole(shape):
        return pl.BlockSpec(shape, lambda i, me: (0,) * len(shape))

    def one(width):
        return pl.BlockSpec((1, block, width), lambda i, me: (i, 0, 0))

    def half(width):
        return pl.BlockSpec((1, block, width), lambda i, me: (i // 2, 0, 0))

    pair = jax.ShapeDtypeStruct((n // 2, block, dm), BF16)
    return pl.pallas_call(
        leave_kernel,
        grid_spec=pltpu.PrefetchScalarGridSpec(
            num_scalar_prefetch=1,
            grid=(n,),
            in_specs=[one(dm), one(wide)] + [whole(a.shape) for a in (w, vecs, sums_two, sums_up)],
            out_specs=[half(dm), half(dm), whole((dm, LANES))],
            scratch_shapes=[
                pltpu.VMEM((8, dm), F32),
                pltpu.VMEM((8, wide), F32),
                pltpu.VMEM((dm, LANES), F32),
            ],
        ),
        out_shape=[
            pair,
            pair,
            jax.ShapeDtypeStruct((dm, LANES), BF16),
        ],
        compiler_params=pltpu.CompilerParams(vmem_limit_bytes=48 * 1024 * 1024),
        cost_estimate=pl.CostEstimate(flops=6 * 1000**3, bytes_accessed=10 * 1000**2, transcendentals=0),
        name="leave",
    )(me, x_all, grads, w, vecs, sums_two, sums_up)


def hand_over_kernel(me_ref, *refs, n, rows):
    blob_a, blob_b, outs_a, outs_b, feed_a, feed_b = refs[:6]
    pieces, (out_ref, down_ref, last_ref) = refs[6 : 6 + n], refs[6 + n :]
    size = n * rows
    blob = blob_a[...].astype(F32) + blob_b[...].astype(F32)
    feed = feed_a[...].astype(F32) + feed_b[...].astype(F32)
    out_ref[...] = outs_a[...].astype(F32) + outs_b[...].astype(F32)
    down_ref[...] = feed[size:]
    last_ref[...] = blob[:, -LANES:]
    both = jnp.concatenate([blob, feed[:size]], 1)
    parts = [both[t * rows : (t + 1) * rows] for t in range(n)]
    for p, ref in enumerate(pieces):
        chosen = parts[0]
        for t in range(1, n):
            chosen = jnp.where((me_ref[0] ^ p) == t, parts[t], chosen)
        ref[...] = chosen.astype(BF16)


def hand_over(me, blob, outs, feeds, rows, n):
    args = [*blob, *outs, *feeds]
    wide = blob[0].shape[1] + feeds[0].shape[1]
    size = blob[0].shape[0]
    vmem = pl.BlockSpec(memory_space=pltpu.VMEM)
    *pieces, out, down, last = pl.pallas_call(
        functools.partial(hand_over_kernel, n=n, rows=rows),
        in_specs=[pl.BlockSpec(memory_space=pltpu.SMEM)] + [vmem] * 6,
        out_specs=[vmem] * (n + 3),
        out_shape=[jax.ShapeDtypeStruct((rows, wide), BF16)] * n
        + [
            jax.ShapeDtypeStruct(outs[0].shape, F32),
            jax.ShapeDtypeStruct((feeds[0].shape[0] - size, feeds[0].shape[1]), F32),
            jax.ShapeDtypeStruct((size, LANES), F32),
        ],
        name="hand_over",
    )(me, *args)
    return pieces, out, down, last


def finish_kernel(me_ref, *refs, n, width, nd):
    pieces, (q_ref, k_ref, v_ref, vec_ref, up_ref) = refs[:n], refs[n:]
    first = 3 * width + LANES
    pieces = [p[...].astype(F32) for p in pieces]
    vec_ref[...] = sum(p[:, 3 * width : first] for p in pieces)
    bit = 1
    while bit < n:
        on = (me_ref[0] & bit) != 0
        for p in range(n):
            if not p & bit:
                a, b = pieces[p], pieces[p | bit]
                pieces[p] = jnp.where(on, b, a)
                pieces[p | bit] = jnp.where(on, a, b)
        bit *= 2
    step = (pieces[0].shape[1] - first) // nd
    for t in range(n):
        for i, ref in enumerate((q_ref, k_ref, v_ref)):
            ref[:, t * width : (t + 1) * width] = pieces[t][:, i * width : (i + 1) * width]
        for j in range(nd):
            to = (j * n + t) * step
            up_ref[:, to : to + step] = pieces[t][:, first + j * step : first + (j + 1) * step]


def finish(me, pieces, width, nd):
    n = len(pieces)
    rows, wide = pieces[0].shape
    weight = jax.ShapeDtypeStruct((rows, n * width), F32)
    tile = jax.ShapeDtypeStruct((rows, LANES), F32)
    vmem = pl.BlockSpec(memory_space=pltpu.VMEM)
    return pl.pallas_call(
        functools.partial(finish_kernel, n=n, width=width, nd=nd),
        in_specs=[pl.BlockSpec(memory_space=pltpu.SMEM)] + [vmem] * n,
        out_specs=[vmem] * 5,
        out_shape=[weight] * 3 + [tile, jax.ShapeDtypeStruct((rows, n * (wide - 3 * width - LANES)), F32)],
        name="finish",
    )(me, *pieces)


def body(
    nd,
    ns,
    tokens,
    cotangent,
    segments,
    w_query,
    w_key,
    w_value,
    w_out,
    w_up,
    w_down,
    ln1_gain,
    ln1_shift,
    query_bias,
    value_bias,
    out_bias,
    ln2_gain,
    ln2_shift,
    up_bias,
    down_bias,
):
    d = lax.axis_index("dp")
    s = lax.axis_index("seq")
    me = s.astype(jnp.int32).reshape(1)
    _, block, dm = tokens.shape
    hd = dm // H
    heads = H // ns
    width = heads * hd
    rows = w_query.shape[0]
    ff_rows, ff = w_down.shape[0], w_up.shape[1]
    ratio = ff_rows // rows
    part = ff // ns
    pad = 16

    me = jnp.stack([s, d]).astype(jnp.int32)
    masks = bits_of(nd)[::-1]
    far = bits_of(ns)[-1]
    x_own = tokens.reshape(block, dm)
    g = cotangent.reshape(block, dm)
    x_far = swap(x_own, "seq", ns, far)

    cols = [w.reshape(rows, ns, width) for w in (w_query, w_key, w_value)]
    vec = jnp.stack([ln1_gain, ln1_shift, ln2_gain, ln2_shift, out_bias, down_bias, query_bias, value_bias], 1)
    vec = jnp.pad(vec, ((0, 0), (0, LANES - vec.shape[1])))
    up_cols = w_up.reshape(rows, nd, ns, ff_rows).transpose(0, 2, 1, 3).reshape(rows, ns, part)
    lanes = LANES * -(-block // (rows * LANES))
    seg = jnp.pad(segments.reshape(block).astype(BF16), (0, rows * lanes - block)).reshape(rows, lanes)
    same = jnp.concatenate([vec, w_out, seg], 1)
    same = jnp.broadcast_to(same[:, None], (rows, ns, same.shape[1]))
    pieces = jnp.concatenate(cols + [same, up_cols], 2).transpose(1, 0, 2)
    first = 3 * width + LANES
    size = ns * rows
    pieces = trade_seq(pieces, s, ns)
    start = first + dm
    segs = jnp.stack([p[:, start : start + lanes].reshape(-1)[:block] for p in pieces]).astype(jnp.int32)
    seg_row = segs.reshape(ns, 1, block)
    seg_col = segs.reshape(ns, block, 1)
    pieces = ordered(pieces, s).reshape(size, -1)
    lane = lax.broadcasted_iota(jnp.int32, (size, first), 1)
    one = jnp.where(lane == 3 * width + 8, jnp.pad(up_bias, (0, size - ff_rows))[:, None], pieces[:, :first])
    two = jnp.concatenate([pieces[:, first:start], pieces[:, start + lanes :], w_down], 0)
    left, right = two[:, : dm // 2], two[:, dm // 2 :]

    turned = masks[:-2] + masks[:-3:-1]
    ones, lefts, rights = [one[None]], None, None
    for step, mask in enumerate(masks):
        both = jnp.concatenate(ones, 0)
        if step == len(masks) - 2:
            both, left, right, seg_row, seg_col = lax.optimization_barrier((both, left, right, seg_row, seg_col))
            lefts, rights = [left[None]], [right[None]]
        got = swap(both, "dp", nd, mask)
        if step == len(masks) - 2:
            got, x_far = lax.optimization_barrier((got, x_far))
            g_far = swap(tie(g, x_far), "seq", ns, far)
            lefts[0], rights[0] = tie(lefts[0], got), tie(rights[0], got)
        ones.append(got)

    for step in range(len(masks) - 2):
        lefts.append(swap(jnp.concatenate(lefts, 0), "dp", nd, masks[step]))
        rights.append(swap(jnp.concatenate(rights, 0), "dp", nd, turned[step]))
    parts = {0: x_own, far: x_far}
    for mask in bits_of(ns)[-2::-1]:
        for p in list(parts):
            parts[p | mask] = swap(parts[p], "seq", ns, mask)
    x_all = jnp.stack([parts[p] for p in range(ns)])

    ones, ids = settle(ones, d, nd, masks, 1)
    ones[-1], x_all = lax.optimization_barrier((ones[-1], x_all))
    qkv, h_one, w_qkv, vecs = enter(me, ones, ids, x_all, width)
    qkv, h_one, w_qkv, vecs, g_far, lefts[-1], rights[-1] = lax.optimization_barrier(
        (qkv, h_one, w_qkv, vecs, g_far, lefts[-1], rights[-1])
    )

    def onward(parts, mask):
        held = jnp.concatenate(parts, 0)
        return held, swap(held, "dp", nd, mask)

    left_held, left_got = onward(lefts, masks[-2])
    right_held, right_got = onward(rights, turned[-2])
    g_parts = {0: g, far: g_far}
    for mask in bits_of(ns)[-2::-1]:
        for p in list(g_parts):
            g_parts[p | mask] = swap(g_parts[p], "seq", ns, mask)
    qkv, left_held, right_held = lax.optimization_barrier((qkv, left_held, right_held))
    o_low, o_full, lse = attend(me, qkv, seg_row, seg_col, heads, hd)
    o_low, o_full, lse, left_got, right_got, *g_last = lax.optimization_barrier(
        (o_low, o_full, lse, left_got, right_got, g_parts[1], g_parts[ns - 1])
    )
    o_got = spread_seq(o_low, ns)
    lefts.append(left_got)
    rights.append(right_got)
    lefts.append(onward(lefts, masks[-1])[1])
    rights.append(onward(rights, turned[-1])[1])
    g_all = jnp.stack([g, g_last[0], g_far, g_last[1]])
    lefts, left_ids = settle(lefts, d, nd, masks, 3)
    rights, right_ids = settle(rights, d, nd, turned, 3)
    ids = (left_ids, right_ids)
    far_h, far_act, far_gu, gh_two, gh_three, sums_up, *weights = feed(
        me, o_got, x_all, g_all, vecs, 2, (lefts, rights), ids
    )
    w_out_all, _, w_down_own = weights

    def over_rows(a, b):
        return jnp.einsum("nbk,nbc->kc", a, b, preferred_element_type=F32)

    d_down = over_rows(far_act, g_all[2:])
    sent = add_low(gh_two, swap(gh_three, "seq", ns, 1))
    far_got = swap(sent, "seq", ns, 2)
    sums_up, sent, d_down = lax.optimization_barrier((sums_up, sent, d_down))
    h_two, act, gu, gh_zero, gh_one, sums_up, x_two = feed(
        me, o_got, x_all, g_all, vecs, 0, weights, None, sums_up
    )
    near_got = swap(gh_one, "seq", ns, 1)
    d_down = (d_down + over_rows(act, g_all[:2])).astype(BF16)
    d_up = (over_rows(far_h, far_gu) + over_rows(h_two, gu)).astype(BF16)
    up_keep, up_sent = halves(d_up.reshape(nd, size, part), d, nd, 1)
    down_keep, down_sent = halves(d_down.reshape(nd, ff_rows, dm), d, nd, 2)
    up_got, down_got = swap(up_sent, "dp", nd, 1), swap(down_sent, "dp", nd, 2)
    far_got, up_sent, down_sent = lax.optimization_barrier((far_got, up_sent, down_sent))
    *gos, gx_two, d_out, sums_two = turn(me, o_got, gh_zero, near_got, far_got, x_two, g, w_out_all, vecs)
    go_got = [gos[0]] + [swap(gos[p], "seq", ns, p) for p in range(1, ns)]
    d_out, sums_two, up_got, down_got = lax.optimization_barrier((d_out, sums_two, up_got, down_got))
    act, far_act = lax.optimization_barrier((act, far_act, gos[0]))[:2]
    out_parts = [dot_nn(a, w_down_own).astype(BF16) for a in (act[0], act[1], far_act[0], far_act[1])]
    out_sent = add_low(out_parts[2], swap(out_parts[3], "seq", ns, 1))
    out_near = swap(out_parts[1], "seq", ns, 1)
    out_far = swap(tie(out_sent, go_got[-1]), "seq", ns, 2)
    outs_keep, outs_sent = halves(d_out.reshape(nd * ns, rows, dm), s, ns, 1)
    outs_got = swap(outs_sent, "seq", ns, 1)
    outs_keep, outs_sent = halves(add_low(outs_keep, outs_got), s >> 1, ns // 2, 1)
    outs_got = swap(outs_sent, "seq", ns, 2)

    up_keep, up_sent = halves(add_low(up_keep, up_got), d >> 1, nd // 2, 1)
    down_keep, down_sent = halves(add_low(down_keep, down_got), d, nd, 1)
    up_got, down_got = swap(up_sent, "dp", nd, 2), swap(down_sent, "dp", nd, 1)
    go_all = jnp.stack(go_got)
    go_all, *_ = lax.optimization_barrier((go_all, out_sent, out_parts, outs_sent, up_sent, down_sent))
    grads, d_qkv = attend_back(me, qkv, go_all, o_full, lse, seg_row, seg_col, h_one, heads, hd)
    grads, d_qkv, out_near, out_far, outs_got, up_got, down_got = lax.optimization_barrier(
        (grads, d_qkv, out_near, out_far, outs_got, up_got, down_got)
    )
    blob_keep, blob_sent = halves(d_qkv.reshape(nd, size, 3 * width), d, nd, 1)
    blob_got = swap(blob_sent, "dp", nd, 1)
    feeds = jnp.concatenate([add_low(up_keep, up_got), add_low(down_keep, down_got)], 1)
    feed_keep, feed_sent = halves(feeds, d >> 2, nd // 4, 1)
    feed_got = swap(feed_sent, "dp", nd, 4)
    outs_keep, outs_sent = halves(add_low(outs_keep, outs_got), d, nd, 1)
    outs_got = swap(outs_sent, "dp", nd, 1)
    grads = lax.optimization_barrier((grads, blob_sent, feed_sent, outs_sent))[0]
    even, odd, tile = leave(me, x_all, grads, w_qkv, vecs, sums_two, sums_up)
    even, odd, tile, blob_got, outs_got, feed_got = lax.optimization_barrier(
        (even, odd, tile, blob_got, outs_got, feed_got)
    )
    blob_keep, blob_sent = halves(add_low(blob_keep, blob_got), d >> 1, nd // 2, 1)
    blob_got = swap(blob_sent, "dp", nd, 2)
    tile = tile.reshape(nd // 4, 4, size, LANES)
    tiles = [lax.dynamic_index_in_dim(tile, (d & 3) ^ p, 1, False) for p in range(4)]
    tiles = [swap(tiles[p], "dp", nd, p) if p else tiles[0] for p in range(4)]
    outs_keep, outs_sent = halves(add_low(outs_keep, outs_got), d >> 1, nd // 2, 1)
    outs_got = swap(outs_sent, "dp", nd, 2)
    keep, sent, got = collect_pairs(even, odd, ns)
    blob_got, sent, outs_got, tiles[1:] = lax.optimization_barrier((blob_got, sent, outs_got, tiles[1:]))
    tile = sum(t.astype(F32) for t in tiles).astype(BF16)
    blob = jnp.concatenate([add_low(blob_keep, blob_got), tile], 2)
    blob_keep, blob_sent = halves(blob, d >> 2, nd // 4, 1)
    blob_got = swap(blob_sent, "dp", nd, 4)
    outs_keep, outs_sent = halves(add_low(outs_keep, outs_got), d >> 2, nd // 4, 1)
    outs_got = swap(outs_sent, "dp", nd, 4)
    blob_got, outs_got = lax.optimization_barrier((blob_got, outs_got))
    if nd > 8:
        rest = [(blob_keep, blob_got), (outs_keep, outs_got), (feed_keep, feed_got)]
        rest = [collect_dp(add_low(a, b), d >> 3, nd // 8, BF16, shift=3) for a, b in rest]
        rest = [(v, jnp.zeros_like(v)) for v in rest]
    else:
        rest = [(blob_keep[0], blob_got[0]), (outs_keep[0], outs_got[0]), (feed_keep[0], feed_got[0])]
    pieces, sum_out, sum_down, last = hand_over(me, *rest, rows, ns)
    out = out_parts[0].astype(F32) + out_near.astype(F32) + out_far.astype(F32) + x_two + vecs[5:6]
    trades = [pieces[0]] + [swap(pieces[p], "seq", ns, p) for p in range(1, ns)]
    gh_one = keep.astype(F32) + got.astype(F32)
    n_own, inv_own = normed_parts(x_own.astype(F32))
    grad_x = gx_two + normalize_back(gh_one, n_own, inv_own, vecs[0:1])
    trades, grad_x, out, last = lax.optimization_barrier((trades, grad_x, out, last))
    sum_q, sum_k, sum_v, vec_sum, sum_up = finish(me, trades, width, nd)
    vec_sum = vec_sum.T
    sum_up_bias = last[:ff_rows, 8]
    v = [vec_sum[i] for i in range(8)]
    return (
        out.reshape(1, block, dm),
        grad_x.reshape(1, block, dm),
        sum_q,
        sum_k,
        sum_v,
        sum_out,
        sum_up,
        sum_down,
        v[0],
        v[1],
        v[6],
        v[7],
        v[4],
        v[2],
        v[3],
        sum_up_bias,
        v[5],
    )


def solution(mesh):
    act = P("dp", "seq", None)
    weight = P(("dp", "seq"), None)
    vector = P(("dp", "seq"))
    return jax.shard_map(
        functools.partial(body, mesh.shape["dp"], mesh.shape["seq"]),
        mesh=mesh,
        in_specs=(act, act, P("dp", "seq")) + (weight,) * 6 + (vector,) * 9,
        out_specs=(act, act) + (weight,) * 6 + (vector,) * 9,
        check_vma=False,
    )
```

```python
import functools
import math

import jax
import jax.numpy as jnp
from jax import lax
from jax.experimental import pallas as pl
from jax.experimental.pallas import tpu as pltpu
from jax.sharding import PartitionSpec as P

H = 12
EPSILON = 1e-05
MASKED = -1e30
F32 = jnp.float32
BF16 = jnp.bfloat16
LANES = 128


def dot_nt(a, b):
    return lax.dot_general(a, b, (((1,), (1,)), ((), ())), preferred_element_type=F32)


def dot_tn(a, b):
    return lax.dot_general(a, b, (((0,), (0,)), ((), ())), preferred_element_type=F32)


def dot_nn(a, b):
    return jnp.dot(a, b, preferred_element_type=F32)


def attend_kernel(me_ref, qkv_ref, seg_row_ref, seg_col_ref, low_ref, full_ref, lse_ref, *, heads, hd):
    me = me_ref[0]
    qi = pl.program_id(0)
    rq = qi ^ me
    block = qkv_ref.shape[1]
    width = heads * hd
    scale = jnp.asarray(1.0 / math.sqrt(hd), BF16)
    queries = [qkv_ref[rq, :, h * hd : (h + 1) * hd] * scale for h in range(heads)]
    seg_q = seg_row_ref[rq]

    def step(rk, state, causal):
        allowed = seg_col_ref[rk] == seg_q
        if causal:
            k_pos = lax.broadcasted_iota(jnp.int32, (block, block), 0)
            q_pos = lax.broadcasted_iota(jnp.int32, (block, block), 1)
            allowed = allowed & (k_pos <= q_pos)
        new = []
        for h in range(heads):
            top, total, mixed = state[h]
            key = qkv_ref[rk, :, width + h * hd : width + (h + 1) * hd]
            value = qkv_ref[rk, :, 2 * width + h * hd : 2 * width + (h + 1) * hd]
            scores = jnp.where(allowed, dot_nt(key, queries[h]), MASKED)
            higher = jnp.maximum(top, jnp.max(scores, 0, keepdims=True))
            weights = jnp.exp(scores - higher)
            fade = jnp.exp(top - higher)
            total = total * fade + jnp.sum(weights, 0, keepdims=True)
            mixed = mixed * fade + dot_tn(value, weights.astype(BF16))
            new.append((higher, total, mixed))
        return tuple(new)

    start = tuple(
        (jnp.full((1, block), MASKED, F32), jnp.zeros((1, block), F32), jnp.zeros((hd, block), F32))
        for _ in range(heads)
    )
    state = lax.fori_loop(0, qi, lambda kj, c: step(kj ^ me, c, False), start)
    state = step(rq, state, True)
    rows = []
    for h in range(heads):
        top, total, mixed = state[h]
        rows.append(mixed / total)
        lse_ref[0, h : h + 1, :] = top + jnp.log(total)
    full = jnp.concatenate(rows, 0)
    full_ref[0] = full
    low_ref[0] = full.astype(BF16)


def attend(me, qkv, seg_row, seg_col, heads, hd):
    n, block, _ = qkv.shape
    width = heads * hd

    def whole(shape):
        return pl.BlockSpec(shape, lambda i, me: (0,) * len(shape))

    def own(shape):
        return pl.BlockSpec(shape, lambda i, me: (i ^ me[0], 0, 0))

    return pl.pallas_call(
        functools.partial(attend_kernel, heads=heads, hd=hd),
        grid_spec=pltpu.PrefetchScalarGridSpec(
            num_scalar_prefetch=1,
            grid=(n,),
            in_specs=[whole(qkv.shape), whole(seg_row.shape), whole(seg_col.shape)],
            out_specs=[own((1, width, block)), own((1, width, block)), own((1, 8, block))],
        ),
        out_shape=[
            jax.ShapeDtypeStruct((n, width, block), BF16),
            jax.ShapeDtypeStruct((n, width, block), F32),
            jax.ShapeDtypeStruct((n, 8, block), F32),
        ],
        compiler_params=pltpu.CompilerParams(vmem_limit_bytes=40 * 1024 * 1024),
        cost_estimate=pl.CostEstimate(
            flops=20 * 1000**3, bytes_accessed=8 * 1000**2, transcendentals=8 * 1000**2
        ),
        name="attend",
    )(me, qkv, seg_row, seg_col)


def attend_back_kernel(
    me_ref, qkv_ref, go_ref, full_ref, lse_ref, seg_row_ref, seg_col_ref, h_ref, grad_ref, d_w_ref,
    gq_ref, dot_ref, total_ref, gk_ref, gv_ref, *, heads, hd
):
    me = me_ref[0]
    kj = pl.program_id(0)
    rk = kj ^ me
    n, block, _ = qkv_ref.shape
    width = heads * hd
    scale = 1.0 / math.sqrt(hd)
    low_scale = jnp.asarray(scale, BF16)

    @pl.when(kj == 0)
    def _():
        gq_ref[...] = jnp.zeros_like(gq_ref)
        total_ref[...] = jnp.zeros_like(total_ref)
        for b in range(n):
            prod = go_ref[b].astype(F32) * full_ref[b]
            for h in range(heads):
                dot_ref[b, h : h + 1, :] = jnp.sum(prod[h * hd : (h + 1) * hd], 0, keepdims=True)

    def step(rq, causal):
        for k0 in range(0, block, 512):
            for q0 in range(0, block, 256):
                if causal and q0 + 256 <= k0:
                    continue
                rows, cols = slice(k0, k0 + 512), slice(q0, q0 + 256)
                allowed = seg_col_ref[rk, rows, :] == seg_row_ref[rq][:, cols]
                if causal and q0 < k0 + 512:
                    k_pos = lax.broadcasted_iota(jnp.int32, (512, 256), 0) + k0
                    q_pos = lax.broadcasted_iota(jnp.int32, (512, 256), 1) + q0
                    allowed = allowed & (k_pos <= q_pos)
                for h in range(heads):
                    head = slice(h * hd, (h + 1) * hd)
                    query = qkv_ref[rq, cols, head] * low_scale
                    key = qkv_ref[rk, rows, width + h * hd : width + (h + 1) * hd]
                    value = qkv_ref[rk, rows, 2 * width + h * hd : 2 * width + (h + 1) * hd]
                    go = go_ref[rq, head, cols]
                    scores = jnp.where(allowed, dot_nt(key, query), MASKED)
                    weights = jnp.exp(scores - lse_ref[rq, h : h + 1, cols])
                    gw = dot_nn(value, go)
                    ds = (weights * (gw - dot_ref[rq, h : h + 1, cols])).astype(BF16)
                    gv = dot_nt(weights.astype(BF16), go)
                    gk = dot_nn(ds, query)
                    if causal and q0 <= k0:
                        gv_ref[h, rows, :] = gv
                        gk_ref[h, rows, :] = gk
                    else:
                        gv_ref[h, rows, :] += gv
                        gk_ref[h, rows, :] += gk
                    gq_ref[rq, head, cols] += dot_tn(key, ds)

    step(rk, True)

    @pl.loop(kj + 1, n)
    def _(qi):
        step(qi ^ me, False)

    grad_ref[0, :, :width] = (gq_ref[rk] * scale).T.astype(BF16)
    for h in range(heads):
        gk, gv = gk_ref[h], gv_ref[h]
        grad_ref[0, :, width + h * hd : width + (h + 1) * hd] = gk.astype(BF16)
        grad_ref[0, :, 2 * width + h * hd : 2 * width + (h + 1) * hd] = gv.astype(BF16)
    total_ref[...] += dot_tn(h_ref[0], grad_ref[0])

    @pl.when(kj == n - 1)
    def _():
        d_w_ref[...] = total_ref[...].astype(BF16)


def attend_back(me, qkv, go, full, lse, seg_row, seg_col, h_one, heads, hd):
    n, block, wide = qkv.shape
    dm = h_one.shape[2]
    width = heads * hd

    def whole(shape):
        return pl.BlockSpec(shape, lambda i, me: (0,) * len(shape))

    return pl.pallas_call(
        functools.partial(attend_back_kernel, heads=heads, hd=hd),
        grid_spec=pltpu.PrefetchScalarGridSpec(
            num_scalar_prefetch=1,
            grid=(n,),
            in_specs=[whole(a.shape) for a in (qkv, go, full, lse, seg_row, seg_col)]
            + [pl.BlockSpec((1, block, dm), lambda i, me: (i ^ me[0], 0, 0))],
            out_specs=[pl.BlockSpec((1, block, wide), lambda i, me: (i ^ me[0], 0, 0)), whole((dm, wide))],
            scratch_shapes=[
                pltpu.VMEM((n, width, block), F32),
                pltpu.VMEM((n, 8, block), F32),
                pltpu.VMEM((dm, wide), F32),
                pltpu.VMEM((heads, block, hd), F32),
                pltpu.VMEM((heads, block, hd), F32),
            ],
        ),
        out_shape=[
            jax.ShapeDtypeStruct((n, block, wide), BF16),
            jax.ShapeDtypeStruct((dm, wide), BF16),
        ],
        compiler_params=pltpu.CompilerParams(vmem_limit_bytes=40 * 1024 * 1024),
        cost_estimate=pl.CostEstimate(
            flops=40 * 1000**3, bytes_accessed=12 * 1000**2, transcendentals=8 * 1000**2
        ),
        name="attend_back",
    )(me, qkv, go, full, lse, seg_row, seg_col, h_one)


def normed_parts(value):
    mean = jnp.mean(value, -1, keepdims=True)
    centred = value - mean
    inv_std = lax.rsqrt(jnp.mean(centred * centred, -1, keepdims=True) + EPSILON)
    return centred * inv_std, inv_std


def normalize_back(grad_in, normed, inv_std, gain):
    scaled = grad_in * gain
    return inv_std * (
        scaled
        - jnp.mean(scaled, -1, keepdims=True)
        - normed * jnp.mean(scaled * normed, -1, keepdims=True)
    )


def gelu_and_slope(value):
    cumul = 0.5 * (1.0 + lax.erf(value * (1.0 / math.sqrt(2.0))))
    slope = cumul + value * jnp.exp(-0.5 * value * value) * (1.0 / math.sqrt(2.0 * math.pi))
    return value * cumul, slope


def tie(value, *others):
    return lax.optimization_barrier((value,) + others)[0] if others else value


def swap(value, axis, size, mask):
    return lax.ppermute(value, axis, [(i, i ^ mask) for i in range(size)])


def bits_of(size):
    count = size.bit_length() - 1
    return [1 << b for b in range(count)]


def ordered(parts, index):
    parts = [part[None] for part in parts]
    bit = 1
    while len(parts) > 1:
        on = (index & bit) != 0
        parts = [
            jnp.where(on, jnp.concatenate([b, a], 0), jnp.concatenate([a, b], 0))
            for a, b in zip(parts[::2], parts[1::2])
        ]
        bit *= 2
    return parts[0]


def gathered_ids(masks):
    held, lists = [0], [[0]]
    for mask in masks:
        new = [r ^ mask for r in held]
        lists.append(new)
        held = held + new
    return lists


def settle(parts, index, size, ids, count):
    rows = parts[0].shape[1] // count
    if rows % 16 == 0:
        return parts, ids
    held = sum(ids, [])
    at = jnp.asarray([held.index(r) for r in range(size)])
    whole = jnp.concatenate(parts, 0)[at[jnp.arange(size) ^ index]]
    whole = whole.reshape(size, count, rows, -1).transpose(1, 0, 2, 3)
    return [whole.reshape(1, size * count * rows, -1)], [[None]]


def place(refs, ids, index, count, put):
    for ref, held in zip(refs, ids):
        rows = ref.shape[1] // count
        for j, r in enumerate(held):
            where = slice(None) if r is None else pl.ds(pl.multiple_of((index ^ r) * rows, rows), rows)
            for k in range(count):
                put(k, where, ref[j, k * rows : (k + 1) * rows, :])


def halves(value, index, size, mask):
    value = value.reshape((-1, 2, mask) + value.shape[1:])
    on = ((index & mask) != 0).astype(jnp.int32)
    shape = (-1,) + value.shape[3:]
    keep = lax.dynamic_index_in_dim(value, on, 1, False).reshape(shape)
    return keep, lax.dynamic_index_in_dim(value, 1 - on, 1, False).reshape(shape)


def add_low(a, b, kind=BF16):
    return (a.astype(F32) + b.astype(F32)).astype(kind)


def collect_dp(value, index, size, last=F32, shift=0):
    masks = bits_of(size)
    shape = value.shape[1:]
    value = value.reshape((2,) * len(masks) + shape)
    for step, mask in enumerate(masks):
        axis = len(masks) - 1 - step
        on = ((index & mask) != 0).astype(jnp.int32)
        keep = lax.dynamic_index_in_dim(value, on, axis, False)
        send = lax.dynamic_index_in_dim(value, 1 - on, axis, False)
        got = swap(send, "dp", size << shift, mask << shift)
        value = keep.astype(F32) + got.astype(F32)
        value = value.astype(BF16 if step < len(masks) - 1 else last)
    return value


def collect_pairs(even, odd, size, tied=()):
    got = swap(odd, "seq", size, 1)
    sums = [(even[i].astype(F32) + got[i].astype(F32)).astype(BF16) for i in range(size // 2)]
    mask = 2
    while len(sums) > 2:
        sent = [swap(b, "seq", size, mask) for b in sums[1::2]]
        sums = [(a.astype(F32) + b.astype(F32)).astype(BF16) for a, b in zip(sums[::2], sent)]
        mask *= 2
    return sums[0], sums[1], swap(tie(sums[1], *tied), "seq", size, mask)


def spread_seq(value, size, gate=()):
    got = {0: value}
    for mask in bits_of(size)[::-1]:
        for p in list(got):
            got[p | mask] = swap(tie(got[p], *gate) if p else got[p], "seq", size, mask)
    return [got[p] for p in range(size)]


def trade_seq(pieces, index, size):
    return [
        swap(lax.dynamic_index_in_dim(pieces, index ^ p, 0, False), "seq", size, p)
        if p
        else lax.dynamic_index_in_dim(pieces, index, 0, False)
        for p in range(size)
    ]


def enter_kernel(me_ref, *refs, ids, n, width, cut):
    count = len(ids[0]) + len(ids[1])
    pieces, (x_ref, qkv_ref, h_ref, w_ref, vec_ref, tile_ref, add_ref) = refs[:count], refs[count:]
    me = me_ref[0]

    @pl.when(pl.program_id(0) == 0)
    def _():
        def put_left(k, where, rows):
            w_ref[where, :cut] = rows

        def put_right(k, where, rows):
            w_ref[where, cut:] = rows[:, : 3 * width - cut]
            tile_ref[where, :] = rows[:, 3 * width - cut :].astype(F32)

        place(pieces[: len(ids[0])], ids[0], me_ref[1], 1, put_left)
        place(pieces[len(ids[0]) :], ids[1], me_ref[1], 1, put_right)
        vecs = tile_ref[...].T[:16]
        vec_ref[...] = vecs
        for i, row in ((0, 6), (2, 7)):
            add = vecs[row : row + 1, :width]
            for t in range(1, n):
                add = jnp.where(me == t, vecs[row : row + 1, t * width : (t + 1) * width], add)
            add_ref[0:1, i * width : (i + 1) * width] = add
        add_ref[0:1, width : 2 * width] = jnp.zeros((1, width), F32)

    normed, _ = normed_parts(x_ref[0].astype(F32))
    h = (normed * vec_ref[0:1, :] + vec_ref[1:2, :]).astype(BF16)
    h_ref[0] = h
    qkv_ref[0] = (dot_nn(h, w_ref[...]) + add_ref[0:1, :]).astype(BF16)


def enter(me, pieces, ids, x_all, width):
    n, block, dm = x_all.shape
    cut = pieces[0][0].shape[2]
    pieces = [*pieces[0], *pieces[1]]

    def whole(shape):
        return pl.BlockSpec(shape, lambda i, me: (0,) * len(shape))

    def one(width):
        return pl.BlockSpec((1, block, width), lambda i, me: (i, 0, 0))

    return pl.pallas_call(
        functools.partial(enter_kernel, ids=ids, n=n, width=width, cut=cut),
        grid_spec=pltpu.PrefetchScalarGridSpec(
            num_scalar_prefetch=1,
            grid=(n,),
            in_specs=[whole(a.shape) for a in pieces] + [one(dm)],
            out_specs=[one(3 * width), one(dm), whole((dm, 3 * width)), whole((16, dm))],
            scratch_shapes=[pltpu.VMEM((dm, LANES), F32), pltpu.VMEM((8, 3 * width), F32)],
        ),
        out_shape=[
            jax.ShapeDtypeStruct((n, block, 3 * width), BF16),
            jax.ShapeDtypeStruct((n, block, dm), BF16),
            jax.ShapeDtypeStruct((dm, 3 * width), BF16),
            jax.ShapeDtypeStruct((16, dm), F32),
        ],
        compiler_params=pltpu.CompilerParams(vmem_limit_bytes=40 * 1024 * 1024),
        cost_estimate=pl.CostEstimate(flops=5 * 1000**3, bytes_accessed=8 * 1000**2, transcendentals=0),
        name="enter",
    )(me, *pieces, x_all)


def feed_kernel(me_ref, *refs, n, base, tile, ids):
    got, refs = refs[:n], refs[n:]
    me = me_ref[0]
    i = pl.program_id(0)
    if base:
        pieces, refs = refs[: len(ids)], refs[len(ids) :]
        x_ref, g_ref, vec_ref = refs[:3]
        h_ref, act_ref, gu_ref, low_ref, high_ref, sum_ref, out_w_ref, up_ref, down_ref = refs[3:]
    else:
        x_ref, g_ref, vec_ref, out_w_ref, up_ref, down_ref, sum_in_ref = refs[:7]
        h_ref, act_ref, gu_ref, low_ref, high_ref, sum_ref, x_two_ref = refs[7:]
    part = up_ref.shape[1]
    width = got[0].shape[1]

    @pl.when(i == 0)
    def _():
        if base:
            sum_ref[...] = jnp.zeros_like(sum_ref)

            def put(k, where, rows):
                (out_w_ref, up_ref, down_ref)[k][where, :] = rows

            place(pieces, ids, me_ref[1], 3, put)
        else:
            sum_ref[...] = sum_in_ref[...]

    x_two = x_ref[0].astype(F32) + vec_ref[4:5, :]
    for p in range(n):
        own = pl.ds(pl.multiple_of((me ^ p) * width, width), width)
        x_two = x_two + dot_tn(got[p][0], out_w_ref[own, :])
    if not base:

        @pl.when(i == 0)
        def _():
            x_two_ref[...] = x_two

    normed, _ = normed_parts(x_two)
    h = (normed * vec_ref[2:3, :] + vec_ref[3:4, :]).astype(BF16)
    h_ref[0] = h
    g = g_ref[0]
    total = None
    for t in range(0, part, tile):
        cols = slice(t, t + tile)
        u = dot_nn(h, up_ref[:, cols]) + vec_ref[8:9, cols]
        act, slope = gelu_and_slope(u)
        act_ref[0, :, cols] = act.astype(BF16)
        gu = (dot_nt(g, down_ref[cols, :]) * slope).astype(BF16)
        gu_ref[0, :, cols] = gu
        sum_ref[0:1, cols] += jnp.sum(gu.astype(F32), 0, keepdims=True)
        term = dot_nt(gu, up_ref[:, cols])
        total = term if total is None else total + term
    total = total.astype(BF16)

    @pl.when(i == 0)
    def _():
        low_ref[...] = total

    @pl.when(i == 1)
    def _():
        high_ref[...] = total


def feed(me, got, x_all, g_all, vecs, base, weights, ids=None, held=()):
    n, block, dm = x_all.shape
    part = dm if base else weights[1].shape[1]
    width = got[0].shape[1]

    def whole(shape):
        return pl.BlockSpec(shape, lambda i, me: (0,) * len(shape))

    def one(width):
        return pl.BlockSpec((1, block, width), lambda i, me: (i + base, 0, 0))

    def new(width):
        return pl.BlockSpec((1, block, width), lambda i, me: (i, 0, 0))

    def piece(p):
        return pl.BlockSpec((1, width, block), lambda i, me: ((i + base) ^ p, 0, 0))

    if base:
        part = weights[0].shape[2]
    wide = jax.ShapeDtypeStruct((2, block, dm), BF16)
    hidden = jax.ShapeDtypeStruct((2, block, part), BF16)
    low = jax.ShapeDtypeStruct((block, dm), BF16)
    outs = [wide, hidden, hidden, low, low, jax.ShapeDtypeStruct((8, part), F32)]
    specs = [new(dm), new(part), new(part)] + [whole(o.shape) for o in outs[3:]]
    more = [(dm, dm), (dm, part), (part, dm)] if base else []
    outs += [jax.ShapeDtypeStruct(m, BF16) for m in more] or [jax.ShapeDtypeStruct((block, dm), F32)]
    specs += [whole(o.shape) for o in outs[6:]]
    args = [*got]
    ins = [piece(p) for p in range(n)]
    if base:
        args += [*weights, x_all, g_all, vecs]
        ins += [whole(a.shape) for a in weights] + [one(dm), one(dm), whole(vecs.shape)]
    else:
        args += [x_all, g_all, vecs, *weights, held]
        ins += [one(dm), one(dm)] + [whole(a.shape) for a in (vecs, *weights, held)]
    return pl.pallas_call(
        functools.partial(feed_kernel, n=n, base=base, tile=256 if part % 256 == 0 else part, ids=ids),
        grid_spec=pltpu.PrefetchScalarGridSpec(num_scalar_prefetch=1, grid=(2,), in_specs=ins, out_specs=specs),
        out_shape=outs,
        compiler_params=pltpu.CompilerParams(vmem_limit_bytes=48 * 1024 * 1024),
        cost_estimate=pl.CostEstimate(
            flops=9 * 1000**3, bytes_accessed=16 * 1000**2, transcendentals=3 * 1000**2
        ),
        name="feed_far" if base else "feed_near",
    )(me, *args)


def turn_kernel(me_ref, *refs, n):
    got, refs = refs[:n], refs[n:]
    keep_ref, near_ref, far_ref, x_two_ref, g_ref, out_w_ref, vec_ref = refs[:7]
    gos, (gx_ref, d_out_ref, sum_ref) = refs[7 : 7 + n], refs[7 + n :]
    me = me_ref[0]
    width = got[0].shape[1]
    gh = keep_ref[...].astype(F32) + near_ref[...].astype(F32) + far_ref[...].astype(F32)
    normed, inv_std = normed_parts(x_two_ref[...])
    g = g_ref[...].astype(F32)
    gx = g + normalize_back(gh, normed, inv_std, vec_ref[2:3, :])
    gx_ref[...] = gx
    gb = gx.astype(BF16)
    for p in range(n):
        own = pl.ds(pl.multiple_of((me ^ p) * width, width), width)
        gos[p][...] = dot_nt(out_w_ref[own, :], gb).astype(BF16)
        d_out_ref[own, :] = dot_nn(got[p][0], gb).astype(BF16)
    sum_ref[0:1, :] = jnp.sum(gh * normed, 0, keepdims=True)
    sum_ref[1:2, :] = jnp.sum(gh, 0, keepdims=True)
    sum_ref[2:3, :] = jnp.sum(gb.astype(F32), 0, keepdims=True)
    sum_ref[3:4, :] = jnp.sum(g, 0, keepdims=True)


def turn(me, got, keep, near, far, x_two, g, out_w, vecs):
    n = len(got)
    _, width, block = got[0].shape
    dm = out_w.shape[1]

    def whole(shape):
        return pl.BlockSpec(shape, lambda i, me: (0,) * len(shape))

    def piece(p):
        return pl.BlockSpec((1, width, block), lambda i, me: (p, 0, 0))

    outs = [jax.ShapeDtypeStruct((width, block), BF16)] * n + [
        jax.ShapeDtypeStruct((block, dm), F32),
        jax.ShapeDtypeStruct(out_w.shape, BF16),
        jax.ShapeDtypeStruct((8, dm), F32),
    ]
    return pl.pallas_call(
        functools.partial(turn_kernel, n=n),
        grid_spec=pltpu.PrefetchScalarGridSpec(
            num_scalar_prefetch=1,
            grid=(1,),
            in_specs=[piece(p) for p in range(n)]
            + [whole(a.shape) for a in (keep, near, far, x_two, g, out_w, vecs)],
            out_specs=[whole(o.shape) for o in outs],
        ),
        out_shape=outs,
        compiler_params=pltpu.CompilerParams(vmem_limit_bytes=48 * 1024 * 1024),
        cost_estimate=pl.CostEstimate(flops=3 * 1000**3, bytes_accessed=8 * 1000**2, transcendentals=0),
        name="turn",
    )(me, *got, keep, near, far, x_two, g, out_w, vecs)


def leave_kernel(
    me_ref, x_ref, grad_ref, w_ref, vec_ref, two_ref, up_ref, even_ref, odd_ref, out_ref, sum_ref, add_ref, tile_ref
):
    i = pl.program_id(0)

    @pl.when(i == 0)
    def _():
        sum_ref[...] = jnp.zeros_like(sum_ref)
        add_ref[...] = jnp.zeros_like(add_ref)

    grads = grad_ref[0]
    gh = dot_nt(grads, w_ref[...])
    normed, _ = normed_parts(x_ref[0].astype(F32))
    low = gh.astype(BF16)

    @pl.when(i % 2 == 0)
    def _():
        even_ref[0] = low

    @pl.when(i % 2 == 1)
    def _():
        odd_ref[0] = low

    sum_ref[0:1, :] += jnp.sum(gh * normed, 0, keepdims=True)
    sum_ref[1:2, :] += jnp.sum(gh, 0, keepdims=True)
    add_ref[0:1, :] += jnp.sum(grads.astype(F32), 0, keepdims=True)

    @pl.when(i == pl.num_programs(0) - 1)
    def _():
        width = grads.shape[1] // 3
        dm = w_ref.shape[0]
        rows = [sum_ref[0:2, :], two_ref[0:4, :], jnp.zeros((2, dm), F32), up_ref[0:1, :]]
        rows = jnp.concatenate(rows + [jnp.zeros((LANES - 9, dm), F32)], 0)
        tile_ref[...] = rows.T
        add = jnp.concatenate(
            [
                jnp.zeros((6, width), F32),
                add_ref[0:1, :width],
                add_ref[0:1, 2 * width :],
                jnp.zeros((LANES - 8, width), F32),
            ],
            0,
        )
        own = pl.ds(pl.multiple_of(me_ref[0] * width, width), width)
        tile_ref[own, :] += add.T
        out_ref[...] = tile_ref[...].astype(BF16)


def leave(me, x_all, grads, w, vecs, sums_two, sums_up):
    n, block, wide = grads.shape
    dm = w.shape[0]

    def whole(shape):
        return pl.BlockSpec(shape, lambda i, me: (0,) * len(shape))

    def one(width):
        return pl.BlockSpec((1, block, width), lambda i, me: (i, 0, 0))

    def half(width):
        return pl.BlockSpec((1, block, width), lambda i, me: (i // 2, 0, 0))

    pair = jax.ShapeDtypeStruct((n // 2, block, dm), BF16)
    return pl.pallas_call(
        leave_kernel,
        grid_spec=pltpu.PrefetchScalarGridSpec(
            num_scalar_prefetch=1,
            grid=(n,),
            in_specs=[one(dm), one(wide)] + [whole(a.shape) for a in (w, vecs, sums_two, sums_up)],
            out_specs=[half(dm), half(dm), whole((dm, LANES))],
            scratch_shapes=[
                pltpu.VMEM((8, dm), F32),
                pltpu.VMEM((8, wide), F32),
                pltpu.VMEM((dm, LANES), F32),
            ],
        ),
        out_shape=[
            pair,
            pair,
            jax.ShapeDtypeStruct((dm, LANES), BF16),
        ],
        compiler_params=pltpu.CompilerParams(vmem_limit_bytes=48 * 1024 * 1024),
        cost_estimate=pl.CostEstimate(flops=6 * 1000**3, bytes_accessed=10 * 1000**2, transcendentals=0),
        name="leave",
    )(me, x_all, grads, w, vecs, sums_two, sums_up)


def hand_over_kernel(me_ref, *refs, n, rows, first):
    blob_a, blob_b, feed_a, feed_b = refs[:4]
    pieces, (out_ref, down_ref, last_ref) = refs[4 : 4 + n], refs[4 + n :]
    size = n * rows
    blob = blob_a[...].astype(F32) + blob_b[...].astype(F32)
    feed = feed_a[...].astype(F32) + feed_b[...].astype(F32)
    out_ref[...] = blob[size:]
    down_ref[...] = feed[size:]
    last_ref[...] = blob[:size, first - LANES : first]
    both = jnp.concatenate([blob[:size, :first], feed[:size]], 1)
    parts = [both[t * rows : (t + 1) * rows] for t in range(n)]
    for p, ref in enumerate(pieces):
        chosen = parts[0]
        for t in range(1, n):
            chosen = jnp.where((me_ref[0] ^ p) == t, parts[t], chosen)
        ref[...] = chosen.astype(BF16)


def hand_over(me, blob, feeds, rows, n, first):
    dm = blob[0].shape[1]
    part = feeds[0].shape[1]
    size = n * rows
    vmem = pl.BlockSpec(memory_space=pltpu.VMEM)
    *pieces, out, down, last = pl.pallas_call(
        functools.partial(hand_over_kernel, n=n, rows=rows, first=first),
        in_specs=[pl.BlockSpec(memory_space=pltpu.SMEM)] + [vmem] * 4,
        out_specs=[vmem] * (n + 3),
        out_shape=[jax.ShapeDtypeStruct((rows, first + part), BF16)] * n
        + [
            jax.ShapeDtypeStruct((rows, dm), F32),
            jax.ShapeDtypeStruct((feeds[0].shape[0] - size, part), F32),
            jax.ShapeDtypeStruct((size, LANES), F32),
        ],
        name="hand_over",
    )(me, *blob, *feeds)
    return pieces, out, down, last


def finish_kernel(me_ref, *refs, n, width, nd):
    pieces, (q_ref, k_ref, v_ref, vec_ref, up_ref) = refs[:n], refs[n:]
    first = 3 * width + LANES
    pieces = [p[...].astype(F32) for p in pieces]
    vec_ref[...] = sum(p[:, 3 * width : first] for p in pieces)
    bit = 1
    while bit < n:
        on = (me_ref[0] & bit) != 0
        for p in range(n):
            if not p & bit:
                a, b = pieces[p], pieces[p | bit]
                pieces[p] = jnp.where(on, b, a)
                pieces[p | bit] = jnp.where(on, a, b)
        bit *= 2
    step = (pieces[0].shape[1] - first) // nd
    for t in range(n):
        for i, ref in enumerate((q_ref, k_ref, v_ref)):
            ref[:, t * width : (t + 1) * width] = pieces[t][:, i * width : (i + 1) * width]
        for j in range(nd):
            to = (j * n + t) * step
            up_ref[:, to : to + step] = pieces[t][:, first + j * step : first + (j + 1) * step]


def finish(me, pieces, width, nd):
    n = len(pieces)
    rows, wide = pieces[0].shape
    weight = jax.ShapeDtypeStruct((rows, n * width), F32)
    tile = jax.ShapeDtypeStruct((rows, LANES), F32)
    vmem = pl.BlockSpec(memory_space=pltpu.VMEM)
    return pl.pallas_call(
        functools.partial(finish_kernel, n=n, width=width, nd=nd),
        in_specs=[pl.BlockSpec(memory_space=pltpu.SMEM)] + [vmem] * n,
        out_specs=[vmem] * 5,
        out_shape=[weight] * 3 + [tile, jax.ShapeDtypeStruct((rows, n * (wide - 3 * width - LANES)), F32)],
        name="finish",
    )(me, *pieces)


def body(
    nd,
    ns,
    tokens,
    cotangent,
    segments,
    w_query,
    w_key,
    w_value,
    w_out,
    w_up,
    w_down,
    ln1_gain,
    ln1_shift,
    query_bias,
    value_bias,
    out_bias,
    ln2_gain,
    ln2_shift,
    up_bias,
    down_bias,
):
    d = lax.axis_index("dp")
    s = lax.axis_index("seq")
    me = s.astype(jnp.int32).reshape(1)
    _, block, dm = tokens.shape
    hd = dm // H
    heads = H // ns
    width = heads * hd
    rows = w_query.shape[0]
    ff_rows, ff = w_down.shape[0], w_up.shape[1]
    ratio = ff_rows // rows
    part = ff // ns
    pad = 16

    me = jnp.stack([s, d]).astype(jnp.int32)
    masks = bits_of(nd)[::-1]
    far = bits_of(ns)[-1]
    x_own = tokens.reshape(block, dm)
    g = cotangent.reshape(block, dm)
    x_far = swap(x_own, "seq", ns, far)

    cols = [w.reshape(rows, ns, width) for w in (w_query, w_key, w_value)]
    vec = jnp.stack([ln1_gain, ln1_shift, ln2_gain, ln2_shift, out_bias, down_bias, query_bias, value_bias], 1)
    vec = jnp.pad(vec, ((0, 0), (0, LANES - vec.shape[1])))
    up_cols = w_up.reshape(rows, nd, ns, ff_rows).transpose(0, 2, 1, 3).reshape(rows, ns, part)
    lanes = LANES * -(-block // (rows * LANES))
    seg = jnp.pad(segments.reshape(block).astype(BF16), (0, rows * lanes - block)).reshape(rows, lanes)
    same = jnp.concatenate([vec, w_out, seg], 1)
    same = jnp.broadcast_to(same[:, None], (rows, ns, same.shape[1]))
    pieces = jnp.concatenate(cols + [same, up_cols], 2).transpose(1, 0, 2)
    first = 3 * width + LANES
    size = ns * rows
    pieces = trade_seq(pieces, s, ns)
    start = first + dm
    segs = jnp.stack([p[:, start : start + lanes].reshape(-1)[:block] for p in pieces]).astype(jnp.int32)
    seg_row = segs.reshape(ns, 1, block)
    seg_col = segs.reshape(ns, block, 1)
    pieces = ordered(pieces, s).reshape(size, -1)
    lane = lax.broadcasted_iota(jnp.int32, (size, first), 1)
    one = jnp.where(lane == 3 * width + 8, jnp.pad(up_bias, (0, size - ff_rows))[:, None], pieces[:, :first])
    two = jnp.concatenate([pieces[:, first:start], pieces[:, start + lanes :], w_down], 0)

    turned = masks[:-2] + masks[:-3:-1]
    ones = [one[None]]
    for mask in masks[:-2]:
        ones.append(swap(jnp.concatenate(ones, 0), "dp", nd, mask))
    ones = jnp.concatenate(ones, 0)
    cut = -(-(first // 2) // LANES) * LANES
    ones = [ones[:, :, :cut]], [ones[:, :, cut:]]
    ones[0][0], ones[1][0], two, seg_row, seg_col = lax.optimization_barrier(
        (ones[0][0], ones[1][0], two, seg_row, seg_col)
    )
    for parts, order in zip(ones, (masks, turned)):
        parts.append(swap(parts[0], "dp", nd, order[-2]))
    ones[0][1], ones[1][1], x_far = lax.optimization_barrier((ones[0][1], ones[1][1], x_far))
    g_far = swap(tie(g, x_far), "seq", ns, far)
    last = [jnp.concatenate(parts, 0) for parts in ones]
    twos = [tie(two, *last)[None]]
    for parts, held, order in zip(ones, last, (masks, turned)):
        parts.append(swap(held, "dp", nd, order[-1]))

    for mask in masks[:-2]:
        twos.append(swap(jnp.concatenate(twos, 0), "dp", nd, mask))
    parts = {0: x_own, far: x_far}
    for mask in bits_of(ns)[-2::-1]:
        for p in list(parts):
            parts[p | mask] = swap(parts[p], "seq", ns, mask)
    x_all = jnp.stack([parts[p] for p in range(ns)])

    ids = [gathered_ids(order) for order in (masks, turned)]
    ids = [[sum(i[:-2], [])] + i[-2:] for i in ids]
    ones, ids = zip(*[settle(p, d, nd, i, 1) for p, i in zip(ones, ids)])
    ones, x_all = lax.optimization_barrier((ones, x_all))
    qkv, h_one, w_qkv, vecs = enter(me, ones, ids, x_all, width)
    qkv, h_one, w_qkv, vecs, g_far, twos = lax.optimization_barrier((qkv, h_one, w_qkv, vecs, g_far, twos))
    two = jnp.concatenate(twos, 0)
    twos = [two] + [swap(two, "dp", nd, p) for p in (1, 2)]

    g_parts = {0: g, far: g_far}
    for mask in bits_of(ns)[-2::-1]:
        for p in list(g_parts):
            g_parts[p | mask] = swap(g_parts[p], "seq", ns, mask)
    qkv, two = lax.optimization_barrier((qkv, two))
    o_low, o_full, lse = attend(me, qkv, seg_row, seg_col, heads, hd)
    o_low, o_full, lse, twos[1:], *g_last = lax.optimization_barrier(
        (o_low, o_full, lse, twos[1:], g_parts[1], g_parts[ns - 1])
    )
    g_all = jnp.stack([g, g_last[0], g_far, g_last[1]])
    o_got = spread_seq(o_low, ns, (g_all,))
    twos.append(swap(tie(two, o_low), "dp", nd, 3))
    ids = sum(gathered_ids(masks[:-2]), [])
    twos, ids = settle(twos, d, nd, [[r ^ p for r in ids] for p in range(4)], 3)
    far_h, far_act, far_gu, gh_two, gh_three, sums_up, *weights = feed(
        me, o_got, x_all, g_all, vecs, 2, twos, ids
    )
    w_out_all, _, w_down_own = weights

    def over_rows(a, b):
        return jnp.einsum("nbk,nbc->kc", a, b, preferred_element_type=F32)

    d_down = over_rows(far_act, g_all[2:])
    sent = add_low(gh_two, swap(gh_three, "seq", ns, 1))
    far_got = swap(sent, "seq", ns, 2)
    sums_up, sent, d_down = lax.optimization_barrier((sums_up, sent, d_down))
    h_two, act, gu, gh_zero, gh_one, sums_up, x_two = feed(
        me, o_got, x_all, g_all, vecs, 0, weights, None, sums_up
    )
    near_got = swap(gh_one, "seq", ns, 1)
    d_down = (d_down + over_rows(act, g_all[:2])).astype(BF16)
    d_up = (over_rows(far_h, far_gu) + over_rows(h_two, gu)).astype(BF16)
    up_keep, up_sent = halves(d_up.reshape(nd, size, part), d, nd, 1)
    down_keep, down_sent = halves(d_down.reshape(nd, ff_rows, dm), d, nd, 2)
    up_got, down_got = swap(up_sent, "dp", nd, 1), swap(down_sent, "dp", nd, 2)
    far_got, up_sent, down_sent = lax.optimization_barrier((far_got, up_sent, down_sent))
    *gos, gx_two, d_out, sums_two = turn(me, o_got, gh_zero, near_got, far_got, x_two, g, w_out_all, vecs)
    go_got = [gos[0]] + [swap(gos[p], "seq", ns, p) for p in range(1, ns)]
    go_got[1], d_out, sums_two = lax.optimization_barrier((go_got[1], d_out, sums_two))
    act, far_act = lax.optimization_barrier((act, far_act, go_got[1]))[:2]
    out_parts = [dot_nn(a, w_down_own).astype(BF16) for a in (act[0], act[1], far_act[0], far_act[1])]
    up_got, down_got = lax.optimization_barrier((up_got, down_got, out_parts))[:2]
    out_sent = add_low(out_parts[2], swap(out_parts[3], "seq", ns, 1))
    out_near = swap(out_parts[1], "seq", ns, 1)
    out_far = swap(tie(out_sent, go_got[-1]), "seq", ns, 2)
    outs_keep, outs_sent = halves(d_out.reshape(nd * ns, rows, dm), s, ns, 1)
    outs_got = swap(outs_sent, "seq", ns, 1)
    outs_keep, outs_sent = halves(add_low(outs_keep, outs_got), s >> 1, ns // 2, 1)
    outs_got = swap(outs_sent, "seq", ns, 2)

    up_keep, up_sent = halves(add_low(up_keep, up_got), d >> 1, nd // 2, 1)
    down_keep, down_sent = halves(add_low(down_keep, down_got), d, nd, 1)
    up_got, down_got = swap(up_sent, "dp", nd, 2), swap(down_sent, "dp", nd, 1)
    go_all = jnp.stack(go_got)
    go_all, *_ = lax.optimization_barrier((go_all, out_sent, out_parts, outs_sent, up_sent, down_sent))
    grads, d_qkv = attend_back(me, qkv, go_all, o_full, lse, seg_row, seg_col, h_one, heads, hd)
    grads, d_qkv, out_near, out_far, outs_got, up_got, down_got = lax.optimization_barrier(
        (grads, d_qkv, out_near, out_far, outs_got, up_got, down_got)
    )
    blob = jnp.concatenate(
        [
            jnp.pad(d_qkv.reshape(nd, size, 3 * width), ((0, 0), (0, 0), (0, dm - 3 * width))),
            add_low(outs_keep, outs_got),
        ],
        1,
    )
    blob_keep, blob_sent = halves(blob, d, nd, 1)
    blob_got = swap(blob_sent, "dp", nd, 1)
    feeds = jnp.concatenate([add_low(up_keep, up_got), add_low(down_keep, down_got)], 1)
    feed_keep, feed_sent = halves(feeds, d >> 2, nd // 4, 1)
    feed_got = swap(feed_sent, "dp", nd, 4)
    grads = lax.optimization_barrier((grads, blob_sent, feed_sent))[0]
    even, odd, tile = leave(me, x_all, grads, w_qkv, vecs, sums_two, sums_up)
    even, odd, tile, blob_got, feed_got = lax.optimization_barrier((even, odd, tile, blob_got, feed_got))
    tile = tile.reshape(nd // 4, 4, size, LANES)
    tiles = [lax.dynamic_index_in_dim(tile, (d & 3) ^ p, 1, False) for p in range(4)]
    tiles = [jnp.pad(t, ((0, 0), (0, rows), (3 * width, dm - first))) for t in tiles[::2]] + tiles[1::2]
    blob_keep, blob_sent = halves(add_low(blob_keep, blob_got), d >> 1, nd // 2, 1)
    blob_keep, blob_sent = blob_keep + tiles[0], blob_sent + tiles[1]
    blob_got = swap(blob_sent, "dp", nd, 2)
    tiles = [swap(t, "dp", nd, p) for t, p in zip(tie(tiles[2:], blob_sent), (1, 3))]
    keep, sent, got = collect_pairs(even, odd, ns)
    blob_got, sent, tiles = lax.optimization_barrier((blob_got, sent, tiles))
    tile = jnp.pad(tiles[0].astype(F32) + tiles[1].astype(F32), ((0, 0), (0, rows), (3 * width, dm - first)))
    blob = (blob_keep.astype(F32) + blob_got.astype(F32) + tile).astype(BF16)
    blob_keep, blob_sent = halves(blob, d >> 2, nd // 4, 1)
    blob_got = swap(blob_sent, "dp", nd, 4)
    blob_got, sent = lax.optimization_barrier((blob_got, sent))
    if nd > 8:
        rest = [(blob_keep, blob_got), (feed_keep, feed_got)]
        rest = [collect_dp(add_low(a, b), d >> 3, nd // 8, BF16, shift=3) for a, b in rest]
        rest = [(v, jnp.zeros_like(v)) for v in rest]
    else:
        rest = [(blob_keep[0], blob_got[0]), (feed_keep[0], feed_got[0])]
    pieces, sum_out, sum_down, last = hand_over(me, *rest, rows, ns, first)
    out = out_parts[0].astype(F32) + out_near.astype(F32) + out_far.astype(F32) + x_two + vecs[5:6]
    trades = [pieces[0]] + [swap(pieces[p], "seq", ns, p) for p in range(1, ns)]
    gh_one = keep.astype(F32) + got.astype(F32)
    n_own, inv_own = normed_parts(tie(x_own, pieces[0]).astype(F32))
    grad_x = gx_two + normalize_back(gh_one, n_own, inv_own, vecs[0:1])
    trades, grad_x, out, last = lax.optimization_barrier((trades, grad_x, out, last))
    sum_q, sum_k, sum_v, vec_sum, sum_up = finish(me, trades, width, nd)
    vec_sum = vec_sum.T
    sum_up_bias = last[:ff_rows, 8]
    v = [vec_sum[i] for i in range(8)]
    return (
        out.reshape(1, block, dm),
        grad_x.reshape(1, block, dm),
        sum_q,
        sum_k,
        sum_v,
        sum_out,
        sum_up,
        sum_down,
        v[0],
        v[1],
        v[6],
        v[7],
        v[4],
        v[2],
        v[3],
        sum_up_bias,
        v[5],
    )


def solution(mesh):
    act = P("dp", "seq", None)
    weight = P(("dp", "seq"), None)
    vector = P(("dp", "seq"))
    return jax.shard_map(
        functools.partial(body, mesh.shape["dp"], mesh.shape["seq"]),
        mesh=mesh,
        in_specs=(act, act, P("dp", "seq")) + (weight,) * 6 + (vector,) * 9,
        out_specs=(act, act) + (weight,) * 6 + (vector,) * 9,
        check_vma=False,
    )
```

```python
import functools
import math

import jax
import jax.numpy as jnp
from jax import lax
from jax.experimental import pallas as pl
from jax.experimental.pallas import tpu as pltpu
from jax.sharding import PartitionSpec as P

H = 12
EPSILON = 1e-05
MASKED = -1e30
F32 = jnp.float32
BF16 = jnp.bfloat16
LANES = 128


def dot_nt(a, b):
    return lax.dot_general(a, b, (((1,), (1,)), ((), ())), preferred_element_type=F32)


def dot_tn(a, b):
    return lax.dot_general(a, b, (((0,), (0,)), ((), ())), preferred_element_type=F32)


def dot_nn(a, b):
    return jnp.dot(a, b, preferred_element_type=F32)


def attend_kernel(me_ref, qkv_ref, seg_row_ref, seg_col_ref, low_ref, full_ref, lse_ref, *, heads, hd):
    me = me_ref[0]
    qi = pl.program_id(0)
    rq = qi ^ me
    block = qkv_ref.shape[1]
    width = heads * hd
    scale = jnp.asarray(1.0 / math.sqrt(hd), BF16)
    queries = [qkv_ref[rq, :, h * hd : (h + 1) * hd] * scale for h in range(heads)]
    seg_q = seg_row_ref[rq]

    def step(rk, state, causal):
        allowed = seg_col_ref[rk] == seg_q
        if causal:
            k_pos = lax.broadcasted_iota(jnp.int32, (block, block), 0)
            q_pos = lax.broadcasted_iota(jnp.int32, (block, block), 1)
            allowed = allowed & (k_pos <= q_pos)
        new = []
        for h in range(heads):
            top, total, mixed = state[h]
            key = qkv_ref[rk, :, width + h * hd : width + (h + 1) * hd]
            value = qkv_ref[rk, :, 2 * width + h * hd : 2 * width + (h + 1) * hd]
            scores = jnp.where(allowed, dot_nt(key, queries[h]), MASKED)
            higher = jnp.maximum(top, jnp.max(scores, 0, keepdims=True))
            weights = jnp.exp(scores - higher)
            fade = jnp.exp(top - higher)
            total = total * fade + jnp.sum(weights, 0, keepdims=True)
            mixed = mixed * fade + dot_tn(value, weights.astype(BF16))
            new.append((higher, total, mixed))
        return tuple(new)

    start = tuple(
        (jnp.full((1, block), MASKED, F32), jnp.zeros((1, block), F32), jnp.zeros((hd, block), F32))
        for _ in range(heads)
    )
    state = lax.fori_loop(0, qi, lambda kj, c: step(kj ^ me, c, False), start)
    state = step(rq, state, True)
    rows = []
    for h in range(heads):
        top, total, mixed = state[h]
        rows.append(mixed / total)
        lse_ref[0, h : h + 1, :] = top + jnp.log(total)
    full = jnp.concatenate(rows, 0)
    full_ref[0] = full
    low_ref[0] = full.astype(BF16)


def attend(me, qkv, seg_row, seg_col, heads, hd):
    n, block, _ = qkv.shape
    width = heads * hd

    def whole(shape):
        return pl.BlockSpec(shape, lambda i, me: (0,) * len(shape))

    def own(shape):
        return pl.BlockSpec(shape, lambda i, me: (i ^ me[0], 0, 0))

    return pl.pallas_call(
        functools.partial(attend_kernel, heads=heads, hd=hd),
        grid_spec=pltpu.PrefetchScalarGridSpec(
            num_scalar_prefetch=1,
            grid=(n,),
            in_specs=[whole(qkv.shape), whole(seg_row.shape), whole(seg_col.shape)],
            out_specs=[own((1, width, block)), own((1, width, block)), own((1, 8, block))],
        ),
        out_shape=[
            jax.ShapeDtypeStruct((n, width, block), BF16),
            jax.ShapeDtypeStruct((n, width, block), F32),
            jax.ShapeDtypeStruct((n, 8, block), F32),
        ],
        compiler_params=pltpu.CompilerParams(vmem_limit_bytes=40 * 1024 * 1024),
        cost_estimate=pl.CostEstimate(
            flops=20 * 1000**3, bytes_accessed=8 * 1000**2, transcendentals=8 * 1000**2
        ),
        name="attend",
    )(me, qkv, seg_row, seg_col)


def attend_back_kernel(
    me_ref, qkv_ref, go_ref, full_ref, lse_ref, seg_row_ref, seg_col_ref, h_ref, grad_ref, d_w_ref,
    gq_ref, dot_ref, total_ref, gk_ref, gv_ref, *, heads, hd
):
    me = me_ref[0]
    kj = pl.program_id(0)
    rk = kj ^ me
    n, block, _ = qkv_ref.shape
    width = heads * hd
    scale = 1.0 / math.sqrt(hd)
    low_scale = jnp.asarray(scale, BF16)

    @pl.when(kj == 0)
    def _():
        gq_ref[...] = jnp.zeros_like(gq_ref)
        total_ref[...] = jnp.zeros_like(total_ref)
        for b in range(n):
            prod = go_ref[b].astype(F32) * full_ref[b]
            for h in range(heads):
                dot_ref[b, h : h + 1, :] = jnp.sum(prod[h * hd : (h + 1) * hd], 0, keepdims=True)

    def step(rq, causal):
        for k0 in range(0, block, 512):
            for q0 in range(0, block, 256):
                if causal and q0 + 256 <= k0:
                    continue
                rows, cols = slice(k0, k0 + 512), slice(q0, q0 + 256)
                allowed = seg_col_ref[rk, rows, :] == seg_row_ref[rq][:, cols]
                if causal and q0 < k0 + 512:
                    k_pos = lax.broadcasted_iota(jnp.int32, (512, 256), 0) + k0
                    q_pos = lax.broadcasted_iota(jnp.int32, (512, 256), 1) + q0
                    allowed = allowed & (k_pos <= q_pos)
                for h in range(heads):
                    head = slice(h * hd, (h + 1) * hd)
                    query = qkv_ref[rq, cols, head] * low_scale
                    key = qkv_ref[rk, rows, width + h * hd : width + (h + 1) * hd]
                    value = qkv_ref[rk, rows, 2 * width + h * hd : 2 * width + (h + 1) * hd]
                    go = go_ref[rq, head, cols]
                    scores = jnp.where(allowed, dot_nt(key, query), MASKED)
                    weights = jnp.exp(scores - lse_ref[rq, h : h + 1, cols])
                    gw = dot_nn(value, go)
                    ds = (weights * (gw - dot_ref[rq, h : h + 1, cols])).astype(BF16)
                    gv = dot_nt(weights.astype(BF16), go)
                    gk = dot_nn(ds, query)
                    if causal and q0 <= k0:
                        gv_ref[h, rows, :] = gv
                        gk_ref[h, rows, :] = gk
                    else:
                        gv_ref[h, rows, :] += gv
                        gk_ref[h, rows, :] += gk
                    gq_ref[rq, head, cols] += dot_tn(key, ds)

    step(rk, True)

    @pl.loop(kj + 1, n)
    def _(qi):
        step(qi ^ me, False)

    grad_ref[0, :, :width] = (gq_ref[rk] * scale).T.astype(BF16)
    for h in range(heads):
        gk, gv = gk_ref[h], gv_ref[h]
        grad_ref[0, :, width + h * hd : width + (h + 1) * hd] = gk.astype(BF16)
        grad_ref[0, :, 2 * width + h * hd : 2 * width + (h + 1) * hd] = gv.astype(BF16)
    total_ref[...] += dot_tn(h_ref[0], grad_ref[0])

    @pl.when(kj == n - 1)
    def _():
        d_w_ref[...] = total_ref[...].astype(BF16)


def attend_back(me, qkv, go, full, lse, seg_row, seg_col, h_one, heads, hd):
    n, block, wide = qkv.shape
    dm = h_one.shape[2]
    width = heads * hd

    def whole(shape):
        return pl.BlockSpec(shape, lambda i, me: (0,) * len(shape))

    return pl.pallas_call(
        functools.partial(attend_back_kernel, heads=heads, hd=hd),
        grid_spec=pltpu.PrefetchScalarGridSpec(
            num_scalar_prefetch=1,
            grid=(n,),
            in_specs=[whole(a.shape) for a in (qkv, go, full, lse, seg_row, seg_col)]
            + [pl.BlockSpec((1, block, dm), lambda i, me: (i ^ me[0], 0, 0))],
            out_specs=[pl.BlockSpec((1, block, wide), lambda i, me: (i ^ me[0], 0, 0)), whole((dm, wide))],
            scratch_shapes=[
                pltpu.VMEM((n, width, block), F32),
                pltpu.VMEM((n, 8, block), F32),
                pltpu.VMEM((dm, wide), F32),
                pltpu.VMEM((heads, block, hd), F32),
                pltpu.VMEM((heads, block, hd), F32),
            ],
        ),
        out_shape=[
            jax.ShapeDtypeStruct((n, block, wide), BF16),
            jax.ShapeDtypeStruct((dm, wide), BF16),
        ],
        compiler_params=pltpu.CompilerParams(vmem_limit_bytes=40 * 1024 * 1024),
        cost_estimate=pl.CostEstimate(
            flops=40 * 1000**3, bytes_accessed=12 * 1000**2, transcendentals=8 * 1000**2
        ),
        name="attend_back",
    )(me, qkv, go, full, lse, seg_row, seg_col, h_one)


def normed_parts(value):
    mean = jnp.mean(value, -1, keepdims=True)
    centred = value - mean
    inv_std = lax.rsqrt(jnp.mean(centred * centred, -1, keepdims=True) + EPSILON)
    return centred * inv_std, inv_std


def normalize_back(grad_in, normed, inv_std, gain):
    scaled = grad_in * gain
    return inv_std * (
        scaled
        - jnp.mean(scaled, -1, keepdims=True)
        - normed * jnp.mean(scaled * normed, -1, keepdims=True)
    )


def gelu_and_slope(value):
    cumul = 0.5 * (1.0 + lax.erf(value * (1.0 / math.sqrt(2.0))))
    slope = cumul + value * jnp.exp(-0.5 * value * value) * (1.0 / math.sqrt(2.0 * math.pi))
    return value * cumul, slope


def tie(value, *others):
    return lax.optimization_barrier((value,) + others)[0] if others else value


def swap(value, axis, size, mask):
    return lax.ppermute(value, axis, [(i, i ^ mask) for i in range(size)])


def bits_of(size):
    count = size.bit_length() - 1
    return [1 << b for b in range(count)]


def ordered(parts, index):
    parts = [part[None] for part in parts]
    bit = 1
    while len(parts) > 1:
        on = (index & bit) != 0
        parts = [
            jnp.where(on, jnp.concatenate([b, a], 0), jnp.concatenate([a, b], 0))
            for a, b in zip(parts[::2], parts[1::2])
        ]
        bit *= 2
    return parts[0]


def gathered_ids(masks):
    held, lists = [0], [[0]]
    for mask in masks:
        new = [r ^ mask for r in held]
        lists.append(new)
        held = held + new
    return lists


def settle(parts, index, size, ids, count):
    rows = parts[0].shape[1] // count
    if rows % 16 == 0:
        return parts, ids
    held = sum(ids, [])
    at = jnp.asarray([held.index(r) for r in range(size)])
    whole = jnp.concatenate(parts, 0)[at[jnp.arange(size) ^ index]]
    whole = whole.reshape(size, count, rows, -1).transpose(1, 0, 2, 3)
    return [whole.reshape(1, size * count * rows, -1)], [[None]]


def place(refs, ids, index, count, put):
    for ref, held in zip(refs, ids):
        rows = ref.shape[1] // count
        for j, r in enumerate(held):
            where = slice(None) if r is None else pl.ds(pl.multiple_of((index ^ r) * rows, rows), rows)
            for k in range(count):
                put(k, where, ref[j, k * rows : (k + 1) * rows, :])


def halves(value, index, size, mask):
    value = value.reshape((-1, 2, mask) + value.shape[1:])
    on = ((index & mask) != 0).astype(jnp.int32)
    shape = (-1,) + value.shape[3:]
    keep = lax.dynamic_index_in_dim(value, on, 1, False).reshape(shape)
    return keep, lax.dynamic_index_in_dim(value, 1 - on, 1, False).reshape(shape)


def add_low(a, b, kind=BF16):
    return (a.astype(F32) + b.astype(F32)).astype(kind)


def collect_dp(value, index, size, last=F32, shift=0):
    masks = bits_of(size)
    shape = value.shape[1:]
    value = value.reshape((2,) * len(masks) + shape)
    for step, mask in enumerate(masks):
        axis = len(masks) - 1 - step
        on = ((index & mask) != 0).astype(jnp.int32)
        keep = lax.dynamic_index_in_dim(value, on, axis, False)
        send = lax.dynamic_index_in_dim(value, 1 - on, axis, False)
        got = swap(send, "dp", size << shift, mask << shift)
        value = keep.astype(F32) + got.astype(F32)
        value = value.astype(BF16 if step < len(masks) - 1 else last)
    return value


def collect_pairs(even, odd, size, tied=()):
    got = swap(odd, "seq", size, 1)
    sums = [(even[i].astype(F32) + got[i].astype(F32)).astype(BF16) for i in range(size // 2)]
    mask = 2
    while len(sums) > 2:
        sent = [swap(b, "seq", size, mask) for b in sums[1::2]]
        sums = [(a.astype(F32) + b.astype(F32)).astype(BF16) for a, b in zip(sums[::2], sent)]
        mask *= 2
    return sums[0], sums[1], swap(tie(sums[1], *tied), "seq", size, mask)


def spread_seq(value, size, gate=()):
    got = {0: value}
    for mask in bits_of(size)[::-1]:
        for p in list(got):
            got[p | mask] = swap(tie(got[p], *gate) if p else got[p], "seq", size, mask)
    return [got[p] for p in range(size)]


def trade_seq(pieces, index, size):
    return [
        swap(lax.dynamic_index_in_dim(pieces, index ^ p, 0, False), "seq", size, p)
        if p
        else lax.dynamic_index_in_dim(pieces, index, 0, False)
        for p in range(size)
    ]


def enter_kernel(me_ref, *refs, ids, n, width, cut):
    count = len(ids[0]) + len(ids[1])
    pieces, (x_ref, qkv_ref, h_ref, w_ref, vec_ref, tile_ref, add_ref) = refs[:count], refs[count:]
    me = me_ref[0]

    @pl.when(pl.program_id(0) == 0)
    def _():
        def put_left(k, where, rows):
            w_ref[where, :cut] = rows

        def put_right(k, where, rows):
            w_ref[where, cut:] = rows[:, : 3 * width - cut]
            tile_ref[where, :] = rows[:, 3 * width - cut :].astype(F32)

        place(pieces[: len(ids[0])], ids[0], me_ref[1], 1, put_left)
        place(pieces[len(ids[0]) :], ids[1], me_ref[1], 1, put_right)
        vecs = tile_ref[...].T[:16]
        vec_ref[...] = vecs
        for i, row in ((0, 6), (2, 7)):
            add = vecs[row : row + 1, :width]
            for t in range(1, n):
                add = jnp.where(me == t, vecs[row : row + 1, t * width : (t + 1) * width], add)
            add_ref[0:1, i * width : (i + 1) * width] = add
        add_ref[0:1, width : 2 * width] = jnp.zeros((1, width), F32)

    normed, _ = normed_parts(x_ref[0].astype(F32))
    h = (normed * vec_ref[0:1, :] + vec_ref[1:2, :]).astype(BF16)
    h_ref[0] = h
    qkv_ref[0] = (dot_nn(h, w_ref[...]) + add_ref[0:1, :]).astype(BF16)


def enter(me, pieces, ids, x_all, width):
    n, block, dm = x_all.shape
    cut = pieces[0][0].shape[2]
    pieces = [*pieces[0], *pieces[1]]

    def whole(shape):
        return pl.BlockSpec(shape, lambda i, me: (0,) * len(shape))

    def one(width):
        return pl.BlockSpec((1, block, width), lambda i, me: (i, 0, 0))

    return pl.pallas_call(
        functools.partial(enter_kernel, ids=ids, n=n, width=width, cut=cut),
        grid_spec=pltpu.PrefetchScalarGridSpec(
            num_scalar_prefetch=1,
            grid=(n,),
            in_specs=[whole(a.shape) for a in pieces] + [one(dm)],
            out_specs=[one(3 * width), one(dm), whole((dm, 3 * width)), whole((16, dm))],
            scratch_shapes=[pltpu.VMEM((dm, LANES), F32), pltpu.VMEM((8, 3 * width), F32)],
        ),
        out_shape=[
            jax.ShapeDtypeStruct((n, block, 3 * width), BF16),
            jax.ShapeDtypeStruct((n, block, dm), BF16),
            jax.ShapeDtypeStruct((dm, 3 * width), BF16),
            jax.ShapeDtypeStruct((16, dm), F32),
        ],
        compiler_params=pltpu.CompilerParams(vmem_limit_bytes=40 * 1024 * 1024),
        cost_estimate=pl.CostEstimate(flops=5 * 1000**3, bytes_accessed=8 * 1000**2, transcendentals=0),
        name="enter",
    )(me, *pieces, x_all)


def feed_kernel(me_ref, *refs, n, base, tile, ids):
    got, refs = refs[:n], refs[n:]
    me = me_ref[0]
    i = pl.program_id(0)
    if base:
        pieces, refs = refs[: len(ids)], refs[len(ids) :]
        x_ref, g_ref, vec_ref = refs[:3]
        h_ref, act_ref, gu_ref, low_ref, high_ref, sum_ref, out_w_ref, up_ref, down_ref = refs[3:]
    else:
        x_ref, g_ref, vec_ref, out_w_ref, up_ref, down_ref, sum_in_ref = refs[:7]
        h_ref, act_ref, gu_ref, low_ref, high_ref, sum_ref, x_two_ref = refs[7:]
    part = up_ref.shape[1]
    width = got[0].shape[1]

    @pl.when(i == 0)
    def _():
        if base:
            sum_ref[...] = jnp.zeros_like(sum_ref)

            def put(k, where, rows):
                (out_w_ref, up_ref, down_ref)[k][where, :] = rows

            place(pieces, ids, me_ref[1], 3, put)
        else:
            sum_ref[...] = sum_in_ref[...]

    x_two = x_ref[0].astype(F32) + vec_ref[4:5, :]
    for p in range(n):
        own = pl.ds(pl.multiple_of((me ^ p) * width, width), width)
        x_two = x_two + dot_tn(got[p][0], out_w_ref[own, :])
    if not base:

        @pl.when(i == 0)
        def _():
            x_two_ref[...] = x_two

    normed, _ = normed_parts(x_two)
    h = (normed * vec_ref[2:3, :] + vec_ref[3:4, :]).astype(BF16)
    h_ref[0] = h
    g = g_ref[0]
    total = None
    for t in range(0, part, tile):
        cols = slice(t, t + tile)
        u = dot_nn(h, up_ref[:, cols]) + vec_ref[8:9, cols]
        act, slope = gelu_and_slope(u)
        act_ref[0, :, cols] = act.astype(BF16)
        gu = (dot_nt(g, down_ref[cols, :]) * slope).astype(BF16)
        gu_ref[0, :, cols] = gu
        sum_ref[0:1, cols] += jnp.sum(gu.astype(F32), 0, keepdims=True)
        term = dot_nt(gu, up_ref[:, cols])
        total = term if total is None else total + term
    total = total.astype(BF16)

    @pl.when(i == 0)
    def _():
        low_ref[...] = total

    @pl.when(i == 1)
    def _():
        high_ref[...] = total


def feed(me, got, x_all, g_all, vecs, base, weights, ids=None, held=()):
    n, block, dm = x_all.shape
    part = dm if base else weights[1].shape[1]
    width = got[0].shape[1]

    def whole(shape):
        return pl.BlockSpec(shape, lambda i, me: (0,) * len(shape))

    def one(width):
        return pl.BlockSpec((1, block, width), lambda i, me: (i + base, 0, 0))

    def new(width):
        return pl.BlockSpec((1, block, width), lambda i, me: (i, 0, 0))

    def piece(p):
        return pl.BlockSpec((1, width, block), lambda i, me: ((i + base) ^ p, 0, 0))

    if base:
        part = weights[0].shape[2]
    wide = jax.ShapeDtypeStruct((2, block, dm), BF16)
    hidden = jax.ShapeDtypeStruct((2, block, part), BF16)
    low = jax.ShapeDtypeStruct((block, dm), BF16)
    outs = [wide, hidden, hidden, low, low, jax.ShapeDtypeStruct((8, part), F32)]
    specs = [new(dm), new(part), new(part)] + [whole(o.shape) for o in outs[3:]]
    more = [(dm, dm), (dm, part), (part, dm)] if base else []
    outs += [jax.ShapeDtypeStruct(m, BF16) for m in more] or [jax.ShapeDtypeStruct((block, dm), F32)]
    specs += [whole(o.shape) for o in outs[6:]]
    args = [*got]
    ins = [piece(p) for p in range(n)]
    if base:
        args += [*weights, x_all, g_all, vecs]
        ins += [whole(a.shape) for a in weights] + [one(dm), one(dm), whole(vecs.shape)]
    else:
        args += [x_all, g_all, vecs, *weights, held]
        ins += [one(dm), one(dm)] + [whole(a.shape) for a in (vecs, *weights, held)]
    return pl.pallas_call(
        functools.partial(feed_kernel, n=n, base=base, tile=256 if part % 256 == 0 else part, ids=ids),
        grid_spec=pltpu.PrefetchScalarGridSpec(num_scalar_prefetch=1, grid=(2,), in_specs=ins, out_specs=specs),
        out_shape=outs,
        compiler_params=pltpu.CompilerParams(vmem_limit_bytes=48 * 1024 * 1024),
        cost_estimate=pl.CostEstimate(
            flops=9 * 1000**3, bytes_accessed=16 * 1000**2, transcendentals=3 * 1000**2
        ),
        name="feed_far" if base else "feed_near",
    )(me, *args)


def turn_kernel(me_ref, *refs, n):
    got, refs = refs[:n], refs[n:]
    keep_ref, near_ref, far_ref, x_two_ref, g_ref, out_w_ref, vec_ref = refs[:7]
    gos, (gx_ref, d_out_ref, sum_ref) = refs[7 : 7 + n], refs[7 + n :]
    me = me_ref[0]
    width = got[0].shape[1]
    gh = keep_ref[...].astype(F32) + near_ref[...].astype(F32) + far_ref[...].astype(F32)
    normed, inv_std = normed_parts(x_two_ref[...])
    g = g_ref[...].astype(F32)
    gx = g + normalize_back(gh, normed, inv_std, vec_ref[2:3, :])
    gx_ref[...] = gx
    gb = gx.astype(BF16)
    for p in range(n):
        own = pl.ds(pl.multiple_of((me ^ p) * width, width), width)
        gos[p][...] = dot_nt(out_w_ref[own, :], gb).astype(BF16)
        d_out_ref[own, :] = dot_nn(got[p][0], gb).astype(BF16)
    sum_ref[0:1, :] = jnp.sum(gh * normed, 0, keepdims=True)
    sum_ref[1:2, :] = jnp.sum(gh, 0, keepdims=True)
    sum_ref[2:3, :] = jnp.sum(gb.astype(F32), 0, keepdims=True)
    sum_ref[3:4, :] = jnp.sum(g, 0, keepdims=True)


def turn(me, got, keep, near, far, x_two, g, out_w, vecs):
    n = len(got)
    _, width, block = got[0].shape
    dm = out_w.shape[1]

    def whole(shape):
        return pl.BlockSpec(shape, lambda i, me: (0,) * len(shape))

    def piece(p):
        return pl.BlockSpec((1, width, block), lambda i, me: (p, 0, 0))

    outs = [jax.ShapeDtypeStruct((width, block), BF16)] * n + [
        jax.ShapeDtypeStruct((block, dm), F32),
        jax.ShapeDtypeStruct(out_w.shape, BF16),
        jax.ShapeDtypeStruct((8, dm), F32),
    ]
    return pl.pallas_call(
        functools.partial(turn_kernel, n=n),
        grid_spec=pltpu.PrefetchScalarGridSpec(
            num_scalar_prefetch=1,
            grid=(1,),
            in_specs=[piece(p) for p in range(n)]
            + [whole(a.shape) for a in (keep, near, far, x_two, g, out_w, vecs)],
            out_specs=[whole(o.shape) for o in outs],
        ),
        out_shape=outs,
        compiler_params=pltpu.CompilerParams(vmem_limit_bytes=48 * 1024 * 1024),
        cost_estimate=pl.CostEstimate(flops=3 * 1000**3, bytes_accessed=8 * 1000**2, transcendentals=0),
        name="turn",
    )(me, *got, keep, near, far, x_two, g, out_w, vecs)


def leave_kernel(
    me_ref, x_ref, grad_ref, w_ref, vec_ref, two_ref, up_ref, even_ref, odd_ref, out_ref, sum_ref, add_ref, tile_ref
):
    i = pl.program_id(0)

    @pl.when(i == 0)
    def _():
        sum_ref[...] = jnp.zeros_like(sum_ref)
        add_ref[...] = jnp.zeros_like(add_ref)

    grads = grad_ref[0]
    gh = dot_nt(grads, w_ref[...])
    normed, _ = normed_parts(x_ref[0].astype(F32))
    low = gh.astype(BF16)

    @pl.when(i % 2 == 0)
    def _():
        even_ref[0] = low

    @pl.when(i % 2 == 1)
    def _():
        odd_ref[0] = low

    sum_ref[0:1, :] += jnp.sum(gh * normed, 0, keepdims=True)
    sum_ref[1:2, :] += jnp.sum(gh, 0, keepdims=True)
    add_ref[0:1, :] += jnp.sum(grads.astype(F32), 0, keepdims=True)

    @pl.when(i == pl.num_programs(0) - 1)
    def _():
        width = grads.shape[1] // 3
        dm = w_ref.shape[0]
        rows = [sum_ref[0:2, :], two_ref[0:4, :], jnp.zeros((2, dm), F32), up_ref[0:1, :]]
        rows = jnp.concatenate(rows + [jnp.zeros((LANES - 9, dm), F32)], 0)
        tile_ref[...] = rows.T
        add = jnp.concatenate(
            [
                jnp.zeros((6, width), F32),
                add_ref[0:1, :width],
                add_ref[0:1, 2 * width :],
                jnp.zeros((LANES - 8, width), F32),
            ],
            0,
        )
        own = pl.ds(pl.multiple_of(me_ref[0] * width, width), width)
        tile_ref[own, :] += add.T
        out_ref[...] = tile_ref[...].astype(BF16)


def leave(me, x_all, grads, w, vecs, sums_two, sums_up):
    n, block, wide = grads.shape
    dm = w.shape[0]

    def whole(shape):
        return pl.BlockSpec(shape, lambda i, me: (0,) * len(shape))

    def one(width):
        return pl.BlockSpec((1, block, width), lambda i, me: (i, 0, 0))

    def half(width):
        return pl.BlockSpec((1, block, width), lambda i, me: (i // 2, 0, 0))

    pair = jax.ShapeDtypeStruct((n // 2, block, dm), BF16)
    return pl.pallas_call(
        leave_kernel,
        grid_spec=pltpu.PrefetchScalarGridSpec(
            num_scalar_prefetch=1,
            grid=(n,),
            in_specs=[one(dm), one(wide)] + [whole(a.shape) for a in (w, vecs, sums_two, sums_up)],
            out_specs=[half(dm), half(dm), whole((dm, LANES))],
            scratch_shapes=[
                pltpu.VMEM((8, dm), F32),
                pltpu.VMEM((8, wide), F32),
                pltpu.VMEM((dm, LANES), F32),
            ],
        ),
        out_shape=[
            pair,
            pair,
            jax.ShapeDtypeStruct((dm, LANES), BF16),
        ],
        compiler_params=pltpu.CompilerParams(vmem_limit_bytes=48 * 1024 * 1024),
        cost_estimate=pl.CostEstimate(flops=6 * 1000**3, bytes_accessed=10 * 1000**2, transcendentals=0),
        name="leave",
    )(me, x_all, grads, w, vecs, sums_two, sums_up)


def hand_over_kernel(me_ref, *refs, n, rows, first):
    blob_a, blob_b, feed_a, feed_b = refs[:4]
    pieces, (out_ref, down_ref, last_ref) = refs[4 : 4 + n], refs[4 + n :]
    size = n * rows
    blob = blob_a[...].astype(F32) + blob_b[...].astype(F32)
    feed = feed_a[...].astype(F32) + feed_b[...].astype(F32)
    out_ref[...] = blob[size:]
    down_ref[...] = feed[size:]
    last_ref[...] = blob[:size, first - LANES : first]
    both = jnp.concatenate([blob[:size, :first], feed[:size]], 1)
    parts = [both[t * rows : (t + 1) * rows] for t in range(n)]
    for p, ref in enumerate(pieces):
        chosen = parts[0]
        for t in range(1, n):
            chosen = jnp.where((me_ref[0] ^ p) == t, parts[t], chosen)
        ref[...] = chosen.astype(BF16)


def hand_over(me, blob, feeds, rows, n, first):
    dm = blob[0].shape[1]
    part = feeds[0].shape[1]
    size = n * rows
    vmem = pl.BlockSpec(memory_space=pltpu.VMEM)
    *pieces, out, down, last = pl.pallas_call(
        functools.partial(hand_over_kernel, n=n, rows=rows, first=first),
        in_specs=[pl.BlockSpec(memory_space=pltpu.SMEM)] + [vmem] * 4,
        out_specs=[vmem] * (n + 3),
        out_shape=[jax.ShapeDtypeStruct((rows, first + part), BF16)] * n
        + [
            jax.ShapeDtypeStruct((rows, dm), F32),
            jax.ShapeDtypeStruct((feeds[0].shape[0] - size, part), F32),
            jax.ShapeDtypeStruct((size, LANES), F32),
        ],
        name="hand_over",
    )(me, *blob, *feeds)
    return pieces, out, down, last


def finish_kernel(me_ref, *refs, n, width, nd):
    pieces, (q_ref, k_ref, v_ref, vec_ref, up_ref) = refs[:n], refs[n:]
    first = 3 * width + LANES
    pieces = [p[...].astype(F32) for p in pieces]
    vec_ref[...] = sum(p[:, 3 * width : first] for p in pieces)
    bit = 1
    while bit < n:
        on = (me_ref[0] & bit) != 0
        for p in range(n):
            if not p & bit:
                a, b = pieces[p], pieces[p | bit]
                pieces[p] = jnp.where(on, b, a)
                pieces[p | bit] = jnp.where(on, a, b)
        bit *= 2
    step = (pieces[0].shape[1] - first) // nd
    for t in range(n):
        for i, ref in enumerate((q_ref, k_ref, v_ref)):
            ref[:, t * width : (t + 1) * width] = pieces[t][:, i * width : (i + 1) * width]
        for j in range(nd):
            to = (j * n + t) * step
            up_ref[:, to : to + step] = pieces[t][:, first + j * step : first + (j + 1) * step]


def finish(me, pieces, width, nd):
    n = len(pieces)
    rows, wide = pieces[0].shape
    weight = jax.ShapeDtypeStruct((rows, n * width), F32)
    tile = jax.ShapeDtypeStruct((rows, LANES), F32)
    vmem = pl.BlockSpec(memory_space=pltpu.VMEM)
    return pl.pallas_call(
        functools.partial(finish_kernel, n=n, width=width, nd=nd),
        in_specs=[pl.BlockSpec(memory_space=pltpu.SMEM)] + [vmem] * n,
        out_specs=[vmem] * 5,
        out_shape=[weight] * 3 + [tile, jax.ShapeDtypeStruct((rows, n * (wide - 3 * width - LANES)), F32)],
        name="finish",
    )(me, *pieces)


def body(
    nd,
    ns,
    tokens,
    cotangent,
    segments,
    w_query,
    w_key,
    w_value,
    w_out,
    w_up,
    w_down,
    ln1_gain,
    ln1_shift,
    query_bias,
    value_bias,
    out_bias,
    ln2_gain,
    ln2_shift,
    up_bias,
    down_bias,
):
    d = lax.axis_index("dp")
    s = lax.axis_index("seq")
    me = s.astype(jnp.int32).reshape(1)
    _, block, dm = tokens.shape
    hd = dm // H
    heads = H // ns
    width = heads * hd
    rows = w_query.shape[0]
    ff_rows, ff = w_down.shape[0], w_up.shape[1]
    ratio = ff_rows // rows
    part = ff // ns
    pad = 16

    me = jnp.stack([s, d]).astype(jnp.int32)
    masks = bits_of(nd)[::-1]
    far = bits_of(ns)[-1]
    x_own = tokens.reshape(block, dm)
    g = cotangent.reshape(block, dm)
    x_far = swap(x_own, "seq", ns, far)

    cols = [w.reshape(rows, ns, width) for w in (w_query, w_key, w_value)]
    vec = jnp.stack([ln1_gain, ln1_shift, ln2_gain, ln2_shift, out_bias, down_bias, query_bias, value_bias], 1)
    vec = jnp.pad(vec, ((0, 0), (0, LANES - vec.shape[1])))
    up_cols = w_up.reshape(rows, nd, ns, ff_rows).transpose(0, 2, 1, 3).reshape(rows, ns, part)
    lanes = LANES * -(-block // (rows * LANES))
    seg = jnp.pad(segments.reshape(block).astype(BF16), (0, rows * lanes - block)).reshape(rows, lanes)
    same = jnp.concatenate([vec, w_out, seg], 1)
    same = jnp.broadcast_to(same[:, None], (rows, ns, same.shape[1]))
    pieces = jnp.concatenate(cols + [same, up_cols], 2).transpose(1, 0, 2)
    first = 3 * width + LANES
    size = ns * rows
    pieces = trade_seq(pieces, s, ns)
    start = first + dm
    segs = jnp.stack([p[:, start : start + lanes].reshape(-1)[:block] for p in pieces]).astype(jnp.int32)
    seg_row = segs.reshape(ns, 1, block)
    seg_col = segs.reshape(ns, block, 1)
    pieces = ordered(pieces, s).reshape(size, -1)
    lane = lax.broadcasted_iota(jnp.int32, (size, first), 1)
    one = jnp.where(lane == 3 * width + 8, jnp.pad(up_bias, (0, size - ff_rows))[:, None], pieces[:, :first])
    two = jnp.concatenate([pieces[:, first:start], pieces[:, start + lanes :], w_down], 0)

    turned = masks[:-2] + masks[:-3:-1]
    ones = [one[None]]
    for mask in masks[:-2]:
        ones.append(swap(jnp.concatenate(ones, 0), "dp", nd, mask))
    ones = jnp.concatenate(ones, 0)
    cut = -(-(first // 2) // LANES) * LANES + LANES
    ones = [ones[:, :, :cut]], [ones[:, :, cut:]]
    ones[0][0], ones[1][0], two, seg_row, seg_col = lax.optimization_barrier(
        (ones[0][0], ones[1][0], two, seg_row, seg_col)
    )
    for parts, order in zip(ones, (masks, turned)):
        parts.append(swap(parts[0], "dp", nd, order[-2]))
    ones[0][1], ones[1][1], x_far = lax.optimization_barrier((ones[0][1], ones[1][1], x_far))
    g_far = swap(tie(g, x_far), "seq", ns, far)
    last = [jnp.concatenate(parts, 0) for parts in ones]
    twos = [tie(two, *last)[None]]
    for parts, held, order in zip(ones, last, (masks, turned)):
        parts.append(swap(held, "dp", nd, order[-1]))

    for mask in masks[:-2]:
        twos.append(swap(jnp.concatenate(twos, 0), "dp", nd, mask))
    parts = {0: x_own, far: x_far}
    for mask in bits_of(ns)[-2::-1]:
        for p in list(parts):
            parts[p | mask] = swap(parts[p], "seq", ns, mask)
    x_all = jnp.stack([parts[p] for p in range(ns)])

    ids = [gathered_ids(order) for order in (masks, turned)]
    ids = [[sum(i[:-2], [])] + i[-2:] for i in ids]
    ones, ids = zip(*[settle(p, d, nd, i, 1) for p, i in zip(ones, ids)])
    ones, x_all = lax.optimization_barrier((ones, x_all))
    qkv, h_one, w_qkv, vecs = enter(me, ones, ids, x_all, width)
    qkv, h_one, w_qkv, vecs, g_far, twos = lax.optimization_barrier((qkv, h_one, w_qkv, vecs, g_far, twos))
    two = jnp.concatenate(twos, 0)
    twos = [two] + [swap(two, "dp", nd, p) for p in (1, 2)]

    g_parts = {0: g, far: g_far}
    for mask in bits_of(ns)[-2::-1]:
        for p in list(g_parts):
            g_parts[p | mask] = swap(g_parts[p], "seq", ns, mask)
    qkv, two = lax.optimization_barrier((qkv, two))
    o_low, o_full, lse = attend(me, qkv, seg_row, seg_col, heads, hd)
    o_low, o_full, lse, twos[1:], *g_last = lax.optimization_barrier(
        (o_low, o_full, lse, twos[1:], g_parts[1], g_parts[ns - 1])
    )
    g_all = jnp.stack([g, g_last[0], g_far, g_last[1]])
    o_got = spread_seq(o_low, ns, (g_all,))
    twos.append(swap(tie(two, o_low), "dp", nd, 3))
    ids = sum(gathered_ids(masks[:-2]), [])
    twos, ids = settle(twos, d, nd, [[r ^ p for r in ids] for p in range(4)], 3)
    far_h, far_act, far_gu, gh_two, gh_three, sums_up, *weights = feed(
        me, o_got, x_all, g_all, vecs, 2, twos, ids
    )
    w_out_all, _, w_down_own = weights

    def over_rows(a, b):
        return jnp.einsum("nbk,nbc->kc", a, b, preferred_element_type=F32)

    d_down = over_rows(far_act, g_all[2:])
    sent = add_low(gh_two, swap(gh_three, "seq", ns, 1))
    far_got = swap(sent, "seq", ns, 2)
    sums_up, sent, d_down = lax.optimization_barrier((sums_up, sent, d_down))
    h_two, act, gu, gh_zero, gh_one, sums_up, x_two = feed(
        me, o_got, x_all, g_all, vecs, 0, weights, None, sums_up
    )
    near_got = swap(gh_one, "seq", ns, 1)
    d_down = (d_down + over_rows(act, g_all[:2])).astype(BF16)
    d_up = (over_rows(far_h, far_gu) + over_rows(h_two, gu)).astype(BF16)
    feeds = jnp.concatenate([d_up.reshape(nd, size, part), d_down.reshape(nd, ff_rows, dm)], 1)
    feed_keep, feed_sent = halves(feeds, d, nd, 1)
    feed_got = swap(feed_sent, "dp", nd, 1)
    far_got, feed_sent = lax.optimization_barrier((far_got, feed_sent))
    *gos, gx_two, d_out, sums_two = turn(me, o_got, gh_zero, near_got, far_got, x_two, g, w_out_all, vecs)
    go_got = [gos[0]] + [swap(gos[p], "seq", ns, p) for p in range(1, ns)]
    go_got[1], d_out, sums_two = lax.optimization_barrier((go_got[1], d_out, sums_two))
    act, far_act = lax.optimization_barrier((act, far_act, go_got[1]))[:2]
    out_parts = [dot_nn(a, w_down_own).astype(BF16) for a in (act[0], act[1], far_act[0], far_act[1])]
    out_sent = add_low(out_parts[2], swap(out_parts[3], "seq", ns, 1))
    out_near = swap(out_parts[1], "seq", ns, 1)
    out_far = swap(tie(out_sent, go_got[-1]), "seq", ns, 2)
    outs_keep, outs_sent = halves(d_out.reshape(nd * ns, rows, dm), s, ns, 1)
    outs_got = swap(outs_sent, "seq", ns, 1)
    outs_keep, outs_sent = halves(add_low(outs_keep, outs_got), s >> 1, ns // 2, 1)
    outs_got = swap(outs_sent, "seq", ns, 2)

    go_all = jnp.stack(go_got)
    go_all, *_ = lax.optimization_barrier((go_all, out_sent, out_parts, outs_sent))
    grads, d_qkv = attend_back(me, qkv, go_all, o_full, lse, seg_row, seg_col, h_one, heads, hd)
    grads, d_qkv, out_near, out_far, outs_got, feed_got = lax.optimization_barrier(
        (grads, d_qkv, out_near, out_far, outs_got, feed_got)
    )
    blob = jnp.concatenate(
        [
            jnp.pad(d_qkv.reshape(nd, size, 3 * width), ((0, 0), (0, 0), (0, dm - 3 * width))),
            add_low(outs_keep, outs_got),
        ],
        1,
    )
    blob_keep, blob_sent = halves(blob, d, nd, 1)
    blob_got = swap(blob_sent, "dp", nd, 1)
    feed_keep, feed_sent = halves(add_low(feed_keep, feed_got), d >> 1, nd // 2, 1)
    feed_got = swap(feed_sent, "dp", nd, 2)
    grads = lax.optimization_barrier((grads, blob_sent, feed_sent))[0]
    even, odd, tile = leave(me, x_all, grads, w_qkv, vecs, sums_two, sums_up)
    even, odd, tile, blob_got, feed_got = lax.optimization_barrier((even, odd, tile, blob_got, feed_got))
    tile = tile.reshape(nd // 4, 4, size, LANES)
    tiles = [lax.dynamic_index_in_dim(tile, (d & 3) ^ p, 1, False) for p in range(4)]
    tiles = [jnp.pad(t, ((0, 0), (0, rows), (3 * width, dm - first))) for t in tiles[::2]] + tiles[1::2]
    blob_keep, blob_sent = halves(add_low(blob_keep, blob_got), d >> 1, nd // 2, 1)
    blob_keep, blob_sent = blob_keep + tiles[0], blob_sent + tiles[1]
    blob_got = swap(blob_sent, "dp", nd, 2)
    tiles = [swap(t, "dp", nd, p) for t, p in zip(tie(tiles[2:], blob_sent), (1, 3))]
    feed_keep, feed_sent = halves(tie(add_low(feed_keep, feed_got), blob_sent), d >> 2, nd // 4, 1)
    feed_got = swap(feed_sent, "dp", nd, 4)
    keep, sent, got = collect_pairs(even, odd, ns)
    blob_got, sent, tiles = lax.optimization_barrier((blob_got, sent, tiles))
    tile = jnp.pad(tiles[0].astype(F32) + tiles[1].astype(F32), ((0, 0), (0, rows), (3 * width, dm - first)))
    blob = (blob_keep.astype(F32) + blob_got.astype(F32) + tile).astype(BF16)
    blob_keep, blob_sent = halves(blob, d >> 2, nd // 4, 1)
    blob_got = swap(blob_sent, "dp", nd, 4)
    blob_got, sent, feed_got = lax.optimization_barrier((blob_got, sent, feed_got))
    if nd > 8:
        rest = [(blob_keep, blob_got), (feed_keep, feed_got)]
        rest = [collect_dp(add_low(a, b), d >> 3, nd // 8, BF16, shift=3) for a, b in rest]
        rest = [(v, jnp.zeros_like(v)) for v in rest]
    else:
        rest = [(blob_keep[0], blob_got[0]), (feed_keep[0], feed_got[0])]
    pieces, sum_out, sum_down, last = hand_over(me, *rest, rows, ns, first)
    out = out_parts[0].astype(F32) + out_near.astype(F32) + out_far.astype(F32) + x_two + vecs[5:6]
    trades = [pieces[0]] + [swap(pieces[p], "seq", ns, p) for p in range(1, ns)]
    gh_one = keep.astype(F32) + got.astype(F32)
    n_own, inv_own = normed_parts(tie(x_own, pieces[0]).astype(F32))
    grad_x = gx_two + normalize_back(gh_one, n_own, inv_own, vecs[0:1])
    trades, grad_x, out, last = lax.optimization_barrier((trades, grad_x, out, last))
    sum_q, sum_k, sum_v, vec_sum, sum_up = finish(me, trades, width, nd)
    vec_sum = vec_sum.T
    sum_up_bias = last[:ff_rows, 8]
    v = [vec_sum[i] for i in range(8)]
    return (
        out.reshape(1, block, dm),
        grad_x.reshape(1, block, dm),
        sum_q,
        sum_k,
        sum_v,
        sum_out,
        sum_up,
        sum_down,
        v[0],
        v[1],
        v[6],
        v[7],
        v[4],
        v[2],
        v[3],
        sum_up_bias,
        v[5],
    )


def solution(mesh):
    act = P("dp", "seq", None)
    weight = P(("dp", "seq"), None)
    vector = P(("dp", "seq"))
    return jax.shard_map(
        functools.partial(body, mesh.shape["dp"], mesh.shape["seq"]),
        mesh=mesh,
        in_specs=(act, act, P("dp", "seq")) + (weight,) * 6 + (vector,) * 9,
        out_specs=(act, act) + (weight,) * 6 + (vector,) * 9,
        check_vma=False,
    )
```

```python
import functools
import math

import jax
import jax.numpy as jnp
from jax import lax
from jax.experimental import pallas as pl
from jax.experimental.pallas import tpu as pltpu
from jax.sharding import PartitionSpec as P

H = 12
EPSILON = 1e-05
MASKED = -1e30
F32 = jnp.float32
BF16 = jnp.bfloat16
LANES = 128


def dot_nt(a, b):
    return lax.dot_general(a, b, (((1,), (1,)), ((), ())), preferred_element_type=F32)


def dot_tn(a, b):
    return lax.dot_general(a, b, (((0,), (0,)), ((), ())), preferred_element_type=F32)


def dot_nn(a, b):
    return jnp.dot(a, b, preferred_element_type=F32)


def attend_kernel(me_ref, qkv_ref, seg_row_ref, seg_col_ref, low_ref, full_ref, lse_ref, *, heads, hd):
    me = me_ref[0]
    qi = pl.program_id(0)
    rq = qi ^ me
    block = qkv_ref.shape[1]
    width = heads * hd
    scale = jnp.asarray(1.0 / math.sqrt(hd), BF16)
    queries = [qkv_ref[rq, :, h * hd : (h + 1) * hd] * scale for h in range(heads)]
    seg_q = seg_row_ref[rq]

    def step(rk, state, causal):
        allowed = seg_col_ref[rk] == seg_q
        if causal:
            k_pos = lax.broadcasted_iota(jnp.int32, (block, block), 0)
            q_pos = lax.broadcasted_iota(jnp.int32, (block, block), 1)
            allowed = allowed & (k_pos <= q_pos)
        new = []
        for h in range(heads):
            top, total, mixed = state[h]
            key = qkv_ref[rk, :, width + h * hd : width + (h + 1) * hd]
            value = qkv_ref[rk, :, 2 * width + h * hd : 2 * width + (h + 1) * hd]
            scores = jnp.where(allowed, dot_nt(key, queries[h]), MASKED)
            higher = jnp.maximum(top, jnp.max(scores, 0, keepdims=True))
            weights = jnp.exp(scores - higher)
            fade = jnp.exp(top - higher)
            total = total * fade + jnp.sum(weights, 0, keepdims=True)
            mixed = mixed * fade + dot_tn(value, weights.astype(BF16))
            new.append((higher, total, mixed))
        return tuple(new)

    start = tuple(
        (jnp.full((1, block), MASKED, F32), jnp.zeros((1, block), F32), jnp.zeros((hd, block), F32))
        for _ in range(heads)
    )
    state = lax.fori_loop(0, qi, lambda kj, c: step(kj ^ me, c, False), start)
    state = step(rq, state, True)
    rows = []
    for h in range(heads):
        top, total, mixed = state[h]
        rows.append(mixed / total)
        lse_ref[0, h : h + 1, :] = top + jnp.log(total)
    full = jnp.concatenate(rows, 0)
    full_ref[0] = full
    low_ref[0] = full.astype(BF16)


def attend(me, qkv, seg_row, seg_col, heads, hd):
    n, block, _ = qkv.shape
    width = heads * hd

    def whole(shape):
        return pl.BlockSpec(shape, lambda i, me: (0,) * len(shape))

    def own(shape):
        return pl.BlockSpec(shape, lambda i, me: (i ^ me[0], 0, 0))

    return pl.pallas_call(
        functools.partial(attend_kernel, heads=heads, hd=hd),
        grid_spec=pltpu.PrefetchScalarGridSpec(
            num_scalar_prefetch=1,
            grid=(n,),
            in_specs=[whole(qkv.shape), whole(seg_row.shape), whole(seg_col.shape)],
            out_specs=[own((1, width, block)), own((1, width, block)), own((1, 8, block))],
        ),
        out_shape=[
            jax.ShapeDtypeStruct((n, width, block), BF16),
            jax.ShapeDtypeStruct((n, width, block), F32),
            jax.ShapeDtypeStruct((n, 8, block), F32),
        ],
        compiler_params=pltpu.CompilerParams(vmem_limit_bytes=40 * 1024 * 1024),
        cost_estimate=pl.CostEstimate(
            flops=20 * 1000**3, bytes_accessed=8 * 1000**2, transcendentals=8 * 1000**2
        ),
        name="attend",
    )(me, qkv, seg_row, seg_col)


def attend_back_kernel(
    me_ref, qkv_ref, go_ref, full_ref, lse_ref, seg_row_ref, seg_col_ref, h_ref, grad_ref, d_w_ref,
    gq_ref, dot_ref, total_ref, gk_ref, gv_ref, *, heads, hd
):
    me = me_ref[0]
    kj = pl.program_id(0)
    rk = kj ^ me
    n, block, _ = qkv_ref.shape
    width = heads * hd
    scale = 1.0 / math.sqrt(hd)
    low_scale = jnp.asarray(scale, BF16)

    @pl.when(kj == 0)
    def _():
        gq_ref[...] = jnp.zeros_like(gq_ref)
        total_ref[...] = jnp.zeros_like(total_ref)
        for b in range(n):
            prod = go_ref[b].astype(F32) * full_ref[b]
            for h in range(heads):
                dot_ref[b, h : h + 1, :] = jnp.sum(prod[h * hd : (h + 1) * hd], 0, keepdims=True)

    def step(rq, causal):
        for k0 in range(0, block, 512):
            for q0 in range(0, block, 256):
                if causal and q0 + 256 <= k0:
                    continue
                rows, cols = slice(k0, k0 + 512), slice(q0, q0 + 256)
                allowed = seg_col_ref[rk, rows, :] == seg_row_ref[rq][:, cols]
                if causal and q0 < k0 + 512:
                    k_pos = lax.broadcasted_iota(jnp.int32, (512, 256), 0) + k0
                    q_pos = lax.broadcasted_iota(jnp.int32, (512, 256), 1) + q0
                    allowed = allowed & (k_pos <= q_pos)
                for h in range(heads):
                    head = slice(h * hd, (h + 1) * hd)
                    query = qkv_ref[rq, cols, head] * low_scale
                    key = qkv_ref[rk, rows, width + h * hd : width + (h + 1) * hd]
                    value = qkv_ref[rk, rows, 2 * width + h * hd : 2 * width + (h + 1) * hd]
                    go = go_ref[rq, head, cols]
                    scores = jnp.where(allowed, dot_nt(key, query), MASKED)
                    weights = jnp.exp(scores - lse_ref[rq, h : h + 1, cols])
                    gw = dot_nn(value, go)
                    ds = (weights * (gw - dot_ref[rq, h : h + 1, cols])).astype(BF16)
                    gv = dot_nt(weights.astype(BF16), go)
                    gk = dot_nn(ds, query)
                    if causal and q0 <= k0:
                        gv_ref[h, rows, :] = gv
                        gk_ref[h, rows, :] = gk
                    else:
                        gv_ref[h, rows, :] += gv
                        gk_ref[h, rows, :] += gk
                    gq_ref[rq, head, cols] += dot_tn(key, ds)

    step(rk, True)

    @pl.loop(kj + 1, n)
    def _(qi):
        step(qi ^ me, False)

    grad_ref[0, :, :width] = (gq_ref[rk] * scale).T.astype(BF16)
    for h in range(heads):
        gk, gv = gk_ref[h], gv_ref[h]
        grad_ref[0, :, width + h * hd : width + (h + 1) * hd] = gk.astype(BF16)
        grad_ref[0, :, 2 * width + h * hd : 2 * width + (h + 1) * hd] = gv.astype(BF16)
    total_ref[...] += dot_tn(h_ref[0], grad_ref[0])

    @pl.when(kj == n - 1)
    def _():
        d_w_ref[...] = total_ref[...].astype(BF16)


def attend_back(me, qkv, go, full, lse, seg_row, seg_col, h_one, heads, hd):
    n, block, wide = qkv.shape
    dm = h_one.shape[2]
    width = heads * hd

    def whole(shape):
        return pl.BlockSpec(shape, lambda i, me: (0,) * len(shape))

    return pl.pallas_call(
        functools.partial(attend_back_kernel, heads=heads, hd=hd),
        grid_spec=pltpu.PrefetchScalarGridSpec(
            num_scalar_prefetch=1,
            grid=(n,),
            in_specs=[whole(a.shape) for a in (qkv, go, full, lse, seg_row, seg_col)]
            + [pl.BlockSpec((1, block, dm), lambda i, me: (i ^ me[0], 0, 0))],
            out_specs=[pl.BlockSpec((1, block, wide), lambda i, me: (i ^ me[0], 0, 0)), whole((dm, wide))],
            scratch_shapes=[
                pltpu.VMEM((n, width, block), F32),
                pltpu.VMEM((n, 8, block), F32),
                pltpu.VMEM((dm, wide), F32),
                pltpu.VMEM((heads, block, hd), F32),
                pltpu.VMEM((heads, block, hd), F32),
            ],
        ),
        out_shape=[
            jax.ShapeDtypeStruct((n, block, wide), BF16),
            jax.ShapeDtypeStruct((dm, wide), BF16),
        ],
        compiler_params=pltpu.CompilerParams(vmem_limit_bytes=40 * 1024 * 1024),
        cost_estimate=pl.CostEstimate(
            flops=40 * 1000**3, bytes_accessed=12 * 1000**2, transcendentals=8 * 1000**2
        ),
        name="attend_back",
    )(me, qkv, go, full, lse, seg_row, seg_col, h_one)


def normed_parts(value):
    mean = jnp.mean(value, -1, keepdims=True)
    centred = value - mean
    inv_std = lax.rsqrt(jnp.mean(centred * centred, -1, keepdims=True) + EPSILON)
    return centred * inv_std, inv_std


def normalize_back(grad_in, normed, inv_std, gain):
    scaled = grad_in * gain
    return inv_std * (
        scaled
        - jnp.mean(scaled, -1, keepdims=True)
        - normed * jnp.mean(scaled * normed, -1, keepdims=True)
    )


def gelu_and_slope(value):
    cumul = 0.5 * (1.0 + lax.erf(value * (1.0 / math.sqrt(2.0))))
    slope = cumul + value * jnp.exp(-0.5 * value * value) * (1.0 / math.sqrt(2.0 * math.pi))
    return value * cumul, slope


def tie(value, *others):
    return lax.optimization_barrier((value,) + others)[0] if others else value


def swap(value, axis, size, mask):
    return lax.ppermute(value, axis, [(i, i ^ mask) for i in range(size)])


def bits_of(size):
    count = size.bit_length() - 1
    return [1 << b for b in range(count)]


def ordered(parts, index):
    parts = [part[None] for part in parts]
    bit = 1
    while len(parts) > 1:
        on = (index & bit) != 0
        parts = [
            jnp.where(on, jnp.concatenate([b, a], 0), jnp.concatenate([a, b], 0))
            for a, b in zip(parts[::2], parts[1::2])
        ]
        bit *= 2
    return parts[0]


def gathered_ids(masks):
    held, lists = [0], [[0]]
    for mask in masks:
        new = [r ^ mask for r in held]
        lists.append(new)
        held = held + new
    return lists


def settle(parts, index, size, ids, count):
    rows = parts[0].shape[1] // count
    if rows % 16 == 0:
        return parts, ids
    held = sum(ids, [])
    at = jnp.asarray([held.index(r) for r in range(size)])
    whole = jnp.concatenate(parts, 0)[at[jnp.arange(size) ^ index]]
    whole = whole.reshape(size, count, rows, -1).transpose(1, 0, 2, 3)
    return [whole.reshape(1, size * count * rows, -1)], [[None]]


def place(refs, ids, index, count, put):
    for ref, held in zip(refs, ids):
        rows = ref.shape[1] // count
        for j, r in enumerate(held):
            where = slice(None) if r is None else pl.ds(pl.multiple_of((index ^ r) * rows, rows), rows)
            for k in range(count):
                put(k, where, ref[j, k * rows : (k + 1) * rows, :])


def halves(value, index, size, mask):
    value = value.reshape((-1, 2, mask) + value.shape[1:])
    on = ((index & mask) != 0).astype(jnp.int32)
    shape = (-1,) + value.shape[3:]
    keep = lax.dynamic_index_in_dim(value, on, 1, False).reshape(shape)
    return keep, lax.dynamic_index_in_dim(value, 1 - on, 1, False).reshape(shape)


def add_low(a, b, kind=BF16):
    return (a.astype(F32) + b.astype(F32)).astype(kind)


def collect_dp(value, index, size, last=F32, shift=0):
    masks = bits_of(size)
    shape = value.shape[1:]
    value = value.reshape((2,) * len(masks) + shape)
    for step, mask in enumerate(masks):
        axis = len(masks) - 1 - step
        on = ((index & mask) != 0).astype(jnp.int32)
        keep = lax.dynamic_index_in_dim(value, on, axis, False)
        send = lax.dynamic_index_in_dim(value, 1 - on, axis, False)
        got = swap(send, "dp", size << shift, mask << shift)
        value = keep.astype(F32) + got.astype(F32)
        value = value.astype(BF16 if step < len(masks) - 1 else last)
    return value


def collect_pairs(even, odd, size, tied=()):
    got = swap(odd, "seq", size, 1)
    sums = [(even[i].astype(F32) + got[i].astype(F32)).astype(BF16) for i in range(size // 2)]
    mask = 2
    while len(sums) > 2:
        sent = [swap(b, "seq", size, mask) for b in sums[1::2]]
        sums = [(a.astype(F32) + b.astype(F32)).astype(BF16) for a, b in zip(sums[::2], sent)]
        mask *= 2
    return sums[0], sums[1], swap(tie(sums[1], *tied), "seq", size, mask)


def spread_seq(value, size, gate=()):
    got = {0: value}
    for mask in bits_of(size)[::-1]:
        for p in list(got):
            got[p | mask] = swap(tie(got[p], *gate) if p else got[p], "seq", size, mask)
    return [got[p] for p in range(size)]


def trade_seq(pieces, index, size):
    return [
        swap(lax.dynamic_index_in_dim(pieces, index ^ p, 0, False), "seq", size, p)
        if p
        else lax.dynamic_index_in_dim(pieces, index, 0, False)
        for p in range(size)
    ]


def enter_kernel(me_ref, *refs, ids, n, width, cut):
    count = len(ids[0]) + len(ids[1])
    pieces, (x_ref, qkv_ref, h_ref, w_ref, vec_ref, tile_ref, add_ref) = refs[:count], refs[count:]
    me = me_ref[0]

    @pl.when(pl.program_id(0) == 0)
    def _():
        def put_left(k, where, rows):
            w_ref[where, :cut] = rows

        def put_right(k, where, rows):
            w_ref[where, cut:] = rows[:, : 3 * width - cut]
            tile_ref[where, :] = rows[:, 3 * width - cut :].astype(F32)

        place(pieces[: len(ids[0])], ids[0], me_ref[1], 1, put_left)
        place(pieces[len(ids[0]) :], ids[1], me_ref[1], 1, put_right)
        vecs = tile_ref[...].T[:16]
        vec_ref[...] = vecs
        for i, row in ((0, 6), (2, 7)):
            add = vecs[row : row + 1, :width]
            for t in range(1, n):
                add = jnp.where(me == t, vecs[row : row + 1, t * width : (t + 1) * width], add)
            add_ref[0:1, i * width : (i + 1) * width] = add
        add_ref[0:1, width : 2 * width] = jnp.zeros((1, width), F32)

    normed, _ = normed_parts(x_ref[0].astype(F32))
    h = (normed * vec_ref[0:1, :] + vec_ref[1:2, :]).astype(BF16)
    h_ref[0] = h
    qkv_ref[0] = (dot_nn(h, w_ref[...]) + add_ref[0:1, :]).astype(BF16)


def enter(me, pieces, ids, x_all, width):
    n, block, dm = x_all.shape
    cut = pieces[0][0].shape[2]
    pieces = [*pieces[0], *pieces[1]]

    def whole(shape):
        return pl.BlockSpec(shape, lambda i, me: (0,) * len(shape))

    def one(width):
        return pl.BlockSpec((1, block, width), lambda i, me: (i, 0, 0))

    return pl.pallas_call(
        functools.partial(enter_kernel, ids=ids, n=n, width=width, cut=cut),
        grid_spec=pltpu.PrefetchScalarGridSpec(
            num_scalar_prefetch=1,
            grid=(n,),
            in_specs=[whole(a.shape) for a in pieces] + [one(dm)],
            out_specs=[one(3 * width), one(dm), whole((dm, 3 * width)), whole((16, dm))],
            scratch_shapes=[pltpu.VMEM((dm, LANES), F32), pltpu.VMEM((8, 3 * width), F32)],
        ),
        out_shape=[
            jax.ShapeDtypeStruct((n, block, 3 * width), BF16),
            jax.ShapeDtypeStruct((n, block, dm), BF16),
            jax.ShapeDtypeStruct((dm, 3 * width), BF16),
            jax.ShapeDtypeStruct((16, dm), F32),
        ],
        compiler_params=pltpu.CompilerParams(vmem_limit_bytes=40 * 1024 * 1024),
        cost_estimate=pl.CostEstimate(flops=5 * 1000**3, bytes_accessed=8 * 1000**2, transcendentals=0),
        name="enter",
    )(me, *pieces, x_all)


def feed_kernel(me_ref, *refs, n, base, tile, ids):
    got, refs = refs[:n], refs[n:]
    me = me_ref[0]
    i = pl.program_id(0)
    if base:
        pieces, refs = refs[: len(ids)], refs[len(ids) :]
        x_ref, g_ref, vec_ref = refs[:3]
        h_ref, act_ref, gu_ref, low_ref, high_ref, sum_ref, out_w_ref, up_ref, down_ref = refs[3:]
    else:
        x_ref, g_ref, vec_ref, out_w_ref, up_ref, down_ref, sum_in_ref = refs[:7]
        h_ref, act_ref, gu_ref, low_ref, high_ref, sum_ref, x_two_ref = refs[7:]
    part = up_ref.shape[1]
    width = got[0].shape[1]

    @pl.when(i == 0)
    def _():
        if base:
            sum_ref[...] = jnp.zeros_like(sum_ref)

            def put(k, where, rows):
                (out_w_ref, up_ref, down_ref)[k][where, :] = rows

            place(pieces, ids, me_ref[1], 3, put)
        else:
            sum_ref[...] = sum_in_ref[...]

    x_two = x_ref[0].astype(F32) + vec_ref[4:5, :]
    for p in range(n):
        own = pl.ds(pl.multiple_of((me ^ p) * width, width), width)
        x_two = x_two + dot_tn(got[p][0], out_w_ref[own, :])
    if not base:

        @pl.when(i == 0)
        def _():
            x_two_ref[...] = x_two

    normed, _ = normed_parts(x_two)
    h = (normed * vec_ref[2:3, :] + vec_ref[3:4, :]).astype(BF16)
    h_ref[0] = h
    g = g_ref[0]
    total = None
    for t in range(0, part, tile):
        cols = slice(t, t + tile)
        u = dot_nn(h, up_ref[:, cols]) + vec_ref[8:9, cols]
        act, slope = gelu_and_slope(u)
        act_ref[0, :, cols] = act.astype(BF16)
        gu = (dot_nt(g, down_ref[cols, :]) * slope).astype(BF16)
        gu_ref[0, :, cols] = gu
        sum_ref[0:1, cols] += jnp.sum(gu.astype(F32), 0, keepdims=True)
        term = dot_nt(gu, up_ref[:, cols])
        total = term if total is None else total + term
    total = total.astype(BF16)

    @pl.when(i == 0)
    def _():
        low_ref[...] = total

    @pl.when(i == 1)
    def _():
        high_ref[...] = total


def feed(me, got, x_all, g_all, vecs, base, weights, ids=None, held=()):
    n, block, dm = x_all.shape
    part = dm if base else weights[1].shape[1]
    width = got[0].shape[1]

    def whole(shape):
        return pl.BlockSpec(shape, lambda i, me: (0,) * len(shape))

    def one(width):
        return pl.BlockSpec((1, block, width), lambda i, me: (i + base, 0, 0))

    def new(width):
        return pl.BlockSpec((1, block, width), lambda i, me: (i, 0, 0))

    def piece(p):
        return pl.BlockSpec((1, width, block), lambda i, me: ((i + base) ^ p, 0, 0))

    if base:
        part = weights[0].shape[2]
    wide = jax.ShapeDtypeStruct((2, block, dm), BF16)
    hidden = jax.ShapeDtypeStruct((2, block, part), BF16)
    low = jax.ShapeDtypeStruct((block, dm), BF16)
    outs = [wide, hidden, hidden, low, low, jax.ShapeDtypeStruct((8, part), F32)]
    specs = [new(dm), new(part), new(part)] + [whole(o.shape) for o in outs[3:]]
    more = [(dm, dm), (dm, part), (part, dm)] if base else []
    outs += [jax.ShapeDtypeStruct(m, BF16) for m in more] or [jax.ShapeDtypeStruct((block, dm), F32)]
    specs += [whole(o.shape) for o in outs[6:]]
    args = [*got]
    ins = [piece(p) for p in range(n)]
    if base:
        args += [*weights, x_all, g_all, vecs]
        ins += [whole(a.shape) for a in weights] + [one(dm), one(dm), whole(vecs.shape)]
    else:
        args += [x_all, g_all, vecs, *weights, held]
        ins += [one(dm), one(dm)] + [whole(a.shape) for a in (vecs, *weights, held)]
    return pl.pallas_call(
        functools.partial(feed_kernel, n=n, base=base, tile=256 if part % 256 == 0 else part, ids=ids),
        grid_spec=pltpu.PrefetchScalarGridSpec(num_scalar_prefetch=1, grid=(2,), in_specs=ins, out_specs=specs),
        out_shape=outs,
        compiler_params=pltpu.CompilerParams(vmem_limit_bytes=48 * 1024 * 1024),
        cost_estimate=pl.CostEstimate(
            flops=9 * 1000**3, bytes_accessed=16 * 1000**2, transcendentals=3 * 1000**2
        ),
        name="feed_far" if base else "feed_near",
    )(me, *args)


def turn_kernel(me_ref, *refs, n):
    got, refs = refs[:n], refs[n:]
    keep_ref, near_ref, far_ref, x_two_ref, g_ref, out_w_ref, vec_ref = refs[:7]
    gos, (gx_ref, d_out_ref, sum_ref) = refs[7 : 7 + n], refs[7 + n :]
    me = me_ref[0]
    width = got[0].shape[1]
    gh = keep_ref[...].astype(F32) + near_ref[...].astype(F32) + far_ref[...].astype(F32)
    normed, inv_std = normed_parts(x_two_ref[...])
    g = g_ref[...].astype(F32)
    gx = g + normalize_back(gh, normed, inv_std, vec_ref[2:3, :])
    gx_ref[...] = gx
    gb = gx.astype(BF16)
    for p in range(n):
        own = pl.ds(pl.multiple_of((me ^ p) * width, width), width)
        gos[p][...] = dot_nt(out_w_ref[own, :], gb).astype(BF16)
        d_out_ref[own, :] = dot_nn(got[p][0], gb).astype(BF16)
    sum_ref[0:1, :] = jnp.sum(gh * normed, 0, keepdims=True)
    sum_ref[1:2, :] = jnp.sum(gh, 0, keepdims=True)
    sum_ref[2:3, :] = jnp.sum(gb.astype(F32), 0, keepdims=True)
    sum_ref[3:4, :] = jnp.sum(g, 0, keepdims=True)


def turn(me, got, keep, near, far, x_two, g, out_w, vecs):
    n = len(got)
    _, width, block = got[0].shape
    dm = out_w.shape[1]

    def whole(shape):
        return pl.BlockSpec(shape, lambda i, me: (0,) * len(shape))

    def piece(p):
        return pl.BlockSpec((1, width, block), lambda i, me: (p, 0, 0))

    outs = [jax.ShapeDtypeStruct((width, block), BF16)] * n + [
        jax.ShapeDtypeStruct((block, dm), F32),
        jax.ShapeDtypeStruct(out_w.shape, BF16),
        jax.ShapeDtypeStruct((8, dm), F32),
    ]
    return pl.pallas_call(
        functools.partial(turn_kernel, n=n),
        grid_spec=pltpu.PrefetchScalarGridSpec(
            num_scalar_prefetch=1,
            grid=(1,),
            in_specs=[piece(p) for p in range(n)]
            + [whole(a.shape) for a in (keep, near, far, x_two, g, out_w, vecs)],
            out_specs=[whole(o.shape) for o in outs],
        ),
        out_shape=outs,
        compiler_params=pltpu.CompilerParams(vmem_limit_bytes=48 * 1024 * 1024),
        cost_estimate=pl.CostEstimate(flops=3 * 1000**3, bytes_accessed=8 * 1000**2, transcendentals=0),
        name="turn",
    )(me, *got, keep, near, far, x_two, g, out_w, vecs)


def leave_kernel(
    me_ref, x_ref, grad_ref, w_ref, vec_ref, two_ref, up_ref, even_ref, odd_ref, out_ref, sum_ref, add_ref, tile_ref
):
    i = pl.program_id(0)

    @pl.when(i == 0)
    def _():
        sum_ref[...] = jnp.zeros_like(sum_ref)
        add_ref[...] = jnp.zeros_like(add_ref)

    grads = grad_ref[0]
    gh = dot_nt(grads, w_ref[...])
    normed, _ = normed_parts(x_ref[0].astype(F32))
    low = gh.astype(BF16)

    @pl.when(i % 2 == 0)
    def _():
        even_ref[0] = low

    @pl.when(i % 2 == 1)
    def _():
        odd_ref[0] = low

    sum_ref[0:1, :] += jnp.sum(gh * normed, 0, keepdims=True)
    sum_ref[1:2, :] += jnp.sum(gh, 0, keepdims=True)
    add_ref[0:1, :] += jnp.sum(grads.astype(F32), 0, keepdims=True)

    @pl.when(i == pl.num_programs(0) - 1)
    def _():
        width = grads.shape[1] // 3
        dm = w_ref.shape[0]
        rows = [sum_ref[0:2, :], two_ref[0:4, :], jnp.zeros((2, dm), F32), up_ref[0:1, :]]
        rows = jnp.concatenate(rows + [jnp.zeros((LANES - 9, dm), F32)], 0)
        tile_ref[...] = rows.T
        add = jnp.concatenate(
            [
                jnp.zeros((6, width), F32),
                add_ref[0:1, :width],
                add_ref[0:1, 2 * width :],
                jnp.zeros((LANES - 8, width), F32),
            ],
            0,
        )
        own = pl.ds(pl.multiple_of(me_ref[0] * width, width), width)
        tile_ref[own, :] += add.T
        out_ref[...] = tile_ref[...].astype(BF16)


def leave(me, x_all, grads, w, vecs, sums_two, sums_up):
    n, block, wide = grads.shape
    dm = w.shape[0]

    def whole(shape):
        return pl.BlockSpec(shape, lambda i, me: (0,) * len(shape))

    def one(width):
        return pl.BlockSpec((1, block, width), lambda i, me: (i, 0, 0))

    def half(width):
        return pl.BlockSpec((1, block, width), lambda i, me: (i // 2, 0, 0))

    pair = jax.ShapeDtypeStruct((n // 2, block, dm), BF16)
    return pl.pallas_call(
        leave_kernel,
        grid_spec=pltpu.PrefetchScalarGridSpec(
            num_scalar_prefetch=1,
            grid=(n,),
            in_specs=[one(dm), one(wide)] + [whole(a.shape) for a in (w, vecs, sums_two, sums_up)],
            out_specs=[half(dm), half(dm), whole((dm, LANES))],
            scratch_shapes=[
                pltpu.VMEM((8, dm), F32),
                pltpu.VMEM((8, wide), F32),
                pltpu.VMEM((dm, LANES), F32),
            ],
        ),
        out_shape=[
            pair,
            pair,
            jax.ShapeDtypeStruct((dm, LANES), BF16),
        ],
        compiler_params=pltpu.CompilerParams(vmem_limit_bytes=48 * 1024 * 1024),
        cost_estimate=pl.CostEstimate(flops=6 * 1000**3, bytes_accessed=10 * 1000**2, transcendentals=0),
        name="leave",
    )(me, x_all, grads, w, vecs, sums_two, sums_up)


def hand_over_kernel(me_ref, *refs, n, rows, first):
    blob_a, blob_b, feed_a, feed_b = refs[:4]
    pieces, (out_ref, down_ref, last_ref) = refs[4 : 4 + n], refs[4 + n :]
    size = n * rows
    blob = blob_a[...].astype(F32) + blob_b[...].astype(F32)
    feed = feed_a[...].astype(F32) + feed_b[...].astype(F32)
    out_ref[...] = blob[size:]
    down_ref[...] = feed[size:]
    last_ref[...] = blob[:size, first - LANES : first]
    both = jnp.concatenate([blob[:size, :first], feed[:size]], 1)
    parts = [both[t * rows : (t + 1) * rows] for t in range(n)]
    for p, ref in enumerate(pieces):
        chosen = parts[0]
        for t in range(1, n):
            chosen = jnp.where((me_ref[0] ^ p) == t, parts[t], chosen)
        ref[...] = chosen.astype(BF16)


def hand_over(me, blob, feeds, rows, n, first):
    dm = blob[0].shape[1]
    part = feeds[0].shape[1]
    size = n * rows
    vmem = pl.BlockSpec(memory_space=pltpu.VMEM)
    *pieces, out, down, last = pl.pallas_call(
        functools.partial(hand_over_kernel, n=n, rows=rows, first=first),
        in_specs=[pl.BlockSpec(memory_space=pltpu.SMEM)] + [vmem] * 4,
        out_specs=[vmem] * (n + 3),
        out_shape=[jax.ShapeDtypeStruct((rows, first + part), BF16)] * n
        + [
            jax.ShapeDtypeStruct((rows, dm), F32),
            jax.ShapeDtypeStruct((feeds[0].shape[0] - size, part), F32),
            jax.ShapeDtypeStruct((size, LANES), F32),
        ],
        name="hand_over",
    )(me, *blob, *feeds)
    return pieces, out, down, last


def finish_kernel(me_ref, *refs, n, width, nd):
    pieces, (q_ref, k_ref, v_ref, vec_ref, up_ref) = refs[:n], refs[n:]
    first = 3 * width + LANES
    pieces = [p[...].astype(F32) for p in pieces]
    vec_ref[...] = sum(p[:, 3 * width : first] for p in pieces)
    bit = 1
    while bit < n:
        on = (me_ref[0] & bit) != 0
        for p in range(n):
            if not p & bit:
                a, b = pieces[p], pieces[p | bit]
                pieces[p] = jnp.where(on, b, a)
                pieces[p | bit] = jnp.where(on, a, b)
        bit *= 2
    step = (pieces[0].shape[1] - first) // nd
    for t in range(n):
        for i, ref in enumerate((q_ref, k_ref, v_ref)):
            ref[:, t * width : (t + 1) * width] = pieces[t][:, i * width : (i + 1) * width]
        for j in range(nd):
            to = (j * n + t) * step
            up_ref[:, to : to + step] = pieces[t][:, first + j * step : first + (j + 1) * step]


def finish(me, pieces, width, nd):
    n = len(pieces)
    rows, wide = pieces[0].shape
    weight = jax.ShapeDtypeStruct((rows, n * width), F32)
    tile = jax.ShapeDtypeStruct((rows, LANES), F32)
    vmem = pl.BlockSpec(memory_space=pltpu.VMEM)
    return pl.pallas_call(
        functools.partial(finish_kernel, n=n, width=width, nd=nd),
        in_specs=[pl.BlockSpec(memory_space=pltpu.SMEM)] + [vmem] * n,
        out_specs=[vmem] * 5,
        out_shape=[weight] * 3 + [tile, jax.ShapeDtypeStruct((rows, n * (wide - 3 * width - LANES)), F32)],
        name="finish",
    )(me, *pieces)


def body(
    nd,
    ns,
    tokens,
    cotangent,
    segments,
    w_query,
    w_key,
    w_value,
    w_out,
    w_up,
    w_down,
    ln1_gain,
    ln1_shift,
    query_bias,
    value_bias,
    out_bias,
    ln2_gain,
    ln2_shift,
    up_bias,
    down_bias,
):
    d = lax.axis_index("dp")
    s = lax.axis_index("seq")
    me = s.astype(jnp.int32).reshape(1)
    _, block, dm = tokens.shape
    hd = dm // H
    heads = H // ns
    width = heads * hd
    rows = w_query.shape[0]
    ff_rows, ff = w_down.shape[0], w_up.shape[1]
    ratio = ff_rows // rows
    part = ff // ns
    pad = 16

    me = jnp.stack([s, d]).astype(jnp.int32)
    masks = bits_of(nd)[::-1]
    far = bits_of(ns)[-1]
    x_own = tokens.reshape(block, dm)
    g = cotangent.reshape(block, dm)
    x_far = swap(x_own, "seq", ns, far)

    cols = [w.reshape(rows, ns, width) for w in (w_query, w_key, w_value)]
    vec = jnp.stack([ln1_gain, ln1_shift, ln2_gain, ln2_shift, out_bias, down_bias, query_bias, value_bias], 1)
    vec = jnp.pad(vec, ((0, 0), (0, LANES - vec.shape[1])))
    up_cols = w_up.reshape(rows, nd, ns, ff_rows).transpose(0, 2, 1, 3).reshape(rows, ns, part)
    lanes = LANES * -(-block // (rows * LANES))
    seg = jnp.pad(segments.reshape(block).astype(BF16), (0, rows * lanes - block)).reshape(rows, lanes)
    same = jnp.concatenate([vec, w_out, seg], 1)
    same = jnp.broadcast_to(same[:, None], (rows, ns, same.shape[1]))
    pieces = jnp.concatenate(cols + [same, up_cols], 2).transpose(1, 0, 2)
    first = 3 * width + LANES
    size = ns * rows
    pieces = trade_seq(pieces, s, ns)
    start = first + dm
    segs = jnp.stack([p[:, start : start + lanes].reshape(-1)[:block] for p in pieces]).astype(jnp.int32)
    seg_row = segs.reshape(ns, 1, block)
    seg_col = segs.reshape(ns, block, 1)
    pieces = ordered(pieces, s).reshape(size, -1)
    lane = lax.broadcasted_iota(jnp.int32, (size, first), 1)
    one = jnp.where(lane == 3 * width + 8, jnp.pad(up_bias, (0, size - ff_rows))[:, None], pieces[:, :first])
    two = jnp.concatenate([pieces[:, first:start], pieces[:, start + lanes :], w_down], 0)

    turned = masks[:-2] + masks[:-3:-1]
    ones = [one[None]]
    for mask in masks[:-2]:
        ones.append(swap(jnp.concatenate(ones, 0), "dp", nd, mask))
    ones = jnp.concatenate(ones, 0)
    cut = -(-(first // 2) // LANES) * LANES + LANES
    ones = [ones[:, :, :cut]], [ones[:, :, cut:]]
    ones[0][0], ones[1][0], two, seg_row, seg_col = lax.optimization_barrier(
        (ones[0][0], ones[1][0], two, seg_row, seg_col)
    )
    for parts, order in zip(ones, (masks, turned)):
        parts.append(swap(parts[0], "dp", nd, order[-2]))
    ones[0][1], ones[1][1], x_far = lax.optimization_barrier((ones[0][1], ones[1][1], x_far))
    g_far = swap(tie(g, x_far), "seq", ns, far)
    last = [jnp.concatenate(parts, 0) for parts in ones]
    twos = [tie(two, ones[0][1])[None]]
    for parts, held, order in zip(ones, last, (masks, turned)):
        parts.append(swap(held, "dp", nd, order[-1]))

    for mask in masks[:-2]:
        twos.append(swap(jnp.concatenate(twos, 0), "dp", nd, mask))
    parts = {0: x_own, far: x_far}
    for mask in bits_of(ns)[-2::-1]:
        for p in list(parts):
            parts[p | mask] = swap(parts[p], "seq", ns, mask)
    x_all = jnp.stack([parts[p] for p in range(ns)])

    ids = [gathered_ids(order) for order in (masks, turned)]
    ids = [[sum(i[:-2], [])] + i[-2:] for i in ids]
    ones, ids = zip(*[settle(p, d, nd, i, 1) for p, i in zip(ones, ids)])
    ones, x_all = lax.optimization_barrier((ones, x_all))
    qkv, h_one, w_qkv, vecs = enter(me, ones, ids, x_all, width)
    qkv, h_one, w_qkv, vecs, g_far, twos = lax.optimization_barrier((qkv, h_one, w_qkv, vecs, g_far, twos))
    two = jnp.concatenate(twos, 0)
    twos = [two] + [swap(two, "dp", nd, p) for p in (1, 2)]

    g_parts = {0: g, far: g_far}
    for mask in bits_of(ns)[-2::-1]:
        for p in list(g_parts):
            g_parts[p | mask] = swap(g_parts[p], "seq", ns, mask)
    qkv, two = lax.optimization_barrier((qkv, two))
    o_low, o_full, lse = attend(me, qkv, seg_row, seg_col, heads, hd)
    o_low, o_full, lse, twos[1:], *g_last = lax.optimization_barrier(
        (o_low, o_full, lse, twos[1:], g_parts[1], g_parts[ns - 1])
    )
    g_all = jnp.stack([g, g_last[0], g_far, g_last[1]])
    o_got = spread_seq(o_low, ns, (g_all,))
    twos.append(swap(tie(two, o_low), "dp", nd, 3))
    ids = sum(gathered_ids(masks[:-2]), [])
    twos, ids = settle(twos, d, nd, [[r ^ p for r in ids] for p in range(4)], 3)
    far_h, far_act, far_gu, gh_two, gh_three, sums_up, *weights = feed(
        me, o_got, x_all, g_all, vecs, 2, twos, ids
    )
    w_out_all, _, w_down_own = weights

    def over_rows(a, b):
        return jnp.einsum("nbk,nbc->kc", a, b, preferred_element_type=F32)

    d_down = over_rows(far_act, g_all[2:])
    sent = add_low(gh_two, swap(gh_three, "seq", ns, 1))
    far_got = swap(sent, "seq", ns, 2)
    sums_up, sent, d_down = lax.optimization_barrier((sums_up, sent, d_down))
    h_two, act, gu, gh_zero, gh_one, sums_up, x_two = feed(
        me, o_got, x_all, g_all, vecs, 0, weights, None, sums_up
    )
    near_got = swap(gh_one, "seq", ns, 1)
    d_down = (d_down + over_rows(act, g_all[:2])).astype(BF16)
    d_up = (over_rows(far_h, far_gu) + over_rows(h_two, gu)).astype(BF16)
    feeds = jnp.concatenate([d_up.reshape(nd, size, part), d_down.reshape(nd, ff_rows, dm)], 1)
    feed_keep, feed_sent = halves(feeds, d, nd, 1)
    feed_got = swap(feed_sent, "dp", nd, 1)
    far_got, feed_sent = lax.optimization_barrier((far_got, feed_sent))
    *gos, gx_two, d_out, sums_two = turn(me, o_got, gh_zero, near_got, far_got, x_two, g, w_out_all, vecs)
    go_got = [gos[0]] + [swap(gos[p], "seq", ns, p) for p in range(1, ns)]
    go_got[1], d_out, sums_two = lax.optimization_barrier((go_got[1], d_out, sums_two))
    act, far_act = lax.optimization_barrier((act, far_act, go_got[1]))[:2]
    out_parts = [dot_nn(a, w_down_own).astype(BF16) for a in (act[0], act[1], far_act[0], far_act[1])]
    out_sent = add_low(out_parts[2], swap(out_parts[3], "seq", ns, 1))
    out_near = swap(out_parts[1], "seq", ns, 1)
    out_far = swap(tie(out_sent, go_got[-1]), "seq", ns, 2)
    outs_keep, outs_sent = halves(d_out.reshape(nd * ns, rows, dm), s, ns, 1)
    outs_got = swap(outs_sent, "seq", ns, 1)
    outs_keep, outs_sent = halves(add_low(outs_keep, outs_got), s >> 1, ns // 2, 1)
    outs_got = swap(outs_sent, "seq", ns, 2)

    go_all = jnp.stack(go_got)
    go_all, *_ = lax.optimization_barrier((go_all, out_sent, out_parts, outs_sent))
    grads, d_qkv = attend_back(me, qkv, go_all, o_full, lse, seg_row, seg_col, h_one, heads, hd)
    grads, d_qkv, out_near, out_far, outs_got, feed_got = lax.optimization_barrier(
        (grads, d_qkv, out_near, out_far, outs_got, feed_got)
    )
    blob = jnp.concatenate(
        [
            jnp.pad(d_qkv.reshape(nd, size, 3 * width), ((0, 0), (0, 0), (0, dm - 3 * width))),
            add_low(outs_keep, outs_got),
        ],
        1,
    )
    blob_keep, blob_sent = halves(blob, d, nd, 1)
    blob_got = swap(blob_sent, "dp", nd, 1)
    feed_keep, feed_sent = halves(add_low(feed_keep, feed_got), d >> 1, nd // 2, 1)
    feed_got = swap(feed_sent, "dp", nd, 2)
    grads = lax.optimization_barrier((grads, blob_sent, feed_sent))[0]
    even, odd, tile = leave(me, x_all, grads, w_qkv, vecs, sums_two, sums_up)
    even, odd, tile, blob_got, feed_got = lax.optimization_barrier((even, odd, tile, blob_got, feed_got))
    tile = tile.reshape(nd // 4, 4, size, LANES)
    tiles = [lax.dynamic_index_in_dim(tile, (d & 3) ^ p, 1, False) for p in range(4)]
    tiles = [jnp.pad(t, ((0, 0), (0, rows), (3 * width, dm - first))) for t in tiles[::2]] + tiles[1::2]
    blob_keep, blob_sent = halves(add_low(blob_keep, blob_got), d >> 1, nd // 2, 1)
    blob_keep, blob_sent = blob_keep + tiles[0], blob_sent + tiles[1]
    blob_got = swap(blob_sent, "dp", nd, 2)
    tiles = [swap(t, "dp", nd, p) for t, p in zip(tie(tiles[2:], blob_sent), (1, 3))]
    feed_keep, feed_sent = halves(tie(add_low(feed_keep, feed_got), blob_sent), d >> 2, nd // 4, 1)
    feed_got = swap(feed_sent, "dp", nd, 4)
    keep, sent, got = collect_pairs(even, odd, ns)
    blob_got, sent, tiles = lax.optimization_barrier((blob_got, sent, tiles))
    tile = jnp.pad(tiles[0].astype(F32) + tiles[1].astype(F32), ((0, 0), (0, rows), (3 * width, dm - first)))
    blob = (blob_keep.astype(F32) + blob_got.astype(F32) + tile).astype(BF16)
    blob_keep, blob_sent = halves(blob, d >> 2, nd // 4, 1)
    blob_got = swap(blob_sent, "dp", nd, 4)
    blob_got, sent, feed_got = lax.optimization_barrier((blob_got, sent, feed_got))
    if nd > 8:
        rest = [(blob_keep, blob_got), (feed_keep, feed_got)]
        rest = [collect_dp(add_low(a, b), d >> 3, nd // 8, BF16, shift=3) for a, b in rest]
        rest = [(v, jnp.zeros_like(v)) for v in rest]
    else:
        rest = [(blob_keep[0], blob_got[0]), (feed_keep[0], feed_got[0])]
    pieces, sum_out, sum_down, last = hand_over(me, *rest, rows, ns, first)
    out = out_parts[0].astype(F32) + out_near.astype(F32) + out_far.astype(F32) + x_two + vecs[5:6]
    trades = [pieces[0]] + [swap(pieces[p], "seq", ns, p) for p in range(1, ns)]
    gh_one = keep.astype(F32) + got.astype(F32)
    n_own, inv_own = normed_parts(tie(x_own, pieces[0]).astype(F32))
    grad_x = gx_two + normalize_back(gh_one, n_own, inv_own, vecs[0:1])
    trades, grad_x, out, last = lax.optimization_barrier((trades, grad_x, out, last))
    sum_q, sum_k, sum_v, vec_sum, sum_up = finish(me, trades, width, nd)
    vec_sum = vec_sum.T
    sum_up_bias = last[:ff_rows, 8]
    v = [vec_sum[i] for i in range(8)]
    return (
        out.reshape(1, block, dm),
        grad_x.reshape(1, block, dm),
        sum_q,
        sum_k,
        sum_v,
        sum_out,
        sum_up,
        sum_down,
        v[0],
        v[1],
        v[6],
        v[7],
        v[4],
        v[2],
        v[3],
        sum_up_bias,
        v[5],
    )


def solution(mesh):
    act = P("dp", "seq", None)
    weight = P(("dp", "seq"), None)
    vector = P(("dp", "seq"))
    return jax.shard_map(
        functools.partial(body, mesh.shape["dp"], mesh.shape["seq"]),
        mesh=mesh,
        in_specs=(act, act, P("dp", "seq")) + (weight,) * 6 + (vector,) * 9,
        out_specs=(act, act) + (weight,) * 6 + (vector,) * 9,
        check_vma=False,
    )
```
